256 devices in a mesh: section: 64 (over z, x, core), tensor: 4 (over y).
Axes of the slice: x: 4, y: 4, z: 8, core: 2. Of those that a mesh axis runs over, the one named last changes fastest.
Arguments:
- hidden_in: bfloat16 [4096, 2048], P('section'), may hold values from -6 to 6
- queries: bfloat16 [4096, 4096], P('section', 'tensor'), may hold values from -48 to 48, as said below
- new_kv: bfloat16 [4096, 2, 512], P('section', None, 'tensor'), may hold values from -6 to 6
- cache: bfloat16 [4096, 2, 96, 512], P('section', None, None, 'tensor'), may hold values from -6 to 6
- lengths: int32 [4096], P('section'), may hold values from 2 to 96, as said below
- out_weight: bfloat16 [4096, 2048], P('tensor'), may hold values from -0.09375 to 0.09375
- moe_gain: float32 [2048], replicated, may hold values from 0.1 to 1.9
- expert_ids: int32 [4096, 8], P('section'), may hold values from 0 to 127, all different within a row; in each aligned block of 64 rows (0 to 63, 64 to 127, ...) at most 10 rows name the same one
- expert_gates: float32 [4096, 8], P('section'), may hold values from 0.1 to 1
- gate_up: bfloat16 [128, 2, 2048, 768], P('section', None, None, 'tensor'), may hold values from -0.125 to 0.125
- down: bfloat16 [128, 768, 2048], P('section', 'tensor'), may hold values from -0.21875 to 0.21875
- owners: int32 [4096], replicated, may hold values from -1 to 63, as said below
Outputs:
- thinker_out: bfloat16 [4096, 2048], P('section', 'tensor')
- talker_rows: bfloat16 [8192, 2048], P('section', 'tensor')
The draws below stay inside these ranges and needn't reach their ends.
Inputs may be any that keep to these rules, and one draw needn't show every extreme that they name: queries and cache keys may be strongly aligned in some rows. `lengths`: among the 64 requests of each section index one has exactly 96. `expert_ids`: each row names 8 different experts; in each aligned block of 64 rows (the rows of one section index) no expert is named by more than 10 rows, a bound that some block reaches. `owners`: -1 marks a request without speech output; of the 64 requests of one section index at most 2 have the same owner, and one owner has exactly 2 from every section index, so it holds 128 rows.
All inputs are finite; a program needn't handle non-finite values.
Results may differ from the reference program's by a relative error of at most 0.015.
Values may be sent and summed in bfloat16 or wider, within the bound.
No kernel may reach another device: no remote copies, remote signals or barrier semaphores. Data moves between devices by JAX's collectives and lax.ppermute only.
A program may use at most 128 MiB of HBM per device.

```python
import math
import jax
import jax.numpy as jnp
import numpy as np
from jax import lax

D = 2048
H = 32
KVH = 4
HD = 128
EXPERTS = 128
TOP = 8
EH = 768
REQ_DEV = 64
CTX = 96
HCAP = 2
CAP = 10
REQ_TOTAL = 4096
OWNCAP = 128
N_SECTION = 64
N_TENSOR = 4


def cache_field(key):
    full_shape = (REQ_TOTAL, 2, CTX, KVH * HD)
    drawn_part = jnp.clip(jax.random.normal(jax.random.fold_in(key, 101), full_shape, jnp.float32), -6.0, 6.0)
    key_field = drawn_part
    aligned = (jnp.arange(REQ_TOTAL) % 16 == 0)[:, None]
    second = key_field[:, 0, 1, :]
    tied_key = jnp.where(aligned, second, second)
    return key_field.at[:, 0, 1, :].set(tied_key)


def draw_cache(key, part):
    key_field = cache_field(key)
    return key_field.astype(jnp.bfloat16)


def draw_queries(key, part):
    key = jax.random.fold_in(key, 5)
    result = jnp.clip(jax.random.normal(key, (REQ_TOTAL, H * HD), jnp.float32), -6.0, 6.0)
    return result.astype(jnp.bfloat16)


def draw_lengths(key, part):
    key = jax.random.fold_in(key, 7)
    key_base, key_pick = jax.random.split(key)
    base_draw = jax.random.randint(key_base, (REQ_TOTAL,), 2, CTX + 1)
    chosen = jax.random.randint(key_pick, (N_SECTION,), 0, REQ_DEV)
    request_index = jnp.arange(REQ_TOTAL)
    local_index = request_index % REQ_DEV
    block_index = request_index // REQ_DEV
    return jnp.where(local_index == chosen[block_index], CTX, base_draw).astype(jnp.int32)


def draw_owners(key, part):
    key = jax.random.fold_in(key, 11)
    key_star, key_rows, key_owner, key_speak = jax.random.split(key, 4)
    star_owner = jax.random.randint(key_star, (), 0, N_SECTION)
    row_order = jax.vmap(lambda sub_key: jax.random.permutation(sub_key, REQ_DEV))(jax.random.split(key_rows, N_SECTION))
    block_of = row_order // HCAP
    owner_order = jax.vmap(lambda sub_key: jax.random.permutation(sub_key, N_SECTION - 1))(jax.random.split(key_owner, N_SECTION)) + 1
    block_clip = jnp.clip(block_of - 1, 0, N_SECTION - 2)
    other_owner = (star_owner + jnp.take_along_axis(owner_order, block_clip, axis=1)) % N_SECTION
    speaking = jax.random.randint(key_speak, (N_SECTION, REQ_DEV), 0, 2)
    keep_other = (block_of <= N_SECTION - 1) & (speaking == 1)
    owner_table = jnp.where(block_of == 0, star_owner, jnp.where(keep_other, other_owner, -1))
    return owner_table.reshape(REQ_TOTAL).astype(jnp.int32)


def levels(stream_key, extent, shards, low, top_value):
    loudness, own = 1.0, jax.random.fold_in(stream_key, 6)
    for dim, shards_of in shards:
        draws = jnp.exp(jax.random.uniform(jax.random.fold_in(own, dim), (shards_of,), jnp.float32, low / len(shards), top_value / len(shards)))
        loudness = loudness * jnp.repeat(draws, extent[dim] // shards_of).reshape([-1 if axis == dim else 1 for axis in range(len(extent))])
    return loudness


def shared_out(own_key, own, number, rows, amount, top, reach, slope):
    sequence = jax.random.permutation(own_key, amount)
    heavy_load, usual = shares(amount, rows * top, reach, slope, True), shares(amount, rows * top, reach, slope, False)
    places = jnp.arange(amount)

    def named(sizes, rotation):
        used = int((sizes > 0).sum())
        fixed = max(1, used // 4)
        passed = fixed + (places - fixed + rotation * (used - fixed)) % max(1, amount - fixed)
        return jnp.zeros((amount,), jnp.int32).at[sequence[jnp.where(places < fixed, places, passed)]].set(jnp.asarray(sizes, jnp.int32))

    sizes = jnp.where(number % 4 == 0, named(heavy_load, number // 4), named(usual, number - number // 4 - 1))
    mixed = jax.random.permutation(jax.random.fold_in(own, 3), amount)
    giver, sink = mixed[0:amount // 2 * 2:2], mixed[1:amount // 2 * 2:2]
    margin = jnp.minimum(sizes[giver] - 1, reach - sizes[sink]) // 2
    margin = jnp.where((giver == sequence[0]) | (sink == sequence[0]) | (sizes[sink] == 0), 0, jnp.maximum(margin, 0))
    passed = jax.random.randint(jax.random.fold_in(own, 4), (amount // 2,), 0, 1 << 20) % (margin + 1)
    sizes = sizes.at[giver].add(-passed).at[sink].add(passed)
    members = jnp.searchsorted(jnp.cumsum(sizes), jnp.arange(rows * top), side="right").astype(jnp.int32)
    listing = members.reshape(top, rows).T
    listing = listing[jax.random.permutation(jax.random.fold_in(own, 1), rows)]
    rotation = jax.random.randint(jax.random.fold_in(own, 2), (rows, 1), 0, top)
    return jnp.take_along_axis(listing, (jnp.arange(top)[None, :] + rotation) % top, axis=1)


def shares(count, total, most, lean, full):
    portions = [(1 << 20) // math.isqrt(grade ** lean) + 1 for grade in range(1, count + 1)]
    largest = most if full else min(most, max(-(-total // count), total * portions[0] // sum(portions)))
    least = 1 if total - largest >= count - 1 else 0
    counts, surplus = [largest] + [least] * (count - 1), total - largest - least * (count - 1)
    while surplus > 0:
        free = [i for i in range(1, count) if counts[i] < largest] or [i for i in range(1, count) if counts[i] < most]
        pool, budget = sum([portions[i] for i in free]), surplus
        for i in free:
            extra = min(most - counts[i], max(1, budget * portions[i] // pool), surplus)
            counts[i] = counts[i] + extra
            surplus = surplus - extra
    return np.array(counts)


def scatter_about(own_key, dims, scale, limit, cuts=(), kind=jnp.bfloat16):
    entries = scale * jax.random.normal(own_key, dims, jnp.float32)
    if cuts:
        entries = entries * levels(own_key, dims, cuts, -0.22, 0.18)
    return jnp.clip(entries, -limit, limit).astype(kind)


def setup_inputs(seed: int = 0) -> dict:
    keys = jax.random.split(jax.random.key(seed), 13)
    hidden_in = scatter_about(keys[0], (REQ_TOTAL, D), 1.0, 6.0, ((0, 64),))
    queries = draw_queries(jax.random.fold_in(keys[12], 71), 0)
    new_kv = scatter_about(keys[2], (REQ_TOTAL, 2, KVH * HD), 1.0, 6.0, ((0, 64), (2, 4)))
    cache = draw_cache(jax.random.fold_in(keys[12], 71), 0)
    lengths = draw_lengths(jax.random.fold_in(keys[12], 71), 0)
    out_weight = scatter_about(keys[5], (H * HD, D), (H * HD) ** -0.5, 0.09375, ((0, 4),))
    moe_gain = jnp.clip(1.0 + 0.18 * jax.random.normal(keys[6], (D,), jnp.float32), 0.1, 1.9)
    expert_ids_keys = jax.random.split(jax.random.fold_in(keys[7], 1), REQ_TOTAL // REQ_DEV)
    expert_ids_turns = jax.random.permutation(jax.random.fold_in(keys[7], 3), REQ_TOTAL // REQ_DEV)
    expert_ids = jax.vmap(lambda own, number: shared_out(jax.random.fold_in(keys[7], 2), own, number, REQ_DEV, EXPERTS, TOP, CAP, 2))(expert_ids_keys, expert_ids_turns).reshape((REQ_TOTAL, TOP))
    expert_gates = jnp.clip(jnp.exp(math.log(1.0) - 2.3025851 * jax.random.uniform(keys[8], (REQ_TOTAL, TOP), jnp.float32) ** levels(keys[8], (REQ_TOTAL, TOP), ((0, 64),), -0.2, 0.2)), 0.1, 1.0)
    gate_up = scatter_about(keys[9], (EXPERTS, 2, D, EH), D ** -0.5, 0.125, ((0, 64), (3, 4)))
    down = scatter_about(keys[10], (EXPERTS, EH, D), EH ** -0.5, 0.21875, ((0, 64), (1, 4)))
    owners = draw_owners(jax.random.fold_in(keys[12], 71), 0)
    return dict(hidden_in=hidden_in, queries=queries, new_kv=new_kv, cache=cache, lengths=lengths, out_weight=out_weight, moe_gain=moe_gain, expert_ids=expert_ids, expert_gates=expert_gates, gate_up=gate_up, down=down, owners=owners)


def attend(queries, new_kv, cache, lengths):
    req_count = queries.shape[0]
    query_heads = queries.astype(jnp.float32).reshape(req_count, KVH, H // KVH, HD)
    cache_keys = cache[:, 0].astype(jnp.float32).reshape(req_count, CTX, KVH, HD)
    cache_values = cache[:, 1].astype(jnp.float32).reshape(req_count, CTX, KVH, HD)
    fresh_keys = new_kv[:, 0].astype(jnp.float32).reshape(req_count, KVH, HD)
    fresh_values = new_kv[:, 1].astype(jnp.float32).reshape(req_count, KVH, HD)
    scale_factor = 1.0 / math.sqrt(HD)
    cache_scores = jnp.einsum('rkgd,rckd->rkgc', query_heads, cache_keys) * scale_factor
    valid_cells = jnp.arange(CTX)[None, :] < lengths[:, None]
    cache_scores = jnp.where(valid_cells[:, None, None, :], cache_scores, -jnp.inf)
    fresh_scores = jnp.einsum('rkgd,rkd->rkg', query_heads, fresh_keys) * scale_factor
    top_score = jnp.maximum(lax.optimization_barrier(jnp.max(cache_scores, axis=-1)), fresh_scores)
    cache_exp = jnp.exp(cache_scores - top_score[..., None])
    fresh_exp = jnp.exp(fresh_scores - top_score)
    total_mass = lax.optimization_barrier(jnp.sum(cache_exp, axis=-1)) + fresh_exp
    cache_weights = lax.optimization_barrier((cache_exp / total_mass[..., None]).astype(jnp.bfloat16)).astype(jnp.float32)
    fresh_weights = lax.optimization_barrier((fresh_exp / total_mass).astype(jnp.bfloat16)).astype(jnp.float32)
    context = jnp.einsum('rkgc,rckd->rkgd', cache_weights, cache_values)
    context = context + fresh_weights[..., None] * fresh_values[:, :, None, :]
    return context.reshape(req_count, H * HD).astype(jnp.bfloat16)

def rms_scale(middle, moe_gain):
    values = middle.astype(jnp.float32)
    mean_square = lax.optimization_barrier(jnp.mean(values * values, axis=-1, keepdims=True))
    return (values * lax.rsqrt(mean_square + 1e-06) * moe_gain).astype(jnp.bfloat16)

def expert_pass(normed, gates, expert_ids, gate_up, down):
    total_rows = normed.shape[0]
    row_block = jnp.arange(total_rows, dtype=jnp.int32) // REQ_DEV

    def one_expert(carry, inputs):
        expert_index, gate_up_one, down_one = inputs
        chosen = expert_ids == expert_index
        picked = jnp.any(chosen, axis=1)
        gate_here = lax.optimization_barrier(jnp.sum(jnp.where(chosen, gates, 0.0), axis=1))
        running = jnp.cumsum(picked.astype(jnp.int32).reshape(N_SECTION, REQ_DEV), axis=1).reshape(total_rows) - 1
        target = jnp.where(picked, row_block * CAP + running, N_SECTION * CAP).astype(jnp.int32)
        source_rows = jnp.zeros((N_SECTION * CAP,), jnp.int32).at[target].set(jnp.arange(total_rows, dtype=jnp.int32), mode='drop')
        filled = jnp.zeros((N_SECTION * CAP,), jnp.bool_).at[target].set(True, mode='drop')
        input_rows = normed[source_rows]
        gate_part = jnp.dot(input_rows, gate_up_one[0], preferred_element_type=jnp.float32)
        up_part = jnp.dot(input_rows, gate_up_one[1], preferred_element_type=jnp.float32)
        activation = (jax.nn.silu(gate_part) * up_part).astype(jnp.bfloat16)
        grouped = activation.astype(jnp.float32).reshape(N_SECTION * CAP, N_TENSOR, EH // N_TENSOR)
        down_groups = down_one.astype(jnp.float32).reshape(N_TENSOR, EH // N_TENSOR, D)
        pieces = jnp.einsum('sgh,ghd->sgd', grouped, down_groups)
        pieces = lax.optimization_barrier(pieces.astype(jnp.bfloat16)).astype(jnp.float32)
        expert_rows = lax.optimization_barrier(jnp.sum(pieces, axis=1)).astype(jnp.bfloat16)
        weighted = gate_here[source_rows][:, None] * expert_rows.astype(jnp.float32)
        destination = jnp.where(filled, source_rows, total_rows).astype(jnp.int32)
        carry = carry.at[destination].add(weighted, mode='drop')
        return (carry, None)
    start = jnp.zeros((total_rows, D), jnp.float32)
    result, _ = lax.scan(one_expert, start, (jnp.arange(EXPERTS, dtype=jnp.int32), gate_up, down))
    return result

def hand_over(thinker_out, owners):
    owner_onehot = (owners[:, None] == jnp.arange(N_SECTION, dtype=jnp.int32)[None, :]).astype(jnp.int32)
    position = lax.optimization_barrier(jnp.sum((jnp.cumsum(owner_onehot, axis=0) - 1) * owner_onehot, axis=1))
    target = jnp.where(owners >= 0, owners * OWNCAP + position, N_SECTION * OWNCAP).astype(jnp.int32)
    return jnp.zeros((N_SECTION * OWNCAP, D), jnp.bfloat16).at[target].set(thinker_out, mode='drop')

def reference(hidden_in, queries, new_kv, cache, lengths, out_weight, moe_gain, expert_ids, expert_gates, gate_up, down, owners):
    context = attend(queries, new_kv, cache, lengths)
    attention = jnp.dot(context, out_weight, preferred_element_type=jnp.float32)
    middle = (hidden_in.astype(jnp.float32) + attention).astype(jnp.bfloat16)
    normed = rms_scale(middle, moe_gain)
    gates = expert_gates / lax.optimization_barrier(jnp.sum(expert_gates, axis=1, keepdims=True))
    mixture = expert_pass(normed, gates, expert_ids, gate_up, down)
    thinker_out = (middle.astype(jnp.float32) + mixture).astype(jnp.bfloat16)
    talker_rows = hand_over(thinker_out, owners)
    return (thinker_out, talker_rows)
```

```python
import math

import jax
import jax.numpy as jnp
from jax import lax
from jax.experimental import pallas as pl
from jax.experimental.pallas import tpu as pltpu
from jax.sharding import Mesh
from jax.sharding import PartitionSpec as P

HD = 128
HCAP = 2
CAP = 10
NZ, NX, NC, NY = 8, 4, 2, 4
REQ = 64
SECTIONS = NZ * NX * NC
TOKENS = NZ * REQ
PLANE = NX * NY
BLOCK = NZ * CAP
QUARTER = 512
WIDTH = 2048
EHQ = 192
VMEM_LIMIT = 56 * 1024 * 1024


def attend_local(queries, new_kv, cache, lengths):
    req_count = queries.shape[0]
    cached_count = cache.shape[2]
    kv_local = new_kv.shape[2] // HD
    group_size = queries.shape[1] // (kv_local * HD)
    query_heads = queries.reshape(req_count, kv_local, group_size, HD)
    cache_keys = cache[:, 0].reshape(req_count, cached_count, kv_local, HD)
    cache_values = cache[:, 1].reshape(req_count, cached_count, kv_local, HD)
    fresh_keys = new_kv[:, 0].reshape(req_count, kv_local, HD)
    fresh_values = new_kv[:, 1].reshape(req_count, kv_local, HD)
    scale_factor = 1.0 / math.sqrt(HD)
    cache_scores = (
        jnp.einsum("rkgd,rckd->rkgc", query_heads, cache_keys, preferred_element_type=jnp.float32)
        * scale_factor
    )
    valid_cells = jnp.arange(cached_count)[None, :] < lengths[:, None]
    cache_scores = jnp.where(valid_cells[:, None, None, :], cache_scores, -jnp.inf)
    fresh_scores = (
        jnp.einsum("rkgd,rkd->rkg", query_heads, fresh_keys, preferred_element_type=jnp.float32)
        * scale_factor
    )
    top_score = jnp.maximum(jnp.max(cache_scores, axis=-1), fresh_scores)
    cache_exp = jnp.exp(cache_scores - top_score[..., None])
    fresh_exp = jnp.exp(fresh_scores - top_score)
    total_mass = jnp.sum(cache_exp, axis=-1) + fresh_exp
    cache_weights = (cache_exp / total_mass[..., None]).astype(jnp.bfloat16)
    fresh_weights = (fresh_exp / total_mass).astype(jnp.bfloat16)
    context = jnp.einsum(
        "rkgc,rckd->rkgd", cache_weights, cache_values, preferred_element_type=jnp.float32
    )
    context = (
        context
        + fresh_weights.astype(jnp.float32)[..., None]
        * fresh_values.astype(jnp.float32)[:, :, None, :]
    )
    return context.reshape(req_count, kv_local * group_size * HD).astype(jnp.bfloat16)


def plan_kernel(base_ref, meta_ref, target_ref, gate_ref):
    base = base_ref[0].astype(jnp.float32)
    expert = base + lax.broadcasted_iota(jnp.int32, (PLANE, TOKENS), 0).astype(jnp.float32)
    chosen = jnp.zeros((PLANE, TOKENS), jnp.float32)
    gate = jnp.zeros((PLANE, TOKENS), jnp.float32)
    total = jnp.sum(meta_ref[8:16, :], axis=0, keepdims=True)
    for k in range(8):
        hit = meta_ref[k : k + 1, :] == expert
        chosen = jnp.where(hit, 1.0, chosen)
        gate = jnp.where(hit, meta_ref[8 + k : 9 + k, :] / total, gate)
    earlier = lax.broadcasted_iota(jnp.int32, (TOKENS, TOKENS), 0)
    column = lax.broadcasted_iota(jnp.int32, (TOKENS, TOKENS), 1)
    same = (earlier // REQ) == (column // REQ)
    before = jnp.where(same & (earlier < column), 1.0, 0.0).astype(jnp.bfloat16)
    rank = jnp.dot(chosen.astype(jnp.bfloat16), before, preferred_element_type=jnp.float32)
    block = lax.broadcasted_iota(jnp.int32, (PLANE, TOKENS), 1) // REQ
    slot = rank.astype(jnp.int32) + block * CAP
    target_ref[...] = jnp.where(chosen > 0.0, slot, -1)
    gate_ref[...] = gate


def gather_kernel(target_ref, rows_ref, out_ref, pick_ref):
    slot = lax.broadcasted_iota(jnp.int32, (BLOCK, TOKENS), 0)
    for e in range(PLANE):
        hit = target_ref[e : e + 1, :] == slot
        pick_ref[e * BLOCK : (e + 1) * BLOCK, :] = jnp.where(hit, 1.0, 0.0).astype(jnp.bfloat16)
    rows = jnp.dot(pick_ref[...], rows_ref[...], preferred_element_type=jnp.float32)
    out_ref[...] = rows.astype(jnp.bfloat16)


def combine_kernel(target_ref, gate_ref, rows_ref, out_ref, high_ref, low_ref):
    slot = lax.broadcasted_iota(jnp.int32, (BLOCK, TOKENS), 0)
    for e in range(PLANE):
        hit = target_ref[e : e + 1, :] == slot
        weight = jnp.where(hit, gate_ref[e : e + 1, :], 0.0)
        high = weight.astype(jnp.bfloat16)
        high_ref[e * BLOCK : (e + 1) * BLOCK, :] = high
        low_ref[e * BLOCK : (e + 1) * BLOCK, :] = (weight - high.astype(jnp.float32)).astype(
            jnp.bfloat16
        )
    dims = (((0,), (0,)), ((), ()))
    rows = rows_ref[...]
    total = lax.dot_general(high_ref[...], rows, dims, preferred_element_type=jnp.float32)
    total = total + lax.dot_general(low_ref[...], rows, dims, preferred_element_type=jnp.float32)
    out_ref[...] = total.astype(jnp.bfloat16)


def expert_kernel(rows_ref, gain_ref, g0, g1, g2, g3, d0, d1, d2, d3, out_ref, *scratch):
    normed_ref, gu_ref, down_ref, total_ref, gu_sem, down_sem = scratch
    gates = (g0, g1, g2, g3)
    downs = (d0, d1, d2, d3)
    gate_copies = [pltpu.make_async_copy(gates[q], gu_ref.at[q], gu_sem.at[q]) for q in range(4)]
    down_copies = [pltpu.make_async_copy(downs[q], down_ref.at[q], down_sem.at[q]) for q in range(4)]
    for q in range(4):
        gate_copies[q].start()
        down_copies[q].start()
    for x in range(NX):
        parts = [rows_ref[x * NY + y].astype(jnp.float32) for y in range(NY)]
        square = sum(jnp.sum(part * part, axis=-1, keepdims=True) for part in parts)
        scale = lax.rsqrt(square * (1.0 / WIDTH) + 1e-06)
        for y in range(NY):
            columns = slice(y * QUARTER, (y + 1) * QUARTER)
            normed_ref[x * BLOCK : (x + 1) * BLOCK, columns] = (
                parts[y] * scale * gain_ref[:, columns]
            ).astype(jnp.bfloat16)
    for q in range(4):
        gate_copies[q].wait()
        both = jnp.dot(normed_ref[...], gu_ref[q], preferred_element_type=jnp.float32)
        gate, up = both[:, :EHQ], both[:, EHQ:]
        activation = (gate / (1.0 + jnp.exp(-gate)) * up).astype(jnp.bfloat16)
        down_copies[q].wait()
        part = jnp.dot(activation, down_ref[q], preferred_element_type=jnp.float32)
        if q == 0:
            total_ref[...] = part
        elif q < 3:
            total_ref[...] += part
        else:
            part = (total_ref[...] + part).astype(jnp.bfloat16)
            for x in range(NX):
                for y in range(NY):
                    out_ref[x * NY + y] = part[
                        x * BLOCK : (x + 1) * BLOCK, y * QUARTER : (y + 1) * QUARTER
                    ]


def vmem():
    return pl.BlockSpec(memory_space=pltpu.VMEM)


def params():
    return pltpu.CompilerParams(vmem_limit_bytes=VMEM_LIMIT)


def make_plan(base, meta):
    return pl.pallas_call(
        plan_kernel,
        out_shape=(
            jax.ShapeDtypeStruct((PLANE, TOKENS), jnp.int32),
            jax.ShapeDtypeStruct((PLANE, TOKENS), jnp.float32),
        ),
        in_specs=[pl.BlockSpec(memory_space=pltpu.SMEM), vmem()],
        out_specs=(vmem(), vmem()),
        compiler_params=params(),
        name="plan",
    )(base, meta)


def gather_rows(target, rows):
    return pl.pallas_call(
        gather_kernel,
        out_shape=jax.ShapeDtypeStruct((PLANE * BLOCK, QUARTER), jnp.bfloat16),
        in_specs=[vmem(), vmem()],
        out_specs=vmem(),
        scratch_shapes=[pltpu.VMEM((PLANE * BLOCK, TOKENS), jnp.bfloat16)],
        compiler_params=params(),
        name="gather_rows",
    )(target, rows)


def combine_rows(target, gate, rows):
    return pl.pallas_call(
        combine_kernel,
        out_shape=jax.ShapeDtypeStruct((TOKENS, QUARTER), jnp.bfloat16),
        in_specs=[vmem(), vmem(), vmem()],
        out_specs=vmem(),
        scratch_shapes=[pltpu.VMEM((PLANE * BLOCK, TOKENS), jnp.bfloat16)] * 2,
        compiler_params=params(),
        name="combine_rows",
    )(target, gate, rows)


def run_expert(rows, gain, gate_blocks, down_blocks):
    return pl.pallas_call(
        expert_kernel,
        out_shape=jax.ShapeDtypeStruct((PLANE, BLOCK, QUARTER), jnp.bfloat16),
        in_specs=[vmem(), vmem()] + [pl.BlockSpec(memory_space=pl.ANY)] * 8,
        out_specs=vmem(),
        scratch_shapes=[
            pltpu.VMEM((NX * BLOCK, WIDTH), jnp.bfloat16),
            pltpu.VMEM((4, WIDTH, 2 * EHQ), jnp.bfloat16),
            pltpu.VMEM((4, EHQ, WIDTH), jnp.bfloat16),
            pltpu.VMEM((NX * BLOCK, WIDTH), jnp.float32),
            pltpu.SemaphoreType.DMA((4,)),
            pltpu.SemaphoreType.DMA((4,)),
        ],
        compiler_params=params(),
        name="expert",
    )(rows, gain, *gate_blocks, *down_blocks)


def expert_weights(gate_up, down):
    y = lax.axis_index("y")
    even, odd = [], []
    for c in range(NC):
        for y_from in range(NY):
            source = c * NY + y_from
            core = y_from // 2
            even.append((source, core * NY + 2 * c + y_from % 2))
            odd.append((source, core * NY + 2 * c + 1 - y_from % 2))
    swap = [(0, 1), (1, 0)]
    gates, downs = [], []
    for index, moves in ((y % 2, even), (1 - y % 2, odd)):
        chosen = lax.dynamic_index_in_dim(gate_up, index, 0, keepdims=False)
        gate_block = jnp.concatenate([chosen[0], chosen[1]], axis=1)
        down_block = lax.dynamic_index_in_dim(down, index, 0, keepdims=False)
        gates.append(lax.ppermute(gate_block, ("c", "y"), moves))
        downs.append(lax.ppermute(down_block, ("c", "y"), moves))
    gates = gates + [lax.ppermute(block, "c", swap) for block in gates]
    downs = downs + [lax.ppermute(block, "c", swap) for block in downs]
    return gates, downs


def talker_plan(owners, section):
    own = lax.dynamic_slice_in_dim(owners, section * REQ, REQ)
    order = jnp.arange(REQ, dtype=jnp.int32)
    same = (own[:, None] == own[None, :]) & (order[:, None] > order[None, :])
    position = jnp.sum(same.astype(jnp.int32), axis=1)
    slot = jnp.where(own >= 0, own * HCAP + position, -1)
    send = (jnp.arange(SECTIONS * HCAP, dtype=jnp.int32)[:, None] == slot[None, :]).astype(
        jnp.bfloat16
    )
    counts = jnp.sum((owners == section).reshape(SECTIONS, REQ).astype(jnp.int32), axis=1)
    place = jnp.arange(SECTIONS, dtype=jnp.int32)
    offsets = jnp.sum(jnp.where(place[None, :] < place[:, None], counts[None, :], 0), axis=1)
    index = jnp.arange(HCAP, dtype=jnp.int32)
    put = jnp.where(index[None, :] < counts[:, None], offsets[:, None] + index[None, :], -1)
    put = put.reshape(SECTIONS * HCAP)
    take = (jnp.arange(SECTIONS * HCAP, dtype=jnp.int32)[:, None] == put[None, :]).astype(
        jnp.bfloat16
    )
    return send, take


def local(
    hidden_in,
    queries,
    new_kv,
    cache,
    lengths,
    out_weight,
    moe_gain,
    expert_ids,
    expert_gates,
    gate_up,
    down,
    owners,
):
    z, x, c, y = (lax.axis_index(name) for name in ("z", "x", "c", "y"))
    section = (z * NX + x) * NC + c
    gate_blocks, down_blocks = expert_weights(gate_up, down)

    meta = jnp.concatenate([expert_ids.astype(jnp.float32), expert_gates], axis=1).T
    meta = lax.all_to_all(jnp.broadcast_to(meta[None], (NZ, 16, REQ)), "z", 0, 0, tiled=True)
    meta = meta.transpose(1, 0, 2).reshape(16, TOKENS)

    context = attend_local(queries, new_kv, cache, lengths)
    attention = jnp.dot(context, out_weight, preferred_element_type=jnp.float32)
    pieces = attention.astype(jnp.bfloat16).reshape(REQ, NY, QUARTER).transpose(1, 0, 2)
    pieces = lax.all_to_all(pieces, "y", 0, 0, tiled=True)
    hidden = lax.dynamic_slice_in_dim(hidden_in, y * QUARTER, QUARTER, 1)
    middle = hidden.astype(jnp.float32) + jnp.sum(pieces.astype(jnp.float32), axis=0)
    middle = middle.astype(jnp.bfloat16)

    spread = lax.all_to_all(
        jnp.broadcast_to(middle[None], (NZ, REQ, QUARTER)), "z", 0, 0, tiled=True
    )
    target, gate = make_plan((z * PLANE).astype(jnp.int32).reshape(1), meta)
    send = gather_rows(target, spread.reshape(TOKENS, QUARTER))
    rows = lax.all_to_all(
        send.reshape(PLANE, BLOCK, QUARTER), ("x", "y"), 0, 0, tiled=True
    )
    done = run_expert(rows, moe_gain.reshape(1, WIDTH), gate_blocks, down_blocks)
    back = lax.all_to_all(done, ("x", "y"), 0, 0, tiled=True)
    part = combine_rows(target, gate, back.reshape(PLANE * BLOCK, QUARTER))
    part = lax.all_to_all(part.reshape(NZ, REQ, QUARTER), "z", 0, 0, tiled=True)
    out = middle.astype(jnp.float32) + jnp.sum(part.astype(jnp.float32), axis=0)
    out = out.astype(jnp.bfloat16)

    send_pick, take_pick = talker_plan(owners, section)
    leaving = jnp.dot(send_pick, out, preferred_element_type=jnp.float32).astype(jnp.bfloat16)
    arrived = lax.all_to_all(
        leaving.reshape(SECTIONS, HCAP, QUARTER), ("z", "x", "c"), 0, 0, tiled=True
    )
    talker = jnp.dot(
        take_pick, arrived.reshape(SECTIONS * HCAP, QUARTER), preferred_element_type=jnp.float32
    ).astype(jnp.bfloat16)
    return (out, talker)


def solution(mesh):
    section = ("z", "x", "c")
    fine = Mesh(mesh.devices.reshape(NZ, NX, NC, NY), ("z", "x", "c", "y"))
    in_specs = (
        P(section, None),
        P(section, "y"),
        P(section, None, "y"),
        P(section, None, None, "y"),
        P(section),
        P("y", None),
        P(),
        P(section, None),
        P(section, None),
        P(section, None, None, "y"),
        P(section, "y", None),
        P(),
    )
    out_specs = (P(section, "y"), P(section, "y"))
    return jax.shard_map(local, mesh=fine, in_specs=in_specs, out_specs=out_specs, check_vma=False)
```

```python
import math

import jax
import jax.numpy as jnp
from jax import lax
from jax.experimental import pallas as pl
from jax.experimental.pallas import tpu as pltpu
from jax.sharding import Mesh
from jax.sharding import PartitionSpec as P

HD = 128
HCAP = 2
CAP = 10
NZ, NX, NC, NY = 8, 4, 2, 4
REQ = 64
SECTIONS = NZ * NX * NC
TOKENS = NZ * REQ
PLANE = NX * NY
BLOCK = NZ * CAP
QUARTER = 512
WIDTH = 2048
EHQ = 192


def attend_local(queries, new_kv, cache, lengths):
    req_count = queries.shape[0]
    cached_count = cache.shape[2]
    kv_local = new_kv.shape[2] // HD
    group_size = queries.shape[1] // (kv_local * HD)
    query_heads = queries.reshape(req_count, kv_local, group_size, HD)
    cache_keys = cache[:, 0].reshape(req_count, cached_count, kv_local, HD)
    cache_values = cache[:, 1].reshape(req_count, cached_count, kv_local, HD)
    fresh_keys = new_kv[:, 0].reshape(req_count, kv_local, HD)
    fresh_values = new_kv[:, 1].reshape(req_count, kv_local, HD)
    scale_factor = 1.0 / math.sqrt(HD)
    cache_scores = (
        jnp.einsum("rkgd,rckd->rkgc", query_heads, cache_keys, preferred_element_type=jnp.float32)
        * scale_factor
    )
    valid_cells = jnp.arange(cached_count)[None, :] < lengths[:, None]
    cache_scores = jnp.where(valid_cells[:, None, None, :], cache_scores, -jnp.inf)
    fresh_scores = (
        jnp.einsum("rkgd,rkd->rkg", query_heads, fresh_keys, preferred_element_type=jnp.float32)
        * scale_factor
    )
    top_score = jnp.maximum(jnp.max(cache_scores, axis=-1), fresh_scores)
    cache_exp = jnp.exp(cache_scores - top_score[..., None])
    fresh_exp = jnp.exp(fresh_scores - top_score)
    total_mass = jnp.sum(cache_exp, axis=-1) + fresh_exp
    cache_weights = (cache_exp / total_mass[..., None]).astype(jnp.bfloat16)
    fresh_weights = (fresh_exp / total_mass).astype(jnp.bfloat16)
    context = jnp.einsum(
        "rkgc,rckd->rkgd", cache_weights, cache_values, preferred_element_type=jnp.float32
    )
    context = (
        context
        + fresh_weights.astype(jnp.float32)[..., None]
        * fresh_values.astype(jnp.float32)[:, :, None, :]
    )
    return context.reshape(req_count, kv_local * group_size * HD).astype(jnp.bfloat16)


def plan_kernel(ids_ref, gates_ref, out_ref):
    ids = jnp.concatenate([ids_ref[...], ids_ref[...]], axis=1)
    gates = jnp.concatenate([gates_ref[...], gates_ref[...]], axis=1)
    gates = gates / jnp.sum(gates, axis=0, keepdims=True)
    experts = NZ * PLANE
    expert = lax.broadcasted_iota(jnp.int32, (experts, 2 * REQ), 0)
    chosen = jnp.zeros((experts, 2 * REQ), jnp.float32)
    gate = jnp.zeros((experts, 2 * REQ), jnp.float32)
    for k in range(8):
        hit = ids[k : k + 1, :] == expert
        chosen = jnp.where(hit, 1.0, chosen)
        gate = jnp.where(hit, gates[k : k + 1, :], gate)
    earlier = lax.broadcasted_iota(jnp.int32, (2 * REQ, 2 * REQ), 0)
    token = lax.broadcasted_iota(jnp.int32, (2 * REQ, 2 * REQ), 1)
    token = jnp.where(token >= REQ, token - REQ, token)
    before = jnp.where(earlier < token, 1.0, 0.0).astype(jnp.bfloat16)
    rank = jnp.dot(chosen.astype(jnp.bfloat16), before, preferred_element_type=jnp.float32)
    slot = jnp.where(chosen > 0.0, rank, -1.0).astype(jnp.bfloat16)
    gate = gate.astype(jnp.bfloat16)
    out_ref[...] = jnp.zeros((NZ, PLANE, QUARTER), jnp.bfloat16)
    for z in range(NZ):
        out_ref[z, :, : 2 * REQ] = slot[z * PLANE : (z + 1) * PLANE, :]
        out_ref[z, :, 2 * REQ : 4 * REQ] = gate[z * PLANE : (z + 1) * PLANE, :]


def pick_kernel(first_ref, after_ref, gate_up, down, even_ref, odd_ref, sems):
    first = first_ref[0]
    copies = []
    for k, out in ((0, even_ref), (1, odd_ref)):
        index = first if k == 0 else 1 - first
        copies.append(pltpu.make_async_copy(gate_up.at[index], out.at[pl.ds(0, 2)], sems.at[2 * k]))
        copies.append(pltpu.make_async_copy(down.at[index], out.at[2], sems.at[2 * k + 1]))
    for copy in copies:
        copy.start()
    for copy in copies:
        copy.wait()


def middle_kernel(pieces_ref, hidden_ref, plan_ref, *refs):
    message_ref, middle_ref = refs[2:4]
    total = hidden_ref[...].astype(jnp.float32)
    for y in range(NY):
        total = total + pieces_ref[y].astype(jnp.float32)
    middle = total.astype(jnp.bfloat16)
    middle_ref[...] = middle
    for z in range(NZ):
        message_ref[z, :REQ, :] = middle
        message_ref[z, REQ:, :] = plan_ref[z]


def gather_kernel(spread_ref, out_ref, target_ref, gate_ref, pick_ref, rows_ref):
    low = lax.broadcasted_iota(jnp.int32, (PLANE, 2 * REQ), 1) < REQ
    for pair in range(NZ // 2):
        left, right = spread_ref[2 * pair, REQ:, :], spread_ref[2 * pair + 1, REQ:, :]
        left, right = left.astype(jnp.float32), right.astype(jnp.float32)
        both = jnp.where(low, left[:, : 2 * REQ], right[:, : 2 * REQ])
        block = jnp.where(low, float(2 * pair * CAP), float((2 * pair + 1) * CAP))
        columns = slice(pair * 2 * REQ, (pair + 1) * 2 * REQ)
        target_ref[:, columns] = jnp.where(both >= 0.0, both + block, -1.0)
        gate_ref[:, columns] = jnp.where(
            low, left[:, 2 * REQ : 4 * REQ], right[:, 2 * REQ : 4 * REQ]
        )
    for z in range(NZ):
        rows_ref[z * REQ : (z + 1) * REQ, :] = spread_ref[z, :REQ, :]
    slot = lax.broadcasted_iota(jnp.int32, (BLOCK, TOKENS), 0).astype(jnp.float32)
    for e in range(PLANE):
        hit = target_ref[e : e + 1, :] == slot
        pick_ref[e * BLOCK : (e + 1) * BLOCK, :] = jnp.where(hit, 1.0, 0.0).astype(jnp.bfloat16)
    for e in range(0, PLANE, 4):
        rows = jnp.dot(
            pick_ref[e * BLOCK : (e + 4) * BLOCK, :],
            rows_ref[...],
            preferred_element_type=jnp.float32,
        ).astype(jnp.bfloat16)
        for k in range(4):
            out_ref[e + k] = rows[k * BLOCK : (k + 1) * BLOCK, :]


def hold_kernel(*refs):
    del refs


def combine_kernel(target_ref, gate_ref, rows_ref, out_ref, weight_ref, packed_ref):
    slot = lax.broadcasted_iota(jnp.int32, (BLOCK, TOKENS), 0).astype(jnp.float32)
    for e in range(PLANE):
        hit = target_ref[e : e + 1, :] == slot
        weight = jnp.where(hit, gate_ref[e : e + 1, :], 0.0)
        weight_ref[e * BLOCK : (e + 1) * BLOCK, :] = weight.astype(jnp.bfloat16)
        packed_ref[e * BLOCK : (e + 1) * BLOCK, :] = rows_ref[e]
    dims = (((0,), (0,)), ((), ()))
    total = lax.dot_general(
        weight_ref[...], packed_ref[...], dims, preferred_element_type=jnp.float32
    ).astype(jnp.bfloat16)
    for z in range(NZ):
        out_ref[z] = total[z * REQ : (z + 1) * REQ, :]


def expert_kernel(rows_ref, gain_ref, w0, w1, w2, w3, out_ref, *scratch):
    normed_ref, weight_ref, act_ref, sems = scratch
    copies = []
    for part in range(3):
        for q, block in enumerate((w0, w1, w2, w3)):
            copies.append(
                pltpu.make_async_copy(
                    block.at[part], weight_ref.at[part, pl.ds(q * EHQ, EHQ)], sems.at[part, q]
                )
            )
    for copy in copies:
        copy.start()
    for x in range(NX):
        parts = [rows_ref[x * NY + y].astype(jnp.float32) for y in range(NY)]
        square = sum(jnp.sum(part * part, axis=-1, keepdims=True) for part in parts)
        scale = lax.rsqrt(square * (1.0 / WIDTH) + 1e-06)
        for y in range(NY):
            columns = slice(y * QUARTER, (y + 1) * QUARTER)
            normed_ref[x * BLOCK : (x + 1) * BLOCK, columns] = (
                parts[y] * scale * gain_ref[:, columns]
            ).astype(jnp.bfloat16)
    dims = (((1,), (1,)), ((), ()))
    for copy in copies[:4]:
        copy.wait()
    gate = lax.dot_general(
        normed_ref[...], weight_ref[0], dims, preferred_element_type=jnp.float32
    )
    for copy in copies[4:8]:
        copy.wait()
    up = lax.dot_general(normed_ref[...], weight_ref[1], dims, preferred_element_type=jnp.float32)
    act_ref[...] = (gate / (1.0 + jnp.exp(-gate)) * up).astype(jnp.bfloat16)
    for copy in copies[8:]:
        copy.wait()
    for y in range(NY):
        part = jnp.dot(
            act_ref[...],
            weight_ref[2, :, y * QUARTER : (y + 1) * QUARTER],
            preferred_element_type=jnp.float32,
        ).astype(jnp.bfloat16)
        for x in range(NX):
            out_ref[x * NY + y] = part[x * BLOCK : (x + 1) * BLOCK, :]


def vmem():
    return pl.BlockSpec(memory_space=pltpu.VMEM)


def anywhere():
    return pl.BlockSpec(memory_space=pl.ANY)


def params(mib=16):
    return pltpu.CompilerParams(vmem_limit_bytes=mib * 1024 * 1024)


def shape(*dims, dtype=jnp.bfloat16):
    return jax.ShapeDtypeStruct(dims, dtype)


def make_plan(ids, gates):
    return pl.pallas_call(
        plan_kernel,
        out_shape=shape(NZ, PLANE, QUARTER),
        in_specs=[vmem(), vmem()],
        out_specs=vmem(),
        compiler_params=params(),
        name="plan",
    )(ids, gates)


def pick_weights(first, after, gate_up, down):
    block = shape(3, EHQ, WIDTH)
    return pl.pallas_call(
        pick_kernel,
        out_shape=(block, block),
        in_specs=[pl.BlockSpec(memory_space=pltpu.SMEM)] + [anywhere()] * 3,
        out_specs=(anywhere(), anywhere()),
        scratch_shapes=[pltpu.SemaphoreType.DMA((4,))],
        compiler_params=params(),
        name="pick_weights",
    )(first, after, gate_up, down)


def sum_middle(pieces, hidden, plan, blocks):
    return pl.pallas_call(
        middle_kernel,
        out_shape=(
            shape(NZ, REQ + PLANE, QUARTER),
            shape(REQ, QUARTER),
            *[shape(*block.shape) for block in blocks],
        ),
        in_specs=[vmem()] * 3 + [anywhere()] * 2,
        out_specs=(vmem(), vmem()) + (anywhere(),) * 2,
        input_output_aliases={3 + k: 2 + k for k in range(2)},
        compiler_params=params(),
        name="sum_middle",
    )(pieces, hidden, plan, *blocks)


def gather_rows(spread):
    return pl.pallas_call(
        gather_kernel,
        out_shape=(
            shape(PLANE, BLOCK, QUARTER),
            shape(PLANE, TOKENS, dtype=jnp.float32),
            shape(PLANE, TOKENS, dtype=jnp.float32),
        ),
        in_specs=[vmem()],
        out_specs=(vmem(), vmem(), vmem()),
        scratch_shapes=[
            pltpu.VMEM((PLANE * BLOCK, TOKENS), jnp.bfloat16),
            pltpu.VMEM((TOKENS, QUARTER), jnp.bfloat16),
        ],
        compiler_params=params(),
        name="gather_rows",
    )(spread)


def hold(after, blocks):
    return pl.pallas_call(
        hold_kernel,
        out_shape=tuple(shape(*block.shape) for block in blocks),
        in_specs=[anywhere()] * 3,
        out_specs=(anywhere(),) * 2,
        input_output_aliases={1 + k: k for k in range(2)},
        compiler_params=params(),
        name="hold",
    )(after, *blocks)


def combine_rows(target, gate, rows):
    return pl.pallas_call(
        combine_kernel,
        out_shape=shape(NZ, REQ, QUARTER),
        in_specs=[vmem(), vmem(), vmem()],
        out_specs=vmem(),
        scratch_shapes=[
            pltpu.VMEM((PLANE * BLOCK, TOKENS), jnp.bfloat16),
            pltpu.VMEM((PLANE * BLOCK, QUARTER), jnp.bfloat16),
        ],
        compiler_params=params(),
        name="combine_rows",
    )(target, gate, rows)


def run_expert(rows, gain, blocks):
    return pl.pallas_call(
        expert_kernel,
        out_shape=shape(PLANE, BLOCK, QUARTER),
        in_specs=[vmem(), vmem()] + [anywhere()] * 4,
        out_specs=vmem(),
        scratch_shapes=[
            pltpu.VMEM((NX * BLOCK, WIDTH), jnp.bfloat16),
            pltpu.VMEM((3, 4 * EHQ, WIDTH), jnp.bfloat16),
            pltpu.VMEM((NX * BLOCK, 4 * EHQ), jnp.bfloat16),
            pltpu.SemaphoreType.DMA((3, 4)),
        ],
        compiler_params=params(32),
        name="expert",
    )(rows, gain, *blocks)


def move_weights(blocks):
    even, odd = [], []
    for c in range(NC):
        for y in range(NY):
            core = (y // 2) * NY
            even.append((c * NY + y, core + 2 * c + y % 2))
            odd.append((c * NY + y, core + 2 * c + 1 - y % 2))
    return [lax.ppermute(block, ("c", "y"), to) for block, to in zip(blocks, (even, odd))]


def talker_plan(owners, section):
    own = lax.dynamic_slice_in_dim(owners, section * REQ, REQ)
    order = jnp.arange(REQ, dtype=jnp.int32)
    same = (own[:, None] == own[None, :]) & (order[:, None] > order[None, :])
    position = jnp.sum(same.astype(jnp.int32), axis=1)
    slot = jnp.where(own >= 0, own * HCAP + position, -1)
    send = (jnp.arange(SECTIONS * HCAP, dtype=jnp.int32)[:, None] == slot[None, :]).astype(
        jnp.bfloat16
    )
    counts = jnp.sum((owners == section).reshape(SECTIONS, REQ).astype(jnp.int32), axis=1)
    place = jnp.arange(SECTIONS, dtype=jnp.int32)
    offsets = jnp.sum(jnp.where(place[None, :] < place[:, None], counts[None, :], 0), axis=1)
    index = jnp.arange(HCAP, dtype=jnp.int32)
    put = jnp.where(index[None, :] < counts[:, None], offsets[:, None] + index[None, :], -1)
    put = put.reshape(SECTIONS * HCAP)
    take = (jnp.arange(SECTIONS * HCAP, dtype=jnp.int32)[:, None] == put[None, :]).astype(
        jnp.bfloat16
    )
    return send, take


def local(
    hidden_in,
    queries,
    new_kv,
    cache,
    lengths,
    out_weight,
    moe_gain,
    expert_ids,
    expert_gates,
    gate_up,
    down,
    owners,
):
    z, x, c, y = (lax.axis_index(name) for name in ("z", "x", "c", "y"))
    section = (z * NX + x) * NC + c
    plan = make_plan(expert_ids.T, expert_gates.T)
    context = attend_local(queries, new_kv, cache, lengths)
    attention = jnp.dot(context, out_weight, preferred_element_type=jnp.float32)
    pieces = attention.astype(jnp.bfloat16).reshape(REQ, NY, QUARTER).transpose(1, 0, 2)
    first = (y % 2).astype(jnp.int32).reshape(1)
    blocks = pick_weights(first, pieces, gate_up.transpose(0, 1, 3, 2), down)
    pieces = lax.all_to_all(pieces, "y", 0, 0, tiled=True)
    hidden = lax.dynamic_slice_in_dim(hidden_in, y * QUARTER, QUARTER, 1)
    message, middle, *blocks = sum_middle(pieces, hidden, plan, blocks)
    blocks = move_weights(blocks)

    spread = lax.all_to_all(message, "z", 0, 0, tiled=True)
    send, target, gate = gather_rows(spread)
    blocks = hold(send, blocks)
    swapped = [lax.ppermute(block, "c", [(0, 1), (1, 0)]) for block in blocks]
    rows = lax.all_to_all(send, ("x", "y"), 0, 0, tiled=True)
    done = run_expert(rows, moe_gain.reshape(1, WIDTH), (*blocks, *swapped))
    back = lax.all_to_all(done, ("x", "y"), 0, 0, tiled=True)
    part = combine_rows(target, gate, back)
    part = lax.all_to_all(part, "z", 0, 0, tiled=True)
    out = middle.astype(jnp.float32) + jnp.sum(part.astype(jnp.float32), axis=0)
    out = out.astype(jnp.bfloat16)

    send_pick, take_pick = talker_plan(owners, section)
    leaving = jnp.dot(send_pick, out, preferred_element_type=jnp.float32).astype(jnp.bfloat16)
    arrived = lax.all_to_all(
        leaving.reshape(SECTIONS, HCAP, QUARTER), ("z", "x", "c"), 0, 0, tiled=True
    )
    talker = jnp.dot(
        take_pick, arrived.reshape(SECTIONS * HCAP, QUARTER), preferred_element_type=jnp.float32
    ).astype(jnp.bfloat16)
    return (out, talker)


def solution(mesh):
    section = ("z", "x", "c")
    fine = Mesh(mesh.devices.reshape(NZ, NX, NC, NY), ("z", "x", "c", "y"))
    in_specs = (
        P(section, None),
        P(section, "y"),
        P(section, None, "y"),
        P(section, None, None, "y"),
        P(section),
        P("y", None),
        P(),
        P(section, None),
        P(section, None),
        P(section, None, None, "y"),
        P(section, "y", None),
        P(),
    )
    out_specs = (P(section, "y"), P(section, "y"))
    return jax.shard_map(local, mesh=fine, in_specs=in_specs, out_specs=out_specs, check_vma=False)
```

```python
import math

import jax
import jax.numpy as jnp
from jax import lax
from jax.experimental import pallas as pl
from jax.experimental.pallas import tpu as pltpu
from jax.sharding import Mesh
from jax.sharding import PartitionSpec as P

HD = 128
HCAP = 2
CAP = 10
NZ, NX, NC, NY = 8, 4, 2, 4
REQ = 64
SECTIONS = NZ * NX * NC
TOKENS = NZ * REQ
PLANE = NX * NY
BLOCK = NZ * CAP
QUARTER = 512
WIDTH = 2048
EHQ = 192


def attend_local(queries, new_kv, cache, lengths):
    req_count = queries.shape[0]
    cached_count = cache.shape[2]
    kv_local = new_kv.shape[2] // HD
    group_size = queries.shape[1] // (kv_local * HD)
    query_heads = queries.reshape(req_count, kv_local, group_size, HD)
    cache_keys = cache[:, 0].reshape(req_count, cached_count, kv_local, HD)
    cache_values = cache[:, 1].reshape(req_count, cached_count, kv_local, HD)
    fresh_keys = new_kv[:, 0].reshape(req_count, kv_local, HD)
    fresh_values = new_kv[:, 1].reshape(req_count, kv_local, HD)
    scale_factor = 1.0 / math.sqrt(HD)
    cache_scores = (
        jnp.einsum("rkgd,rckd->rkgc", query_heads, cache_keys, preferred_element_type=jnp.float32)
        * scale_factor
    )
    valid_cells = jnp.arange(cached_count)[None, :] < lengths[:, None]
    cache_scores = jnp.where(valid_cells[:, None, None, :], cache_scores, -jnp.inf)
    fresh_scores = (
        jnp.einsum("rkgd,rkd->rkg", query_heads, fresh_keys, preferred_element_type=jnp.float32)
        * scale_factor
    )
    top_score = jnp.maximum(jnp.max(cache_scores, axis=-1), fresh_scores)
    cache_exp = jnp.exp(cache_scores - top_score[..., None])
    fresh_exp = jnp.exp(fresh_scores - top_score)
    total_mass = jnp.sum(cache_exp, axis=-1) + fresh_exp
    cache_weights = (cache_exp / total_mass[..., None]).astype(jnp.bfloat16)
    fresh_weights = (fresh_exp / total_mass).astype(jnp.bfloat16)
    context = jnp.einsum(
        "rkgc,rckd->rkgd", cache_weights, cache_values, preferred_element_type=jnp.float32
    )
    context = (
        context
        + fresh_weights.astype(jnp.float32)[..., None]
        * fresh_values.astype(jnp.float32)[:, :, None, :]
    )
    return context.reshape(req_count, kv_local * group_size * HD).astype(jnp.bfloat16)


def plan_kernel(ids_ref, gates_ref, out_ref):
    ids = jnp.concatenate([ids_ref[...], ids_ref[...]], axis=1)
    gates = jnp.concatenate([gates_ref[...], gates_ref[...]], axis=1)
    gates = gates / jnp.sum(gates, axis=0, keepdims=True)
    experts = NZ * PLANE
    expert = lax.broadcasted_iota(jnp.int32, (experts, 2 * REQ), 0)
    chosen = jnp.zeros((experts, 2 * REQ), jnp.float32)
    gate = jnp.zeros((experts, 2 * REQ), jnp.float32)
    for k in range(8):
        hit = ids[k : k + 1, :] == expert
        chosen = jnp.where(hit, 1.0, chosen)
        gate = jnp.where(hit, gates[k : k + 1, :], gate)
    earlier = lax.broadcasted_iota(jnp.int32, (2 * REQ, 2 * REQ), 0)
    token = lax.broadcasted_iota(jnp.int32, (2 * REQ, 2 * REQ), 1)
    token = jnp.where(token >= REQ, token - REQ, token)
    before = jnp.where(earlier < token, 1.0, 0.0).astype(jnp.bfloat16)
    rank = jnp.dot(chosen.astype(jnp.bfloat16), before, preferred_element_type=jnp.float32)
    slot = jnp.where(chosen > 0.0, rank, -1.0).astype(jnp.bfloat16)
    gate = gate.astype(jnp.bfloat16)
    out_ref[...] = jnp.zeros((NZ, PLANE, QUARTER), jnp.bfloat16)
    for z in range(NZ):
        out_ref[z, :, : 2 * REQ] = slot[z * PLANE : (z + 1) * PLANE, :]
        out_ref[z, :, 2 * REQ : 4 * REQ] = gate[z * PLANE : (z + 1) * PLANE, :]


def pick_kernel(first_ref, after_ref, gate_up, down, even_ref, odd_ref, sems):
    first = first_ref[0]
    copies = []
    for k, out in ((0, even_ref), (1, odd_ref)):
        index = first if k == 0 else 1 - first
        copies.append(pltpu.make_async_copy(gate_up.at[index], out.at[pl.ds(0, 2)], sems.at[2 * k]))
        copies.append(pltpu.make_async_copy(down.at[index], out.at[2], sems.at[2 * k + 1]))
    for copy in copies:
        copy.start()
    for copy in copies:
        copy.wait()


def middle_kernel(pieces_ref, hidden_ref, plan_ref, message_ref, middle_ref):
    total = hidden_ref[...].astype(jnp.float32)
    for y in range(NY):
        total = total + pieces_ref[y].astype(jnp.float32)
    middle = total.astype(jnp.bfloat16)
    middle_ref[...] = middle
    for z in range(NZ):
        message_ref[z, :REQ, :] = middle
        message_ref[z, REQ:, :] = plan_ref[z]


def gather_kernel(spread_ref, out_ref, target_ref, gate_ref, pick_ref, rows_ref):
    low = lax.broadcasted_iota(jnp.int32, (PLANE, 2 * REQ), 1) < REQ
    for pair in range(NZ // 2):
        left, right = spread_ref[2 * pair, REQ:, :], spread_ref[2 * pair + 1, REQ:, :]
        left, right = left.astype(jnp.float32), right.astype(jnp.float32)
        both = jnp.where(low, left[:, : 2 * REQ], right[:, : 2 * REQ])
        block = jnp.where(low, float(2 * pair * CAP), float((2 * pair + 1) * CAP))
        columns = slice(pair * 2 * REQ, (pair + 1) * 2 * REQ)
        target_ref[:, columns] = jnp.where(both >= 0.0, both + block, -1.0)
        gate_ref[:, columns] = jnp.where(
            low, left[:, 2 * REQ : 4 * REQ], right[:, 2 * REQ : 4 * REQ]
        )
    for z in range(NZ):
        rows_ref[z * REQ : (z + 1) * REQ, :] = spread_ref[z, :REQ, :]
    slot = lax.broadcasted_iota(jnp.int32, (BLOCK, TOKENS), 0).astype(jnp.float32)
    for e in range(PLANE):
        hit = target_ref[e : e + 1, :] == slot
        pick_ref[e * BLOCK : (e + 1) * BLOCK, :] = jnp.where(hit, 1.0, 0.0).astype(jnp.bfloat16)
    for e in range(0, PLANE, 4):
        rows = jnp.dot(
            pick_ref[e * BLOCK : (e + 4) * BLOCK, :],
            rows_ref[...],
            preferred_element_type=jnp.float32,
        ).astype(jnp.bfloat16)
        for k in range(4):
            out_ref[e + k] = rows[k * BLOCK : (k + 1) * BLOCK, :]


def hold_kernel(*refs):
    del refs


def combine_kernel(target_ref, gate_ref, rows_ref, out_ref, weight_ref, packed_ref):
    slot = lax.broadcasted_iota(jnp.int32, (BLOCK, TOKENS), 0).astype(jnp.float32)
    for e in range(PLANE):
        hit = target_ref[e : e + 1, :] == slot
        weight = jnp.where(hit, gate_ref[e : e + 1, :], 0.0)
        weight_ref[e * BLOCK : (e + 1) * BLOCK, :] = weight.astype(jnp.bfloat16)
        packed_ref[e * BLOCK : (e + 1) * BLOCK, :] = rows_ref[e]
    dims = (((0,), (0,)), ((), ()))
    total = lax.dot_general(
        weight_ref[...], packed_ref[...], dims, preferred_element_type=jnp.float32
    ).astype(jnp.bfloat16)
    for z in range(NZ):
        out_ref[z] = total[z * REQ : (z + 1) * REQ, :]


def load_weights(blocks, weight_ref, sems):
    copies = []
    for part in range(3):
        for q, block in enumerate(blocks):
            copies.append(
                pltpu.make_async_copy(
                    block.at[part], weight_ref.at[part, pl.ds(q * EHQ, EHQ)], sems.at[part, q]
                )
            )
    for copy in copies:
        copy.start()
    return copies


def activate(normed_ref, weight_ref, act_ref, copies):
    dims = (((1,), (1,)), ((), ()))
    for copy in copies[:2]:
        copy.wait()
    gate = lax.dot_general(
        normed_ref[...], weight_ref[0], dims, preferred_element_type=jnp.float32
    )
    for copy in copies[2:4]:
        copy.wait()
    up = lax.dot_general(normed_ref[...], weight_ref[1], dims, preferred_element_type=jnp.float32)
    act_ref[...] = (gate / (1.0 + jnp.exp(-gate)) * up).astype(jnp.bfloat16)
    for copy in copies[4:]:
        copy.wait()


def first_half_kernel(rows_ref, gain_ref, w0, w1, normed_ref, part_ref, weight_ref, act_ref, sems):
    copies = load_weights((w0, w1), weight_ref, sems)
    for x in range(NX):
        parts = [rows_ref[x * NY + y].astype(jnp.float32) for y in range(NY)]
        square = sum(jnp.sum(part * part, axis=-1, keepdims=True) for part in parts)
        scale = lax.rsqrt(square * (1.0 / WIDTH) + 1e-06)
        for y in range(NY):
            columns = slice(y * QUARTER, (y + 1) * QUARTER)
            normed_ref[x * BLOCK : (x + 1) * BLOCK, columns] = (
                parts[y] * scale * gain_ref[:, columns]
            ).astype(jnp.bfloat16)
    activate(normed_ref, weight_ref, act_ref, copies)
    part_ref[...] = jnp.dot(act_ref[...], weight_ref[2], preferred_element_type=jnp.float32)


def second_half_kernel(normed_ref, part_ref, w2, w3, out_ref, weight_ref, act_ref, sems):
    copies = load_weights((w2, w3), weight_ref, sems)
    activate(normed_ref, weight_ref, act_ref, copies)
    for y in range(NY):
        columns = slice(y * QUARTER, (y + 1) * QUARTER)
        part = part_ref[:, columns] + jnp.dot(
            act_ref[...], weight_ref[2, :, columns], preferred_element_type=jnp.float32
        )
        part = part.astype(jnp.bfloat16)
        for x in range(NX):
            out_ref[x * NY + y] = part[x * BLOCK : (x + 1) * BLOCK, :]


def vmem():
    return pl.BlockSpec(memory_space=pltpu.VMEM)


def anywhere():
    return pl.BlockSpec(memory_space=pl.ANY)


def params(mib=16):
    return pltpu.CompilerParams(vmem_limit_bytes=mib * 1024 * 1024)


def shape(*dims, dtype=jnp.bfloat16):
    return jax.ShapeDtypeStruct(dims, dtype)


def make_plan(ids, gates):
    return pl.pallas_call(
        plan_kernel,
        out_shape=shape(NZ, PLANE, QUARTER),
        in_specs=[vmem(), vmem()],
        out_specs=vmem(),
        compiler_params=params(),
        name="plan",
    )(ids, gates)


def pick_weights(first, after, gate_up, down):
    block = shape(3, EHQ, WIDTH)
    return pl.pallas_call(
        pick_kernel,
        out_shape=(block, block),
        in_specs=[pl.BlockSpec(memory_space=pltpu.SMEM), anywhere()]
        + [pl.BlockSpec(memory_space=pltpu.HBM)] * 2,
        out_specs=(anywhere(), anywhere()),
        scratch_shapes=[pltpu.SemaphoreType.DMA((4,))],
        compiler_params=params(),
        name="pick_weights",
    )(first, after, gate_up, down)


def sum_middle(pieces, hidden, plan):
    return pl.pallas_call(
        middle_kernel,
        out_shape=(shape(NZ, REQ + PLANE, QUARTER), shape(REQ, QUARTER)),
        in_specs=[vmem()] * 3,
        out_specs=(vmem(), vmem()),
        compiler_params=params(),
        name="sum_middle",
    )(pieces, hidden, plan)


def gather_rows(spread):
    return pl.pallas_call(
        gather_kernel,
        out_shape=(
            shape(PLANE, BLOCK, QUARTER),
            shape(PLANE, TOKENS, dtype=jnp.float32),
            shape(PLANE, TOKENS, dtype=jnp.float32),
        ),
        in_specs=[vmem()],
        out_specs=(vmem(), vmem(), vmem()),
        scratch_shapes=[
            pltpu.VMEM((PLANE * BLOCK, TOKENS), jnp.bfloat16),
            pltpu.VMEM((TOKENS, QUARTER), jnp.bfloat16),
        ],
        compiler_params=params(),
        name="gather_rows",
    )(spread)


def hold(after, blocks):
    return pl.pallas_call(
        hold_kernel,
        out_shape=tuple(shape(*block.shape) for block in blocks),
        in_specs=[anywhere()] * 3,
        out_specs=(anywhere(),) * 2,
        input_output_aliases={1 + k: k for k in range(2)},
        compiler_params=params(),
        name="hold",
    )(after, *blocks)


def combine_rows(target, gate, rows):
    return pl.pallas_call(
        combine_kernel,
        out_shape=shape(NZ, REQ, QUARTER),
        in_specs=[vmem(), vmem(), vmem()],
        out_specs=vmem(),
        scratch_shapes=[
            pltpu.VMEM((PLANE * BLOCK, TOKENS), jnp.bfloat16),
            pltpu.VMEM((PLANE * BLOCK, QUARTER), jnp.bfloat16),
        ],
        compiler_params=params(),
        name="combine_rows",
    )(target, gate, rows)


def half_scratch():
    return [
        pltpu.VMEM((3, 2 * EHQ, WIDTH), jnp.bfloat16),
        pltpu.VMEM((NX * BLOCK, 2 * EHQ), jnp.bfloat16),
        pltpu.SemaphoreType.DMA((3, 2)),
    ]


def first_half(rows, gain, blocks):
    return pl.pallas_call(
        first_half_kernel,
        out_shape=(shape(NX * BLOCK, WIDTH), shape(NX * BLOCK, WIDTH, dtype=jnp.float32)),
        in_specs=[vmem(), vmem()] + [anywhere()] * 2,
        out_specs=(vmem(), vmem()),
        scratch_shapes=half_scratch(),
        compiler_params=params(24),
        name="first_half",
    )(rows, gain, *blocks)


def second_half(normed, part, blocks):
    return pl.pallas_call(
        second_half_kernel,
        out_shape=shape(PLANE, BLOCK, QUARTER),
        in_specs=[vmem(), vmem()] + [anywhere()] * 2,
        out_specs=vmem(),
        scratch_shapes=half_scratch(),
        compiler_params=params(24),
        name="second_half",
    )(normed, part, *blocks)


def move_weights(blocks):
    even, odd = [], []
    for c in range(NC):
        for y in range(NY):
            core = (y // 2) * NY
            even.append((c * NY + y, core + 2 * c + y % 2))
            odd.append((c * NY + y, core + 2 * c + 1 - y % 2))
    return [lax.ppermute(block, ("c", "y"), to) for block, to in zip(blocks, (even, odd))]


def talker_plan(owners, section):
    own = lax.dynamic_slice_in_dim(owners, section * REQ, REQ)
    order = jnp.arange(REQ, dtype=jnp.int32)
    same = (own[:, None] == own[None, :]) & (order[:, None] > order[None, :])
    position = jnp.sum(same.astype(jnp.int32), axis=1)
    slot = jnp.where(own >= 0, own * HCAP + position, -1)
    send = (jnp.arange(SECTIONS * HCAP, dtype=jnp.int32)[:, None] == slot[None, :]).astype(
        jnp.bfloat16
    )
    counts = jnp.sum((owners == section).reshape(SECTIONS, REQ).astype(jnp.int32), axis=1)
    place = jnp.arange(SECTIONS, dtype=jnp.int32)
    offsets = jnp.sum(jnp.where(place[None, :] < place[:, None], counts[None, :], 0), axis=1)
    index = jnp.arange(HCAP, dtype=jnp.int32)
    put = jnp.where(index[None, :] < counts[:, None], offsets[:, None] + index[None, :], -1)
    put = put.reshape(SECTIONS * HCAP)
    take = (jnp.arange(SECTIONS * HCAP, dtype=jnp.int32)[:, None] == put[None, :]).astype(
        jnp.bfloat16
    )
    return send, take


def local(
    hidden_in,
    queries,
    new_kv,
    cache,
    lengths,
    out_weight,
    moe_gain,
    expert_ids,
    expert_gates,
    gate_up,
    down,
    owners,
):
    z, x, c, y = (lax.axis_index(name) for name in ("z", "x", "c", "y"))
    section = (z * NX + x) * NC + c
    plan = make_plan(expert_ids.T, expert_gates.T)
    context = attend_local(queries, new_kv, cache, lengths)
    attention = jnp.dot(context, out_weight, preferred_element_type=jnp.float32)
    pieces = attention.astype(jnp.bfloat16).reshape(REQ, NY, QUARTER).transpose(1, 0, 2)
    first = (y % 2).astype(jnp.int32).reshape(1)
    blocks = pick_weights(first, pieces, gate_up.transpose(0, 1, 3, 2), down)
    pieces = lax.all_to_all(pieces, "y", 0, 0, tiled=True)
    hidden = lax.dynamic_slice_in_dim(hidden_in, y * QUARTER, QUARTER, 1)
    message, middle = sum_middle(pieces, hidden, plan)
    blocks = move_weights(blocks)

    spread = lax.all_to_all(message, "z", 0, 0, tiled=True)
    send, target, gate = gather_rows(spread)
    rows = lax.all_to_all(send, ("x", "y"), 0, 0, tiled=True)
    blocks = hold(rows, blocks)
    swapped = [lax.ppermute(block, "c", [(0, 1), (1, 0)]) for block in blocks]
    normed, half = first_half(rows, moe_gain.reshape(1, WIDTH), blocks)
    done = second_half(normed, half, swapped)
    back = lax.all_to_all(done, ("x", "y"), 0, 0, tiled=True)
    part = combine_rows(target, gate, back)
    part = lax.all_to_all(part, "z", 0, 0, tiled=True)
    out = middle.astype(jnp.float32) + jnp.sum(part.astype(jnp.float32), axis=0)
    out = out.astype(jnp.bfloat16)

    send_pick, take_pick = talker_plan(owners, section)
    leaving = jnp.dot(send_pick, out, preferred_element_type=jnp.float32).astype(jnp.bfloat16)
    arrived = lax.all_to_all(
        leaving.reshape(SECTIONS, HCAP, QUARTER), ("z", "x", "c"), 0, 0, tiled=True
    )
    talker = jnp.dot(
        take_pick, arrived.reshape(SECTIONS * HCAP, QUARTER), preferred_element_type=jnp.float32
    ).astype(jnp.bfloat16)
    return (out, talker)


def solution(mesh):
    section = ("z", "x", "c")
    fine = Mesh(mesh.devices.reshape(NZ, NX, NC, NY), ("z", "x", "c", "y"))
    in_specs = (
        P(section, None),
        P(section, "y"),
        P(section, None, "y"),
        P(section, None, None, "y"),
        P(section),
        P("y", None),
        P(),
        P(section, None),
        P(section, None),
        P(section, None, None, "y"),
        P(section, "y", None),
        P(),
    )
    out_specs = (P(section, "y"), P(section, "y"))
    return jax.shard_map(local, mesh=fine, in_specs=in_specs, out_specs=out_specs, check_vma=False)
```

```python
import math

import jax
import jax.numpy as jnp
from jax import lax
from jax.experimental import pallas as pl
from jax.experimental.pallas import tpu as pltpu
from jax.sharding import Mesh
from jax.sharding import PartitionSpec as P

HD = 128
HCAP = 2
CAP = 10
NZ, NX, NC, NY = 8, 4, 2, 4
REQ = 64
SECTIONS = NZ * NX * NC
TOKENS = NZ * REQ
PLANE = NX * NY
BLOCK = NZ * CAP
ROWS = REQ // PLANE
QUARTER = 512
WIDTH = 2048
EHQ = 192


def attend_local(queries, new_kv, cache, lengths):
    req_count = queries.shape[0]
    cached_count = cache.shape[2]
    kv_local = new_kv.shape[2] // HD
    group_size = queries.shape[1] // (kv_local * HD)
    query_heads = queries.reshape(req_count, kv_local, group_size, HD)
    cache_keys = cache[:, 0].reshape(req_count, cached_count, kv_local, HD)
    cache_values = cache[:, 1].reshape(req_count, cached_count, kv_local, HD)
    fresh_keys = new_kv[:, 0].reshape(req_count, kv_local, HD)
    fresh_values = new_kv[:, 1].reshape(req_count, kv_local, HD)
    scale_factor = 1.0 / math.sqrt(HD)
    cache_scores = (
        jnp.einsum("rkgd,rckd->rkgc", query_heads, cache_keys, preferred_element_type=jnp.float32)
        * scale_factor
    )
    valid_cells = jnp.arange(cached_count)[None, :] < lengths[:, None]
    cache_scores = jnp.where(valid_cells[:, None, None, :], cache_scores, -jnp.inf)
    fresh_scores = (
        jnp.einsum("rkgd,rkd->rkg", query_heads, fresh_keys, preferred_element_type=jnp.float32)
        * scale_factor
    )
    top_score = jnp.maximum(jnp.max(cache_scores, axis=-1), fresh_scores)
    cache_exp = jnp.exp(cache_scores - top_score[..., None])
    fresh_exp = jnp.exp(fresh_scores - top_score)
    total_mass = jnp.sum(cache_exp, axis=-1) + fresh_exp
    cache_weights = (cache_exp / total_mass[..., None]).astype(jnp.bfloat16)
    fresh_weights = (fresh_exp / total_mass).astype(jnp.bfloat16)
    context = jnp.einsum(
        "rkgc,rckd->rkgd", cache_weights, cache_values, preferred_element_type=jnp.float32
    )
    context = (
        context
        + fresh_weights.astype(jnp.float32)[..., None]
        * fresh_values.astype(jnp.float32)[:, :, None, :]
    )
    return context.reshape(req_count, kv_local * group_size * HD).astype(jnp.bfloat16)


def plan_kernel(ids_ref, gates_ref, out_ref):
    ids = jnp.concatenate([ids_ref[...], ids_ref[...]], axis=1)
    gates = jnp.concatenate([gates_ref[...], gates_ref[...]], axis=1)
    gates = gates / jnp.sum(gates, axis=0, keepdims=True)
    experts = NZ * PLANE
    expert = lax.broadcasted_iota(jnp.int32, (experts, 2 * REQ), 0)
    chosen = jnp.zeros((experts, 2 * REQ), jnp.float32)
    gate = jnp.zeros((experts, 2 * REQ), jnp.float32)
    for k in range(8):
        hit = ids[k : k + 1, :] == expert
        chosen = jnp.where(hit, 1.0, chosen)
        gate = jnp.where(hit, gates[k : k + 1, :], gate)
    earlier = lax.broadcasted_iota(jnp.int32, (2 * REQ, 2 * REQ), 0)
    token = lax.broadcasted_iota(jnp.int32, (2 * REQ, 2 * REQ), 1)
    token = jnp.where(token >= REQ, token - REQ, token)
    before = jnp.where(earlier < token, 1.0, 0.0).astype(jnp.bfloat16)
    rank = jnp.dot(chosen.astype(jnp.bfloat16), before, preferred_element_type=jnp.float32)
    slot = jnp.where(chosen > 0.0, rank, -1.0)
    first = lax.broadcasted_iota(jnp.int32, (experts, 2 * REQ), 1) < REQ
    both = jnp.where(first, slot, gate).astype(jnp.bfloat16)
    for z in range(NZ):
        out_ref[z] = both[z * PLANE : (z + 1) * PLANE, :]


def pick_kernel(first_ref, after_ref, gate_up, down, even_ref, odd_ref, sems):
    first = first_ref[0]
    copies = []
    for k, out in ((0, even_ref), (1, odd_ref)):
        index = first if k == 0 else 1 - first
        copies.append(pltpu.make_async_copy(gate_up.at[index], out.at[pl.ds(0, 2)], sems.at[2 * k]))
        copies.append(pltpu.make_async_copy(down.at[index], out.at[2], sems.at[2 * k + 1]))
    for copy in copies:
        copy.start()
    for copy in copies:
        copy.wait()


def middle_kernel(pieces_ref, hidden_ref, plan_ref, even, odd, message_ref, middle_ref, *same):
    total = hidden_ref[...].astype(jnp.float32)
    for y in range(NY):
        total = total + pieces_ref[y].astype(jnp.float32)
    middle = total.astype(jnp.bfloat16)
    middle_ref[...] = middle
    for z in range(NZ):
        for k in range(ROWS):
            message_ref[z, :, k * QUARTER : (k + 1) * QUARTER] = middle[k * PLANE : (k + 1) * PLANE, :]
        message_ref[z, :, WIDTH:] = plan_ref[z]


def gather_kernel(spread_ref, after_ref, out_ref, target_ref, gate_ref, pick_ref, rows_ref):
    low = lax.broadcasted_iota(jnp.int32, (PLANE, 2 * REQ), 1) < REQ
    for pair in range(NZ // 2):
        left = spread_ref[2 * pair, :, WIDTH:].astype(jnp.float32)
        right = spread_ref[2 * pair + 1, :, WIDTH:].astype(jnp.float32)
        both = jnp.concatenate([left[:, :REQ], right[:, :REQ]], axis=1)
        block = jnp.where(low, float(2 * pair * CAP), float((2 * pair + 1) * CAP))
        columns = slice(pair * 2 * REQ, (pair + 1) * 2 * REQ)
        target_ref[:, columns] = jnp.where(both >= 0.0, both + block, -1.0)
        gate_ref[:, columns] = jnp.concatenate([left[:, REQ:], right[:, REQ:]], axis=1)
    for z in range(NZ):
        for k in range(ROWS):
            first = z * REQ + k * PLANE
            rows_ref[first : first + PLANE, :] = spread_ref[z, :, k * QUARTER : (k + 1) * QUARTER]
    slot = lax.broadcasted_iota(jnp.int32, (BLOCK, TOKENS), 0).astype(jnp.float32)
    for e in range(PLANE):
        hit = target_ref[e : e + 1, :] == slot
        pick_ref[e * BLOCK : (e + 1) * BLOCK, :] = jnp.where(hit, 1.0, 0.0).astype(jnp.bfloat16)
    for e in range(0, PLANE, 4):
        rows = jnp.dot(
            pick_ref[e * BLOCK : (e + 4) * BLOCK, :],
            rows_ref[...],
            preferred_element_type=jnp.float32,
        ).astype(jnp.bfloat16)
        for k in range(4):
            out_ref[e + k] = rows[k * BLOCK : (k + 1) * BLOCK, :]


def hold_kernel(*refs):
    del refs


def combine_kernel(target_ref, gate_ref, rows_ref, out_ref, weight_ref, packed_ref):
    slot = lax.broadcasted_iota(jnp.int32, (BLOCK, TOKENS), 0).astype(jnp.float32)
    for e in range(PLANE):
        hit = target_ref[e : e + 1, :] == slot
        weight = jnp.where(hit, gate_ref[e : e + 1, :], 0.0)
        weight_ref[e * BLOCK : (e + 1) * BLOCK, :] = weight.astype(jnp.bfloat16)
        packed_ref[e * BLOCK : (e + 1) * BLOCK, :] = rows_ref[e]
    dims = (((0,), (0,)), ((), ()))
    total = lax.dot_general(
        weight_ref[...], packed_ref[...], dims, preferred_element_type=jnp.float32
    ).astype(jnp.bfloat16)
    for z in range(NZ):
        out_ref[z] = total[z * REQ : (z + 1) * REQ, :]


def load_weights(blocks, weight_ref, sems):
    copies = []
    for part in range(3):
        for q, block in enumerate(blocks):
            copies.append(
                pltpu.make_async_copy(
                    block.at[part], weight_ref.at[part, pl.ds(q * EHQ, EHQ)], sems.at[part, q]
                )
            )
    for copy in copies:
        copy.start()
    return copies


def activate(normed_ref, weight_ref, act_ref, copies):
    dims = (((1,), (1,)), ((), ()))
    for copy in copies[:2]:
        copy.wait()
    gate = lax.dot_general(
        normed_ref[...], weight_ref[0], dims, preferred_element_type=jnp.float32
    )
    for copy in copies[2:4]:
        copy.wait()
    up = lax.dot_general(normed_ref[...], weight_ref[1], dims, preferred_element_type=jnp.float32)
    act_ref[...] = (gate / (1.0 + jnp.exp(-gate)) * up).astype(jnp.bfloat16)
    for copy in copies[4:]:
        copy.wait()


def first_half_kernel(rows_ref, gain_ref, w0, w1, normed_ref, part_ref, weight_ref, act_ref, sems):
    copies = load_weights((w0, w1), weight_ref, sems)
    for x in range(NX):
        parts = [rows_ref[x * NY + y].astype(jnp.float32) for y in range(NY)]
        square = sum(jnp.sum(part * part, axis=-1, keepdims=True) for part in parts)
        scale = lax.rsqrt(square * (1.0 / WIDTH) + 1e-06)
        for y in range(NY):
            columns = slice(y * QUARTER, (y + 1) * QUARTER)
            normed_ref[x * BLOCK : (x + 1) * BLOCK, columns] = (
                parts[y] * scale * gain_ref[:, columns]
            ).astype(jnp.bfloat16)
    activate(normed_ref, weight_ref, act_ref, copies)
    part_ref[...] = jnp.dot(act_ref[...], weight_ref[2], preferred_element_type=jnp.float32)


def second_half_kernel(normed_ref, part_ref, w2, w3, out_ref, weight_ref, act_ref, sems):
    copies = load_weights((w2, w3), weight_ref, sems)
    activate(normed_ref, weight_ref, act_ref, copies)
    for y in range(NY):
        columns = slice(y * QUARTER, (y + 1) * QUARTER)
        part = part_ref[:, columns] + jnp.dot(
            act_ref[...], weight_ref[2, :, columns], preferred_element_type=jnp.float32
        )
        part = part.astype(jnp.bfloat16)
        for x in range(NX):
            out_ref[x * NY + y] = part[x * BLOCK : (x + 1) * BLOCK, :]


def vmem():
    return pl.BlockSpec(memory_space=pltpu.VMEM)


def anywhere():
    return pl.BlockSpec(memory_space=pl.ANY)


def params(mib=16):
    return pltpu.CompilerParams(vmem_limit_bytes=mib * 1024 * 1024)


def shape(*dims, dtype=jnp.bfloat16):
    return jax.ShapeDtypeStruct(dims, dtype)


def make_plan(ids, gates):
    return pl.pallas_call(
        plan_kernel,
        out_shape=shape(NZ, PLANE, 2 * REQ),
        in_specs=[vmem(), vmem()],
        out_specs=vmem(),
        compiler_params=params(),
        name="plan",
    )(ids, gates)


def pick_weights(first, after, gate_up, down):
    block = shape(3, EHQ, WIDTH)
    return pl.pallas_call(
        pick_kernel,
        out_shape=(block, block),
        in_specs=[pl.BlockSpec(memory_space=pltpu.SMEM), anywhere()]
        + [pl.BlockSpec(memory_space=pltpu.HBM)] * 2,
        out_specs=(anywhere(), anywhere()),
        scratch_shapes=[pltpu.SemaphoreType.DMA((4,))],
        compiler_params=params(),
        name="pick_weights",
    )(first, after, gate_up, down)


def sum_middle(pieces, hidden, plan, blocks):
    return pl.pallas_call(
        middle_kernel,
        out_shape=(
            shape(NZ, PLANE, WIDTH + 2 * REQ),
            shape(REQ, QUARTER),
            *[shape(*block.shape) for block in blocks],
        ),
        in_specs=[vmem()] * 3 + [anywhere()] * 2,
        out_specs=(vmem(), vmem()) + (anywhere(),) * 2,
        input_output_aliases={3: 2, 4: 3},
        compiler_params=params(),
        name="sum_middle",
    )(pieces, hidden, plan, *blocks)


def gather_rows(spread, after):
    return pl.pallas_call(
        gather_kernel,
        out_shape=(
            shape(PLANE, BLOCK, QUARTER),
            shape(PLANE, TOKENS, dtype=jnp.float32),
            shape(PLANE, TOKENS, dtype=jnp.float32),
        ),
        in_specs=[vmem(), anywhere()],
        out_specs=(vmem(), vmem(), vmem()),
        scratch_shapes=[
            pltpu.VMEM((PLANE * BLOCK, TOKENS), jnp.bfloat16),
            pltpu.VMEM((TOKENS, QUARTER), jnp.bfloat16),
        ],
        compiler_params=params(),
        name="gather_rows",
    )(spread, after)


def hold(after, block):
    return pl.pallas_call(
        hold_kernel,
        out_shape=shape(*block.shape),
        in_specs=[anywhere()] * 2,
        out_specs=anywhere(),
        input_output_aliases={1: 0},
        compiler_params=params(),
        name="hold",
    )(after, block)


def combine_rows(target, gate, rows):
    return pl.pallas_call(
        combine_kernel,
        out_shape=shape(NZ, REQ, QUARTER),
        in_specs=[vmem(), vmem(), vmem()],
        out_specs=vmem(),
        scratch_shapes=[
            pltpu.VMEM((PLANE * BLOCK, TOKENS), jnp.bfloat16),
            pltpu.VMEM((PLANE * BLOCK, QUARTER), jnp.bfloat16),
        ],
        compiler_params=params(),
        name="combine_rows",
    )(target, gate, rows)


def half_scratch():
    return [
        pltpu.VMEM((3, 2 * EHQ, WIDTH), jnp.bfloat16),
        pltpu.VMEM((NX * BLOCK, 2 * EHQ), jnp.bfloat16),
        pltpu.SemaphoreType.DMA((3, 2)),
    ]


def first_half(rows, gain, blocks):
    return pl.pallas_call(
        first_half_kernel,
        out_shape=(shape(NX * BLOCK, WIDTH), shape(NX * BLOCK, WIDTH, dtype=jnp.float32)),
        in_specs=[vmem(), vmem()] + [anywhere()] * 2,
        out_specs=(vmem(), vmem()),
        scratch_shapes=half_scratch(),
        compiler_params=params(24),
        name="first_half",
    )(rows, gain, *blocks)


def second_half(normed, part, blocks):
    return pl.pallas_call(
        second_half_kernel,
        out_shape=shape(PLANE, BLOCK, QUARTER),
        in_specs=[vmem(), vmem()] + [anywhere()] * 2,
        out_specs=vmem(),
        scratch_shapes=half_scratch(),
        compiler_params=params(24),
        name="second_half",
    )(normed, part, *blocks)


def move_weights(blocks):
    even, odd = [], []
    for c in range(NC):
        for y in range(NY):
            core = (y // 2) * NY
            even.append((c * NY + y, core + 2 * c + y % 2))
            odd.append((c * NY + y, core + 2 * c + 1 - y % 2))
    return [lax.ppermute(block, ("c", "y"), to) for block, to in zip(blocks, (even, odd))]


def talker_plan(owners, section):
    own = lax.dynamic_slice_in_dim(owners, section * REQ, REQ)
    order = jnp.arange(REQ, dtype=jnp.int32)
    same = (own[:, None] == own[None, :]) & (order[:, None] > order[None, :])
    position = jnp.sum(same.astype(jnp.int32), axis=1)
    slot = jnp.where(own >= 0, own * HCAP + position, -1)
    send = (jnp.arange(SECTIONS * HCAP, dtype=jnp.int32)[:, None] == slot[None, :]).astype(
        jnp.bfloat16
    )
    counts = jnp.sum((owners == section).reshape(SECTIONS, REQ).astype(jnp.int32), axis=1)
    place = jnp.arange(SECTIONS, dtype=jnp.int32)
    offsets = jnp.sum(jnp.where(place[None, :] < place[:, None], counts[None, :], 0), axis=1)
    index = jnp.arange(HCAP, dtype=jnp.int32)
    put = jnp.where(index[None, :] < counts[:, None], offsets[:, None] + index[None, :], -1)
    put = put.reshape(SECTIONS * HCAP)
    take = (jnp.arange(SECTIONS * HCAP, dtype=jnp.int32)[:, None] == put[None, :]).astype(
        jnp.bfloat16
    )
    return send, take


def local(
    hidden_in,
    queries,
    new_kv,
    cache,
    lengths,
    out_weight,
    moe_gain,
    expert_ids,
    expert_gates,
    gate_up,
    down,
    owners,
):
    z, x, c, y = (lax.axis_index(name) for name in ("z", "x", "c", "y"))
    section = (z * NX + x) * NC + c
    plan = make_plan(expert_ids.T, expert_gates.T)
    context = attend_local(queries, new_kv, cache, lengths)
    attention = jnp.dot(context, out_weight, preferred_element_type=jnp.float32)
    pieces = attention.astype(jnp.bfloat16).reshape(REQ, NY, QUARTER).transpose(1, 0, 2)
    first = (y % 2).astype(jnp.int32).reshape(1)
    blocks = pick_weights(first, pieces, gate_up.transpose(0, 1, 3, 2), down)
    pieces = lax.all_to_all(pieces, "y", 0, 0, tiled=True)
    hidden = lax.dynamic_slice_in_dim(hidden_in, y * QUARTER, QUARTER, 1)
    message, middle, *blocks = sum_middle(pieces, hidden, plan, blocks)
    even, odd = move_weights(blocks)
    swap = [(0, 1), (1, 0)]

    spread = lax.all_to_all(message, "z", 0, 0, tiled=True)
    send, target, gate = gather_rows(spread, odd)
    rows = lax.all_to_all(send, ("x", "y"), 0, 0, tiled=True)
    even = hold(rows, even)
    odd_swapped = lax.ppermute(odd, "c", swap)
    even_swapped = lax.ppermute(even, "c", swap)
    normed, half = first_half(rows, moe_gain.reshape(1, WIDTH), (odd, odd_swapped))
    done = second_half(normed, half, (even, even_swapped))
    back = lax.all_to_all(done, ("x", "y"), 0, 0, tiled=True)
    part = combine_rows(target, gate, back)
    part = lax.all_to_all(part, "z", 0, 0, tiled=True)
    out = middle.astype(jnp.float32) + jnp.sum(part.astype(jnp.float32), axis=0)
    out = out.astype(jnp.bfloat16)

    send_pick, take_pick = talker_plan(owners, section)
    leaving = jnp.dot(send_pick, out, preferred_element_type=jnp.float32).astype(jnp.bfloat16)
    arrived = lax.all_to_all(
        leaving.reshape(SECTIONS, HCAP, QUARTER), ("z", "x", "c"), 0, 0, tiled=True
    )
    talker = jnp.dot(
        take_pick, arrived.reshape(SECTIONS * HCAP, QUARTER), preferred_element_type=jnp.float32
    ).astype(jnp.bfloat16)
    return (out, talker)


def solution(mesh):
    section = ("z", "x", "c")
    fine = Mesh(mesh.devices.reshape(NZ, NX, NC, NY), ("z", "x", "c", "y"))
    in_specs = (
        P(section, None),
        P(section, "y"),
        P(section, None, "y"),
        P(section, None, None, "y"),
        P(section),
        P("y", None),
        P(),
        P(section, None),
        P(section, None),
        P(section, None, None, "y"),
        P(section, "y", None),
        P(),
    )
    out_specs = (P(section, "y"), P(section, "y"))
    return jax.shard_map(local, mesh=fine, in_specs=in_specs, out_specs=out_specs, check_vma=False)
```

```python
import math

import jax
import jax.numpy as jnp
from jax import lax
from jax.experimental import pallas as pl
from jax.experimental.pallas import tpu as pltpu
from jax.sharding import Mesh
from jax.sharding import PartitionSpec as P

HD = 128
HCAP = 2
CAP = 10
NZ, NX, NC, NY = 8, 4, 2, 4
REQ = 64
SECTIONS = NZ * NX * NC
TOKENS = NZ * REQ
PLANE = NX * NY
BLOCK = NZ * CAP
ROWS = REQ // PLANE
QUARTER = 512
WIDTH = 2048
EHQ = 192


def attend_local(queries, new_kv, cache, lengths):
    req_count = queries.shape[0]
    cached_count = cache.shape[2]
    kv_local = new_kv.shape[2] // HD
    group_size = queries.shape[1] // (kv_local * HD)
    query_heads = queries.reshape(req_count, kv_local, group_size, HD)
    cache_keys = cache[:, 0].reshape(req_count, cached_count, kv_local, HD)
    cache_values = cache[:, 1].reshape(req_count, cached_count, kv_local, HD)
    fresh_keys = new_kv[:, 0].reshape(req_count, kv_local, HD)
    fresh_values = new_kv[:, 1].reshape(req_count, kv_local, HD)
    scale_factor = 1.0 / math.sqrt(HD)
    cache_scores = (
        jnp.einsum("rkgd,rckd->rkgc", query_heads, cache_keys, preferred_element_type=jnp.float32)
        * scale_factor
    )
    valid_cells = jnp.arange(cached_count)[None, :] < lengths[:, None]
    cache_scores = jnp.where(valid_cells[:, None, None, :], cache_scores, -jnp.inf)
    fresh_scores = (
        jnp.einsum("rkgd,rkd->rkg", query_heads, fresh_keys, preferred_element_type=jnp.float32)
        * scale_factor
    )
    top_score = jnp.maximum(jnp.max(cache_scores, axis=-1), fresh_scores)
    cache_exp = jnp.exp(cache_scores - top_score[..., None])
    fresh_exp = jnp.exp(fresh_scores - top_score)
    total_mass = jnp.sum(cache_exp, axis=-1) + fresh_exp
    cache_weights = (cache_exp / total_mass[..., None]).astype(jnp.bfloat16)
    fresh_weights = (fresh_exp / total_mass).astype(jnp.bfloat16)
    context = jnp.einsum(
        "rkgc,rckd->rkgd", cache_weights, cache_values, preferred_element_type=jnp.float32
    )
    context = (
        context
        + fresh_weights.astype(jnp.float32)[..., None]
        * fresh_values.astype(jnp.float32)[:, :, None, :]
    )
    return context.reshape(req_count, kv_local * group_size * HD).astype(jnp.bfloat16)


def plan_kernel(ids_ref, gates_ref, out_ref):
    ids = jnp.concatenate([ids_ref[...], ids_ref[...]], axis=1)
    gates = jnp.concatenate([gates_ref[...], gates_ref[...]], axis=1)
    gates = gates / jnp.sum(gates, axis=0, keepdims=True)
    experts = NZ * PLANE
    expert = lax.broadcasted_iota(jnp.int32, (experts, 2 * REQ), 0)
    chosen = jnp.zeros((experts, 2 * REQ), jnp.float32)
    gate = jnp.zeros((experts, 2 * REQ), jnp.float32)
    for k in range(8):
        hit = ids[k : k + 1, :] == expert
        chosen = jnp.where(hit, 1.0, chosen)
        gate = jnp.where(hit, gates[k : k + 1, :], gate)
    earlier = lax.broadcasted_iota(jnp.int32, (2 * REQ, 2 * REQ), 0)
    token = lax.broadcasted_iota(jnp.int32, (2 * REQ, 2 * REQ), 1)
    token = jnp.where(token >= REQ, token - REQ, token)
    before = jnp.where(earlier < token, 1.0, 0.0).astype(jnp.bfloat16)
    rank = jnp.dot(chosen.astype(jnp.bfloat16), before, preferred_element_type=jnp.float32)
    slot = jnp.where(chosen > 0.0, rank, -1.0)
    first = lax.broadcasted_iota(jnp.int32, (experts, 2 * REQ), 1) < REQ
    both = jnp.where(first, slot, gate).astype(jnp.bfloat16)
    for z in range(NZ):
        out_ref[z] = both[z * PLANE : (z + 1) * PLANE, :]


def pick_kernel(first_ref, after_ref, gate_up, down, even_ref, odd_ref, sems):
    first = first_ref[0]
    copies = []
    for k, out in ((0, even_ref), (1, odd_ref)):
        index = first if k == 0 else 1 - first
        copies.append(pltpu.make_async_copy(gate_up.at[index], out.at[pl.ds(0, 2)], sems.at[2 * k]))
        copies.append(pltpu.make_async_copy(down.at[index], out.at[2], sems.at[2 * k + 1]))
    for copy in copies:
        copy.start()
    for copy in copies:
        copy.wait()


def middle_kernel(pieces_ref, hidden_ref, plan_ref, even, odd, message_ref, middle_ref, *same):
    total = hidden_ref[...].astype(jnp.float32)
    for y in range(NY):
        total = total + pieces_ref[y].astype(jnp.float32)
    middle = total.astype(jnp.bfloat16)
    middle_ref[...] = middle
    for z in range(NZ):
        for k in range(ROWS):
            message_ref[z, :, k * QUARTER : (k + 1) * QUARTER] = middle[k * PLANE : (k + 1) * PLANE, :]
        message_ref[z, :, WIDTH:] = plan_ref[z]


def gather_kernel(spread_ref, out_ref, target_ref, gate_ref, pick_ref, rows_ref):
    low = lax.broadcasted_iota(jnp.int32, (PLANE, 2 * REQ), 1) < REQ
    for pair in range(NZ // 2):
        left = spread_ref[2 * pair, :, WIDTH:].astype(jnp.float32)
        right = spread_ref[2 * pair + 1, :, WIDTH:].astype(jnp.float32)
        both = jnp.concatenate([left[:, :REQ], right[:, :REQ]], axis=1)
        block = jnp.where(low, float(2 * pair * CAP), float((2 * pair + 1) * CAP))
        columns = slice(pair * 2 * REQ, (pair + 1) * 2 * REQ)
        target_ref[:, columns] = jnp.where(both >= 0.0, both + block, -1.0)
        gate_ref[:, columns] = jnp.concatenate([left[:, REQ:], right[:, REQ:]], axis=1)
    for z in range(NZ):
        for k in range(ROWS):
            first = z * REQ + k * PLANE
            rows_ref[first : first + PLANE, :] = spread_ref[z, :, k * QUARTER : (k + 1) * QUARTER]
    slot = lax.broadcasted_iota(jnp.int32, (BLOCK, TOKENS), 0).astype(jnp.float32)
    for e in range(PLANE):
        hit = target_ref[e : e + 1, :] == slot
        pick_ref[e * BLOCK : (e + 1) * BLOCK, :] = jnp.where(hit, 1.0, 0.0).astype(jnp.bfloat16)
    for e in range(0, PLANE, 4):
        rows = jnp.dot(
            pick_ref[e * BLOCK : (e + 4) * BLOCK, :],
            rows_ref[...],
            preferred_element_type=jnp.float32,
        ).astype(jnp.bfloat16)
        for k in range(4):
            out_ref[e + k] = rows[k * BLOCK : (k + 1) * BLOCK, :]


def hold_kernel(*refs):
    del refs


def combine_kernel(target_ref, gate_ref, rows_ref, out_ref, weight_ref, packed_ref):
    slot = lax.broadcasted_iota(jnp.int32, (BLOCK, TOKENS), 0).astype(jnp.float32)
    for e in range(PLANE):
        hit = target_ref[e : e + 1, :] == slot
        weight = jnp.where(hit, gate_ref[e : e + 1, :], 0.0)
        weight_ref[e * BLOCK : (e + 1) * BLOCK, :] = weight.astype(jnp.bfloat16)
        packed_ref[e * BLOCK : (e + 1) * BLOCK, :] = rows_ref[e]
    dims = (((0,), (0,)), ((), ()))
    total = lax.dot_general(
        weight_ref[...], packed_ref[...], dims, preferred_element_type=jnp.float32
    ).astype(jnp.bfloat16)
    for z in range(NZ):
        out_ref[z] = total[z * REQ : (z + 1) * REQ, :]


def load_weights(blocks, weight_ref, sems):
    copies = []
    for part in range(3):
        for q, block in enumerate(blocks):
            copies.append(
                pltpu.make_async_copy(
                    block.at[part], weight_ref.at[part, pl.ds(q * EHQ, EHQ)], sems.at[part, q]
                )
            )
    for copy in copies:
        copy.start()
    return copies


def activate(normed_ref, weight_ref, act_ref, copies):
    dims = (((1,), (1,)), ((), ()))
    for copy in copies[:2]:
        copy.wait()
    gate = lax.dot_general(
        normed_ref[...], weight_ref[0], dims, preferred_element_type=jnp.float32
    )
    for copy in copies[2:4]:
        copy.wait()
    up = lax.dot_general(normed_ref[...], weight_ref[1], dims, preferred_element_type=jnp.float32)
    act_ref[...] = (gate / (1.0 + jnp.exp(-gate)) * up).astype(jnp.bfloat16)
    for copy in copies[4:]:
        copy.wait()


def first_half_kernel(rows_ref, gain_ref, w0, w1, normed_ref, part_ref, weight_ref, act_ref, sems):
    copies = load_weights((w0, w1), weight_ref, sems)
    for x in range(NX):
        parts = [rows_ref[x * NY + y].astype(jnp.float32) for y in range(NY)]
        square = sum(jnp.sum(part * part, axis=-1, keepdims=True) for part in parts)
        scale = lax.rsqrt(square * (1.0 / WIDTH) + 1e-06)
        for y in range(NY):
            columns = slice(y * QUARTER, (y + 1) * QUARTER)
            normed_ref[x * BLOCK : (x + 1) * BLOCK, columns] = (
                parts[y] * scale * gain_ref[:, columns]
            ).astype(jnp.bfloat16)
    activate(normed_ref, weight_ref, act_ref, copies)
    part_ref[...] = jnp.dot(act_ref[...], weight_ref[2], preferred_element_type=jnp.float32)


def second_half_kernel(normed_ref, part_ref, w2, w3, out_ref, weight_ref, act_ref, sems):
    copies = load_weights((w2, w3), weight_ref, sems)
    activate(normed_ref, weight_ref, act_ref, copies)
    for y in range(NY):
        columns = slice(y * QUARTER, (y + 1) * QUARTER)
        part = part_ref[:, columns] + jnp.dot(
            act_ref[...], weight_ref[2, :, columns], preferred_element_type=jnp.float32
        )
        part = part.astype(jnp.bfloat16)
        for x in range(NX):
            out_ref[x * NY + y] = part[x * BLOCK : (x + 1) * BLOCK, :]


def vmem():
    return pl.BlockSpec(memory_space=pltpu.VMEM)


def anywhere():
    return pl.BlockSpec(memory_space=pl.ANY)


def params(mib=16):
    return pltpu.CompilerParams(vmem_limit_bytes=mib * 1024 * 1024)


def shape(*dims, dtype=jnp.bfloat16):
    return jax.ShapeDtypeStruct(dims, dtype)


def make_plan(ids, gates):
    return pl.pallas_call(
        plan_kernel,
        out_shape=shape(NZ, PLANE, 2 * REQ),
        in_specs=[vmem(), vmem()],
        out_specs=vmem(),
        compiler_params=params(),
        name="plan",
    )(ids, gates)


def pick_weights(first, after, gate_up, down):
    block = shape(3, EHQ, WIDTH)
    return pl.pallas_call(
        pick_kernel,
        out_shape=(block, block),
        in_specs=[pl.BlockSpec(memory_space=pltpu.SMEM), anywhere()]
        + [pl.BlockSpec(memory_space=pltpu.HBM)] * 2,
        out_specs=(anywhere(), anywhere()),
        scratch_shapes=[pltpu.SemaphoreType.DMA((4,))],
        compiler_params=params(),
        name="pick_weights",
    )(first, after, gate_up, down)


def sum_middle(pieces, hidden, plan, blocks):
    return pl.pallas_call(
        middle_kernel,
        out_shape=(
            shape(NZ, PLANE, WIDTH + 2 * REQ),
            shape(REQ, QUARTER),
            *[shape(*block.shape) for block in blocks],
        ),
        in_specs=[vmem()] * 3 + [anywhere()] * 2,
        out_specs=(vmem(), vmem()) + (anywhere(),) * 2,
        input_output_aliases={3: 2, 4: 3},
        compiler_params=params(),
        name="sum_middle",
    )(pieces, hidden, plan, *blocks)


def gather_rows(spread):
    return pl.pallas_call(
        gather_kernel,
        out_shape=(
            shape(PLANE, BLOCK, QUARTER),
            shape(PLANE, TOKENS, dtype=jnp.float32),
            shape(PLANE, TOKENS, dtype=jnp.float32),
        ),
        in_specs=[vmem()],
        out_specs=(vmem(), vmem(), vmem()),
        scratch_shapes=[
            pltpu.VMEM((PLANE * BLOCK, TOKENS), jnp.bfloat16),
            pltpu.VMEM((TOKENS, QUARTER), jnp.bfloat16),
        ],
        compiler_params=params(),
        name="gather_rows",
    )(spread)


def hold(after, block):
    return pl.pallas_call(
        hold_kernel,
        out_shape=shape(*block.shape),
        in_specs=[anywhere()] * 2,
        out_specs=anywhere(),
        input_output_aliases={1: 0},
        compiler_params=params(),
        name="hold",
    )(after, block)


def combine_rows(target, gate, rows):
    return pl.pallas_call(
        combine_kernel,
        out_shape=shape(NZ, REQ, QUARTER),
        in_specs=[vmem(), vmem(), vmem()],
        out_specs=vmem(),
        scratch_shapes=[
            pltpu.VMEM((PLANE * BLOCK, TOKENS), jnp.bfloat16),
            pltpu.VMEM((PLANE * BLOCK, QUARTER), jnp.bfloat16),
        ],
        compiler_params=params(),
        name="combine_rows",
    )(target, gate, rows)


def half_scratch():
    return [
        pltpu.VMEM((3, 2 * EHQ, WIDTH), jnp.bfloat16),
        pltpu.VMEM((NX * BLOCK, 2 * EHQ), jnp.bfloat16),
        pltpu.SemaphoreType.DMA((3, 2)),
    ]


def first_half(rows, gain, blocks):
    return pl.pallas_call(
        first_half_kernel,
        out_shape=(shape(NX * BLOCK, WIDTH), shape(NX * BLOCK, WIDTH, dtype=jnp.float32)),
        in_specs=[vmem(), vmem()] + [anywhere()] * 2,
        out_specs=(vmem(), vmem()),
        scratch_shapes=half_scratch(),
        compiler_params=params(24),
        name="first_half",
    )(rows, gain, *blocks)


def second_half(normed, part, blocks):
    return pl.pallas_call(
        second_half_kernel,
        out_shape=shape(PLANE, BLOCK, QUARTER),
        in_specs=[vmem(), vmem()] + [anywhere()] * 2,
        out_specs=vmem(),
        scratch_shapes=half_scratch(),
        compiler_params=params(24),
        name="second_half",
    )(normed, part, *blocks)


def move_weights(blocks):
    even, odd = [], []
    for c in range(NC):
        for y in range(NY):
            core = (y // 2) * NY
            even.append((c * NY + y, core + 2 * c + y % 2))
            odd.append((c * NY + y, core + 2 * c + 1 - y % 2))
    return [lax.ppermute(block, ("c", "y"), to) for block, to in zip(blocks, (even, odd))]


def talker_plan(owners, section):
    own = lax.dynamic_slice_in_dim(owners, section * REQ, REQ)
    order = jnp.arange(REQ, dtype=jnp.int32)
    same = (own[:, None] == own[None, :]) & (order[:, None] > order[None, :])
    position = jnp.sum(same.astype(jnp.int32), axis=1)
    slot = jnp.where(own >= 0, own * HCAP + position, -1)
    send = (jnp.arange(SECTIONS * HCAP, dtype=jnp.int32)[:, None] == slot[None, :]).astype(
        jnp.bfloat16
    )
    counts = jnp.sum((owners == section).reshape(SECTIONS, REQ).astype(jnp.int32), axis=1)
    place = jnp.arange(SECTIONS, dtype=jnp.int32)
    offsets = jnp.sum(jnp.where(place[None, :] < place[:, None], counts[None, :], 0), axis=1)
    index = jnp.arange(HCAP, dtype=jnp.int32)
    put = jnp.where(index[None, :] < counts[:, None], offsets[:, None] + index[None, :], -1)
    put = put.reshape(SECTIONS * HCAP)
    take = (jnp.arange(SECTIONS * HCAP, dtype=jnp.int32)[:, None] == put[None, :]).astype(
        jnp.bfloat16
    )
    return send, take


def local(
    hidden_in,
    queries,
    new_kv,
    cache,
    lengths,
    out_weight,
    moe_gain,
    expert_ids,
    expert_gates,
    gate_up,
    down,
    owners,
):
    z, x, c, y = (lax.axis_index(name) for name in ("z", "x", "c", "y"))
    section = (z * NX + x) * NC + c
    plan = make_plan(expert_ids.T, expert_gates.T)
    context = attend_local(queries, new_kv, cache, lengths)
    attention = jnp.dot(context, out_weight, preferred_element_type=jnp.float32)
    pieces = attention.astype(jnp.bfloat16).reshape(REQ, NY, QUARTER).transpose(1, 0, 2)
    first = (y % 2).astype(jnp.int32).reshape(1)
    blocks = pick_weights(first, pieces, gate_up.transpose(0, 1, 3, 2), down)
    pieces = lax.all_to_all(pieces, "y", 0, 0, tiled=True)
    hidden = lax.dynamic_slice_in_dim(hidden_in, y * QUARTER, QUARTER, 1)
    message, middle, *blocks = sum_middle(pieces, hidden, plan, blocks)
    even, odd = move_weights(blocks)
    swap = [(0, 1), (1, 0)]

    spread = lax.all_to_all(message, "z", 0, 0, tiled=True)
    send, target, gate = gather_rows(spread)
    rows = lax.all_to_all(send, ("x", "y"), 0, 0, tiled=True)
    odd = hold(rows, odd)
    even_swapped = lax.ppermute(even, "c", swap)
    odd_swapped = lax.ppermute(odd, "c", swap)
    normed, half = first_half(rows, moe_gain.reshape(1, WIDTH), (even, even_swapped))
    done = second_half(normed, half, (odd, odd_swapped))
    back = lax.all_to_all(done, ("x", "y"), 0, 0, tiled=True)
    part = combine_rows(target, gate, back)
    part = lax.all_to_all(part, "z", 0, 0, tiled=True)
    out = middle.astype(jnp.float32) + jnp.sum(part.astype(jnp.float32), axis=0)
    out = out.astype(jnp.bfloat16)

    send_pick, take_pick = talker_plan(owners, section)
    leaving = jnp.dot(send_pick, out, preferred_element_type=jnp.float32).astype(jnp.bfloat16)
    arrived = lax.all_to_all(
        leaving.reshape(SECTIONS, HCAP, QUARTER), ("z", "x", "c"), 0, 0, tiled=True
    )
    talker = jnp.dot(
        take_pick, arrived.reshape(SECTIONS * HCAP, QUARTER), preferred_element_type=jnp.float32
    ).astype(jnp.bfloat16)
    return (out, talker)


def solution(mesh):
    section = ("z", "x", "c")
    fine = Mesh(mesh.devices.reshape(NZ, NX, NC, NY), ("z", "x", "c", "y"))
    in_specs = (
        P(section, None),
        P(section, "y"),
        P(section, None, "y"),
        P(section, None, None, "y"),
        P(section),
        P("y", None),
        P(),
        P(section, None),
        P(section, None),
        P(section, None, None, "y"),
        P(section, "y", None),
        P(),
    )
    out_specs = (P(section, "y"), P(section, "y"))
    return jax.shard_map(local, mesh=fine, in_specs=in_specs, out_specs=out_specs, check_vma=False)
```

```python
import math

import jax
import jax.numpy as jnp
from jax import lax
from jax.experimental import pallas as pl
from jax.experimental.pallas import tpu as pltpu
from jax.sharding import Mesh
from jax.sharding import PartitionSpec as P

HD = 128
HCAP = 2
CAP = 10
NZ, NX, NC, NY = 8, 4, 2, 4
REQ = 64
SECTIONS = NZ * NX * NC
TOKENS = NZ * REQ
PLANE = NX * NY
BLOCK = NZ * CAP
ROWS = REQ // PLANE
QUARTER = 512
HEADS = 8
CTX = 96
CHUNK = 16
WIDTH = 2048
EHQ = 192


def attention_kernel(lengths_ref, queries_ref, fresh_ref, cache, weight, out_ref, *scratch):
    cache_ref, weight_ref, context_ref, cache_sem, weight_sem = scratch
    loads = []
    for i in range(REQ // CHUNK):
        rows = pl.ds(i * CHUNK, CHUNK)
        loads.append(pltpu.make_async_copy(cache.at[rows], cache_ref.at[rows], cache_sem.at[i]))
    for copy in loads:
        copy.start()
    whole = pltpu.make_async_copy(weight, weight_ref, weight_sem)
    whole.start()
    scale = 1.0 / math.sqrt(HD)
    cell = lax.broadcasted_iota(jnp.int32, (HEADS, CTX), 1)
    for i in range(REQ // CHUNK):
        rows = slice(i * CHUNK, (i + 1) * CHUNK)
        heads = queries_ref[rows, :].astype(jnp.float32).reshape(CHUNK, HEADS, HD)
        fresh = fresh_ref[rows].astype(jnp.float32)
        loads[i].wait()
        keys, values = cache_ref[rows, 0], cache_ref[rows, 1]
        scores = lax.dot_general(
            heads.astype(jnp.bfloat16), keys, (((2,), (2,)), ((0,), (0,))), preferred_element_type=jnp.float32
        )
        scores = scores * scale
        scores = jnp.stack(
            [jnp.where(cell < lengths_ref[i * CHUNK + r], scores[r], -jnp.inf) for r in range(CHUNK)]
        )
        new = jnp.sum(heads * fresh[:, 0:1, :], axis=-1, keepdims=True) * scale
        top = jnp.maximum(jnp.max(scores, axis=-1, keepdims=True), new)
        mass = jnp.exp(scores - top)
        new = jnp.exp(new - top)
        total = jnp.sum(mass, axis=-1, keepdims=True) + new
        mass = (mass / total).astype(jnp.bfloat16)
        new = (new / total).astype(jnp.bfloat16).astype(jnp.float32)
        context = lax.dot_general(
            mass, values, (((2,), (1,)), ((0,), (0,))), preferred_element_type=jnp.float32
        ) + new * fresh[:, 1:2, :]
        context_ref[rows, :] = context.reshape(CHUNK, HEADS * HD).astype(jnp.bfloat16)
    whole.wait()
    for y in range(NY):
        out_ref[y] = jnp.dot(
            context_ref[...], weight_ref[:, y * QUARTER : (y + 1) * QUARTER],
            preferred_element_type=jnp.float32,
        ).astype(jnp.bfloat16)


def plan_kernel(ids_ref, gates_ref, out_ref):
    ids = jnp.concatenate([ids_ref[...], ids_ref[...]], axis=1)
    gates = jnp.concatenate([gates_ref[...], gates_ref[...]], axis=1)
    gates = gates / jnp.sum(gates, axis=0, keepdims=True)
    experts = NZ * PLANE
    expert = lax.broadcasted_iota(jnp.int32, (experts, 2 * REQ), 0)
    chosen = jnp.zeros((experts, 2 * REQ), jnp.float32)
    gate = jnp.zeros((experts, 2 * REQ), jnp.float32)
    for k in range(8):
        hit = ids[k : k + 1, :] == expert
        chosen = jnp.where(hit, 1.0, chosen)
        gate = jnp.where(hit, gates[k : k + 1, :], gate)
    earlier = lax.broadcasted_iota(jnp.int32, (2 * REQ, 2 * REQ), 0)
    token = lax.broadcasted_iota(jnp.int32, (2 * REQ, 2 * REQ), 1)
    token = jnp.where(token >= REQ, token - REQ, token)
    before = jnp.where(earlier < token, 1.0, 0.0).astype(jnp.bfloat16)
    rank = jnp.dot(chosen.astype(jnp.bfloat16), before, preferred_element_type=jnp.float32)
    slot = jnp.where(chosen > 0.0, rank, -1.0)
    first = lax.broadcasted_iota(jnp.int32, (experts, 2 * REQ), 1) < REQ
    both = jnp.where(first, slot, gate).astype(jnp.bfloat16)
    for z in range(NZ):
        out_ref[z] = both[z * PLANE : (z + 1) * PLANE, :]


def pick_kernel(first_ref, after_ref, gate_up, down, even_ref, odd_ref, sems):
    first = first_ref[0]
    copies = []
    for k, out in ((0, even_ref), (1, odd_ref)):
        index = first if k == 0 else 1 - first
        copies.append(pltpu.make_async_copy(gate_up.at[index], out.at[pl.ds(0, 2)], sems.at[2 * k]))
        copies.append(pltpu.make_async_copy(down.at[index], out.at[2], sems.at[2 * k + 1]))
    for copy in copies:
        copy.start()
    for copy in copies:
        copy.wait()


def middle_kernel(pieces_ref, hidden_ref, plan_ref, even, odd, message_ref, middle_ref, *same):
    total = hidden_ref[...].astype(jnp.float32)
    for y in range(NY):
        total = total + pieces_ref[y].astype(jnp.float32)
    middle = total.astype(jnp.bfloat16)
    middle_ref[...] = middle
    for z in range(NZ):
        for k in range(ROWS):
            message_ref[z, :, k * QUARTER : (k + 1) * QUARTER] = middle[k * PLANE : (k + 1) * PLANE, :]
        message_ref[z, :, WIDTH:] = plan_ref[z]


def gather_kernel(spread_ref, out_ref, target_ref, gate_ref, pick_ref, rows_ref):
    low = lax.broadcasted_iota(jnp.int32, (PLANE, 2 * REQ), 1) < REQ
    for pair in range(NZ // 2):
        left = spread_ref[2 * pair, :, WIDTH:].astype(jnp.float32)
        right = spread_ref[2 * pair + 1, :, WIDTH:].astype(jnp.float32)
        both = jnp.concatenate([left[:, :REQ], right[:, :REQ]], axis=1)
        block = jnp.where(low, float(2 * pair * CAP), float((2 * pair + 1) * CAP))
        columns = slice(pair * 2 * REQ, (pair + 1) * 2 * REQ)
        target_ref[:, columns] = jnp.where(both >= 0.0, both + block, -1.0)
        gate_ref[:, columns] = jnp.concatenate([left[:, REQ:], right[:, REQ:]], axis=1)
    for z in range(NZ):
        for k in range(ROWS):
            first = z * REQ + k * PLANE
            rows_ref[first : first + PLANE, :] = spread_ref[z, :, k * QUARTER : (k + 1) * QUARTER]
    slot = lax.broadcasted_iota(jnp.int32, (BLOCK, TOKENS), 0).astype(jnp.float32)
    for e in range(PLANE):
        hit = target_ref[e : e + 1, :] == slot
        pick_ref[e * BLOCK : (e + 1) * BLOCK, :] = jnp.where(hit, 1.0, 0.0).astype(jnp.bfloat16)
    for e in range(0, PLANE, 4):
        rows = jnp.dot(
            pick_ref[e * BLOCK : (e + 4) * BLOCK, :],
            rows_ref[...],
            preferred_element_type=jnp.float32,
        ).astype(jnp.bfloat16)
        for k in range(4):
            out_ref[e + k] = rows[k * BLOCK : (k + 1) * BLOCK, :]


def hold_kernel(*refs):
    del refs


def combine_kernel(target_ref, gate_ref, rows_ref, out_ref, weight_ref, packed_ref):
    slot = lax.broadcasted_iota(jnp.int32, (BLOCK, TOKENS), 0).astype(jnp.float32)
    for e in range(PLANE):
        hit = target_ref[e : e + 1, :] == slot
        weight = jnp.where(hit, gate_ref[e : e + 1, :], 0.0)
        weight_ref[e * BLOCK : (e + 1) * BLOCK, :] = weight.astype(jnp.bfloat16)
        packed_ref[e * BLOCK : (e + 1) * BLOCK, :] = rows_ref[e]
    dims = (((0,), (0,)), ((), ()))
    total = lax.dot_general(
        weight_ref[...], packed_ref[...], dims, preferred_element_type=jnp.float32
    ).astype(jnp.bfloat16)
    for z in range(NZ):
        out_ref[z] = total[z * REQ : (z + 1) * REQ, :]


def load_weights(blocks, weight_ref, sems):
    copies = []
    for part in range(3):
        for q, block in enumerate(blocks):
            copies.append(
                pltpu.make_async_copy(
                    block.at[part], weight_ref.at[part, pl.ds(q * EHQ, EHQ)], sems.at[part, q]
                )
            )
    for copy in copies:
        copy.start()
    return copies


def activate(normed_ref, weight_ref, act_ref, copies):
    dims = (((1,), (1,)), ((), ()))
    for copy in copies[:2]:
        copy.wait()
    gate = lax.dot_general(
        normed_ref[...], weight_ref[0], dims, preferred_element_type=jnp.float32
    )
    for copy in copies[2:4]:
        copy.wait()
    up = lax.dot_general(normed_ref[...], weight_ref[1], dims, preferred_element_type=jnp.float32)
    act_ref[...] = (gate / (1.0 + jnp.exp(-gate)) * up).astype(jnp.bfloat16)
    for copy in copies[4:]:
        copy.wait()


def first_half_kernel(rows_ref, gain_ref, w0, w1, normed_ref, part_ref, weight_ref, act_ref, sems):
    copies = load_weights((w0, w1), weight_ref, sems)
    for x in range(NX):
        parts = [rows_ref[x * NY + y].astype(jnp.float32) for y in range(NY)]
        square = sum(jnp.sum(part * part, axis=-1, keepdims=True) for part in parts)
        scale = lax.rsqrt(square * (1.0 / WIDTH) + 1e-06)
        for y in range(NY):
            columns = slice(y * QUARTER, (y + 1) * QUARTER)
            normed_ref[x * BLOCK : (x + 1) * BLOCK, columns] = (
                parts[y] * scale * gain_ref[:, columns]
            ).astype(jnp.bfloat16)
    activate(normed_ref, weight_ref, act_ref, copies)
    part_ref[...] = jnp.dot(act_ref[...], weight_ref[2], preferred_element_type=jnp.float32)


def second_half_kernel(normed_ref, part_ref, w2, w3, out_ref, weight_ref, act_ref, sems):
    copies = load_weights((w2, w3), weight_ref, sems)
    activate(normed_ref, weight_ref, act_ref, copies)
    for y in range(NY):
        columns = slice(y * QUARTER, (y + 1) * QUARTER)
        part = part_ref[:, columns] + jnp.dot(
            act_ref[...], weight_ref[2, :, columns], preferred_element_type=jnp.float32
        )
        part = part.astype(jnp.bfloat16)
        for x in range(NX):
            out_ref[x * NY + y] = part[x * BLOCK : (x + 1) * BLOCK, :]


def vmem():
    return pl.BlockSpec(memory_space=pltpu.VMEM)


def anywhere():
    return pl.BlockSpec(memory_space=pl.ANY)


def params(mib=16):
    return pltpu.CompilerParams(vmem_limit_bytes=mib * 1024 * 1024)


def shape(*dims, dtype=jnp.bfloat16):
    return jax.ShapeDtypeStruct(dims, dtype)


def attend(lengths, queries, fresh, cache, weight):
    hbm = pl.BlockSpec(memory_space=pltpu.HBM)
    return pl.pallas_call(
        attention_kernel,
        out_shape=shape(NY, REQ, QUARTER),
        in_specs=[pl.BlockSpec(memory_space=pltpu.SMEM), vmem(), vmem(), hbm, hbm],
        out_specs=vmem(),
        scratch_shapes=[
            pltpu.VMEM((REQ, 2, CTX, HD), jnp.bfloat16),
            pltpu.VMEM((HEADS * HD, WIDTH), jnp.bfloat16),
            pltpu.VMEM((REQ, HEADS * HD), jnp.bfloat16),
            pltpu.SemaphoreType.DMA((REQ // CHUNK,)),
            pltpu.SemaphoreType.DMA,
        ],
        compiler_params=params(24),
        name="attend",
    )(lengths, queries, fresh, cache, weight)


def make_plan(ids, gates):
    return pl.pallas_call(
        plan_kernel,
        out_shape=shape(NZ, PLANE, 2 * REQ),
        in_specs=[vmem(), vmem()],
        out_specs=vmem(),
        compiler_params=params(),
        name="plan",
    )(ids, gates)


def pick_weights(first, after, gate_up, down):
    block = shape(3, EHQ, WIDTH)
    return pl.pallas_call(
        pick_kernel,
        out_shape=(block, block),
        in_specs=[pl.BlockSpec(memory_space=pltpu.SMEM), anywhere()]
        + [pl.BlockSpec(memory_space=pltpu.HBM)] * 2,
        out_specs=(anywhere(), anywhere()),
        scratch_shapes=[pltpu.SemaphoreType.DMA((4,))],
        compiler_params=params(),
        name="pick_weights",
    )(first, after, gate_up, down)


def sum_middle(pieces, hidden, plan, blocks):
    return pl.pallas_call(
        middle_kernel,
        out_shape=(
            shape(NZ, PLANE, WIDTH + 2 * REQ),
            shape(REQ, QUARTER),
            *[shape(*block.shape) for block in blocks],
        ),
        in_specs=[vmem()] * 3 + [anywhere()] * 2,
        out_specs=(vmem(), vmem()) + (anywhere(),) * 2,
        input_output_aliases={3: 2, 4: 3},
        compiler_params=params(),
        name="sum_middle",
    )(pieces, hidden, plan, *blocks)


def gather_rows(spread):
    return pl.pallas_call(
        gather_kernel,
        out_shape=(
            shape(PLANE, BLOCK, QUARTER),
            shape(PLANE, TOKENS, dtype=jnp.float32),
            shape(PLANE, TOKENS, dtype=jnp.float32),
        ),
        in_specs=[vmem()],
        out_specs=(vmem(), vmem(), vmem()),
        scratch_shapes=[
            pltpu.VMEM((PLANE * BLOCK, TOKENS), jnp.bfloat16),
            pltpu.VMEM((TOKENS, QUARTER), jnp.bfloat16),
        ],
        compiler_params=params(),
        name="gather_rows",
    )(spread)


def hold(after, block):
    return pl.pallas_call(
        hold_kernel,
        out_shape=shape(*block.shape),
        in_specs=[anywhere()] * 2,
        out_specs=anywhere(),
        input_output_aliases={1: 0},
        compiler_params=params(),
        name="hold",
    )(after, block)


def combine_rows(target, gate, rows):
    return pl.pallas_call(
        combine_kernel,
        out_shape=shape(NZ, REQ, QUARTER),
        in_specs=[vmem(), vmem(), vmem()],
        out_specs=vmem(),
        scratch_shapes=[
            pltpu.VMEM((PLANE * BLOCK, TOKENS), jnp.bfloat16),
            pltpu.VMEM((PLANE * BLOCK, QUARTER), jnp.bfloat16),
        ],
        compiler_params=params(),
        name="combine_rows",
    )(target, gate, rows)


def half_scratch():
    return [
        pltpu.VMEM((3, 2 * EHQ, WIDTH), jnp.bfloat16),
        pltpu.VMEM((NX * BLOCK, 2 * EHQ), jnp.bfloat16),
        pltpu.SemaphoreType.DMA((3, 2)),
    ]


def first_half(rows, gain, blocks):
    return pl.pallas_call(
        first_half_kernel,
        out_shape=(shape(NX * BLOCK, WIDTH), shape(NX * BLOCK, WIDTH, dtype=jnp.float32)),
        in_specs=[vmem(), vmem()] + [anywhere()] * 2,
        out_specs=(vmem(), vmem()),
        scratch_shapes=half_scratch(),
        compiler_params=params(24),
        name="first_half",
    )(rows, gain, *blocks)


def second_half(normed, part, blocks):
    return pl.pallas_call(
        second_half_kernel,
        out_shape=shape(PLANE, BLOCK, QUARTER),
        in_specs=[vmem(), vmem()] + [anywhere()] * 2,
        out_specs=vmem(),
        scratch_shapes=half_scratch(),
        compiler_params=params(24),
        name="second_half",
    )(normed, part, *blocks)


def move_weights(blocks):
    even, odd = [], []
    for c in range(NC):
        for y in range(NY):
            even.append((c * NY + y, (1 - y // 2) * NY + 2 * c + y % 2))
            odd.append((c * NY + y, (y // 2) * NY + 2 * c + 1 - y % 2))
    return [lax.ppermute(block, ("c", "y"), to) for block, to in zip(blocks, (even, odd))]


def talker_plan(owners, section):
    own = lax.dynamic_slice_in_dim(owners, section * REQ, REQ)
    order = jnp.arange(REQ, dtype=jnp.int32)
    same = (own[:, None] == own[None, :]) & (order[:, None] > order[None, :])
    position = jnp.sum(same.astype(jnp.int32), axis=1)
    slot = jnp.where(own >= 0, own * HCAP + position, -1)
    send = (jnp.arange(SECTIONS * HCAP, dtype=jnp.int32)[:, None] == slot[None, :]).astype(
        jnp.bfloat16
    )
    counts = jnp.sum((owners == section).reshape(SECTIONS, REQ).astype(jnp.int32), axis=1)
    place = jnp.arange(SECTIONS, dtype=jnp.int32)
    offsets = jnp.sum(jnp.where(place[None, :] < place[:, None], counts[None, :], 0), axis=1)
    index = jnp.arange(HCAP, dtype=jnp.int32)
    put = jnp.where(index[None, :] < counts[:, None], offsets[:, None] + index[None, :], -1)
    put = put.reshape(SECTIONS * HCAP)
    take = (jnp.arange(SECTIONS * HCAP, dtype=jnp.int32)[:, None] == put[None, :]).astype(
        jnp.bfloat16
    )
    return send, take


def local(
    hidden_in,
    queries,
    new_kv,
    cache,
    lengths,
    out_weight,
    moe_gain,
    expert_ids,
    expert_gates,
    gate_up,
    down,
    owners,
):
    z, x, c, y = (lax.axis_index(name) for name in ("z", "x", "c", "y"))
    section = (z * NX + x) * NC + c
    plan = make_plan(expert_ids.T, expert_gates.T)
    pieces = attend(lengths, queries, new_kv, cache, out_weight)
    first = (y % 2).astype(jnp.int32).reshape(1)
    blocks = pick_weights(first, pieces, gate_up.transpose(0, 1, 3, 2), down)
    pieces = lax.all_to_all(pieces, "y", 0, 0, tiled=True)
    hidden = lax.dynamic_slice_in_dim(hidden_in, y * QUARTER, QUARTER, 1)
    message, middle, *blocks = sum_middle(pieces, hidden, plan, blocks)
    even, odd = move_weights(blocks)
    swap = [(0, 1), (1, 0)]

    spread = lax.all_to_all(message, "z", 0, 0, tiled=True)
    send, target, gate = gather_rows(spread)
    rows = lax.all_to_all(send, ("x", "y"), 0, 0, tiled=True)
    odd = hold(rows, odd)
    even_swapped = lax.ppermute(even, "c", swap)
    odd_swapped = lax.ppermute(odd, "c", swap)
    normed, half = first_half(rows, moe_gain.reshape(1, WIDTH), (even, even_swapped))
    done = second_half(normed, half, (odd, odd_swapped))
    back = lax.all_to_all(done, ("x", "y"), 0, 0, tiled=True)
    part = combine_rows(target, gate, back)
    part = lax.all_to_all(part, "z", 0, 0, tiled=True)
    out = middle.astype(jnp.float32) + jnp.sum(part.astype(jnp.float32), axis=0)
    out = out.astype(jnp.bfloat16)

    send_pick, take_pick = talker_plan(owners, section)
    leaving = jnp.dot(send_pick, out, preferred_element_type=jnp.float32).astype(jnp.bfloat16)
    arrived = lax.all_to_all(
        leaving.reshape(SECTIONS, HCAP, QUARTER), ("z", "x", "c"), 0, 0, tiled=True
    )
    talker = jnp.dot(
        take_pick, arrived.reshape(SECTIONS * HCAP, QUARTER), preferred_element_type=jnp.float32
    ).astype(jnp.bfloat16)
    return (out, talker)


def solution(mesh):
    section = ("z", "x", "c")
    fine = Mesh(mesh.devices.reshape(NZ, NX, NC, NY), ("z", "x", "c", "y"))
    in_specs = (
        P(section, None),
        P(section, "y"),
        P(section, None, "y"),
        P(section, None, None, "y"),
        P(section),
        P("y", None),
        P(),
        P(section, None),
        P(section, None),
        P(section, None, None, "y"),
        P(section, "y", None),
        P(),
    )
    out_specs = (P(section, "y"), P(section, "y"))
    return jax.shard_map(local, mesh=fine, in_specs=in_specs, out_specs=out_specs, check_vma=False)
```

```python
import math

import jax
import jax.numpy as jnp
from jax import lax
from jax.experimental import pallas as pl
from jax.experimental.pallas import tpu as pltpu
from jax.sharding import Mesh
from jax.sharding import PartitionSpec as P

HD = 128
HCAP = 2
CAP = 10
NZ, NX, NC, NY = 8, 4, 2, 4
REQ = 64
SECTIONS = NZ * NX * NC
TOKENS = NZ * REQ
PLANE = NX * NY
BLOCK = NZ * CAP
ROWS = REQ // PLANE
QUARTER = 512
HEADS = 8
CTX = 96
CHUNK = 16
WIDTH = 2048
EHQ = 192


def attention_kernel(lengths_ref, queries_ref, fresh_ref, cache, weight, out_ref, *scratch):
    cache_ref, weight_ref, context_ref, cache_sem, weight_sem = scratch
    loads = []
    for i in range(REQ // CHUNK):
        rows = pl.ds(i * CHUNK, CHUNK)
        loads.append(pltpu.make_async_copy(cache.at[rows], cache_ref.at[rows], cache_sem.at[i]))
    for copy in loads:
        copy.start()
    whole = pltpu.make_async_copy(weight, weight_ref, weight_sem)
    whole.start()
    scale = 1.0 / math.sqrt(HD)
    cell = lax.broadcasted_iota(jnp.int32, (HEADS, CTX), 1)
    for i in range(REQ // CHUNK):
        rows = slice(i * CHUNK, (i + 1) * CHUNK)
        heads = queries_ref[rows, :].astype(jnp.float32).reshape(CHUNK, HEADS, HD)
        fresh = fresh_ref[rows].astype(jnp.float32)
        loads[i].wait()
        keys, values = cache_ref[rows, 0], cache_ref[rows, 1]
        scores = lax.dot_general(
            heads.astype(jnp.bfloat16), keys, (((2,), (2,)), ((0,), (0,))), preferred_element_type=jnp.float32
        )
        scores = scores * scale
        scores = jnp.stack(
            [jnp.where(cell < lengths_ref[i * CHUNK + r], scores[r], -jnp.inf) for r in range(CHUNK)]
        )
        new = jnp.sum(heads * fresh[:, 0:1, :], axis=-1, keepdims=True) * scale
        top = jnp.maximum(jnp.max(scores, axis=-1, keepdims=True), new)
        mass = jnp.exp(scores - top)
        new = jnp.exp(new - top)
        total = jnp.sum(mass, axis=-1, keepdims=True) + new
        mass = (mass / total).astype(jnp.bfloat16)
        new = (new / total).astype(jnp.bfloat16).astype(jnp.float32)
        context = lax.dot_general(
            mass, values, (((2,), (1,)), ((0,), (0,))), preferred_element_type=jnp.float32
        ) + new * fresh[:, 1:2, :]
        context_ref[rows, :] = context.reshape(CHUNK, HEADS * HD).astype(jnp.bfloat16)
    whole.wait()
    for y in range(NY):
        out_ref[y] = jnp.dot(
            context_ref[...], weight_ref[:, y * QUARTER : (y + 1) * QUARTER],
            preferred_element_type=jnp.float32,
        ).astype(jnp.bfloat16)


def plan_kernel(ids_ref, gates_ref, out_ref):
    ids = jnp.concatenate([ids_ref[...], ids_ref[...]], axis=1)
    gates = jnp.concatenate([gates_ref[...], gates_ref[...]], axis=1)
    gates = gates / jnp.sum(gates, axis=0, keepdims=True)
    experts = NZ * PLANE
    expert = lax.broadcasted_iota(jnp.int32, (experts, 2 * REQ), 0)
    chosen = jnp.zeros((experts, 2 * REQ), jnp.float32)
    gate = jnp.zeros((experts, 2 * REQ), jnp.float32)
    for k in range(8):
        hit = ids[k : k + 1, :] == expert
        chosen = jnp.where(hit, 1.0, chosen)
        gate = jnp.where(hit, gates[k : k + 1, :], gate)
    earlier = lax.broadcasted_iota(jnp.int32, (2 * REQ, 2 * REQ), 0)
    token = lax.broadcasted_iota(jnp.int32, (2 * REQ, 2 * REQ), 1)
    token = jnp.where(token >= REQ, token - REQ, token)
    before = jnp.where(earlier < token, 1.0, 0.0).astype(jnp.bfloat16)
    rank = jnp.dot(chosen.astype(jnp.bfloat16), before, preferred_element_type=jnp.float32)
    slot = jnp.where(chosen > 0.0, rank, -1.0)
    first = lax.broadcasted_iota(jnp.int32, (experts, 2 * REQ), 1) < REQ
    both = jnp.where(first, slot, gate).astype(jnp.bfloat16)
    for z in range(NZ):
        out_ref[z] = both[z * PLANE : (z + 1) * PLANE, :]


def pick_kernel(first_ref, after_ref, gate_up, down, even_ref, odd_ref, sems):
    first = first_ref[0]
    copies = []
    for k, out in ((0, even_ref), (1, odd_ref)):
        index = first if k == 0 else 1 - first
        copies.append(pltpu.make_async_copy(gate_up.at[index], out.at[pl.ds(0, 2)], sems.at[2 * k]))
        copies.append(pltpu.make_async_copy(down.at[index], out.at[2], sems.at[2 * k + 1]))
    for copy in copies:
        copy.start()
    for copy in copies:
        copy.wait()


def middle_kernel(pieces_ref, hidden_ref, plan_ref, message_ref, middle_ref):
    total = hidden_ref[...].astype(jnp.float32)
    for y in range(NY):
        total = total + pieces_ref[y].astype(jnp.float32)
    middle = total.astype(jnp.bfloat16)
    middle_ref[...] = middle
    for z in range(NZ):
        for k in range(ROWS):
            message_ref[z, :, k * QUARTER : (k + 1) * QUARTER] = middle[k * PLANE : (k + 1) * PLANE, :]
        message_ref[z, :, WIDTH:] = plan_ref[z]


def gather_kernel(spread_ref, out_ref, target_ref, gate_ref, pick_ref, rows_ref):
    low = lax.broadcasted_iota(jnp.int32, (PLANE, 2 * REQ), 1) < REQ
    for pair in range(NZ // 2):
        left = spread_ref[2 * pair, :, WIDTH:].astype(jnp.float32)
        right = spread_ref[2 * pair + 1, :, WIDTH:].astype(jnp.float32)
        both = jnp.concatenate([left[:, :REQ], right[:, :REQ]], axis=1)
        block = jnp.where(low, float(2 * pair * CAP), float((2 * pair + 1) * CAP))
        columns = slice(pair * 2 * REQ, (pair + 1) * 2 * REQ)
        target_ref[:, columns] = jnp.where(both >= 0.0, both + block, -1.0)
        gate_ref[:, columns] = jnp.concatenate([left[:, REQ:], right[:, REQ:]], axis=1)
    for z in range(NZ):
        for k in range(ROWS):
            first = z * REQ + k * PLANE
            rows_ref[first : first + PLANE, :] = spread_ref[z, :, k * QUARTER : (k + 1) * QUARTER]
    slot = lax.broadcasted_iota(jnp.int32, (BLOCK, TOKENS), 0).astype(jnp.float32)
    for e in range(PLANE):
        hit = target_ref[e : e + 1, :] == slot
        pick_ref[e * BLOCK : (e + 1) * BLOCK, :] = jnp.where(hit, 1.0, 0.0).astype(jnp.bfloat16)
    for e in range(0, PLANE, 4):
        rows = jnp.dot(
            pick_ref[e * BLOCK : (e + 4) * BLOCK, :],
            rows_ref[...],
            preferred_element_type=jnp.float32,
        ).astype(jnp.bfloat16)
        for k in range(4):
            out_ref[e + k] = rows[k * BLOCK : (k + 1) * BLOCK, :]


def hold_kernel(*refs):
    del refs


def combine_kernel(target_ref, gate_ref, rows_ref, out_ref, weight_ref, packed_ref):
    slot = lax.broadcasted_iota(jnp.int32, (BLOCK, TOKENS), 0).astype(jnp.float32)
    for e in range(PLANE):
        hit = target_ref[e : e + 1, :] == slot
        weight = jnp.where(hit, gate_ref[e : e + 1, :], 0.0)
        weight_ref[e * BLOCK : (e + 1) * BLOCK, :] = weight.astype(jnp.bfloat16)
        packed_ref[e * BLOCK : (e + 1) * BLOCK, :] = rows_ref[e]
    dims = (((0,), (0,)), ((), ()))
    total = lax.dot_general(
        weight_ref[...], packed_ref[...], dims, preferred_element_type=jnp.float32
    ).astype(jnp.bfloat16)
    for z in range(NZ):
        out_ref[z] = total[z * REQ : (z + 1) * REQ, :]


def load_weights(blocks, weight_ref, sems):
    copies = []
    for part in range(3):
        for q, block in enumerate(blocks):
            copies.append(
                pltpu.make_async_copy(
                    block.at[part], weight_ref.at[part, pl.ds(q * EHQ, EHQ)], sems.at[part, q]
                )
            )
    for copy in copies:
        copy.start()
    return copies


def activate(normed_ref, weight_ref, act_ref, copies):
    dims = (((1,), (1,)), ((), ()))
    for copy in copies[:2]:
        copy.wait()
    gate = lax.dot_general(
        normed_ref[...], weight_ref[0], dims, preferred_element_type=jnp.float32
    )
    for copy in copies[2:4]:
        copy.wait()
    up = lax.dot_general(normed_ref[...], weight_ref[1], dims, preferred_element_type=jnp.float32)
    act_ref[...] = (gate / (1.0 + jnp.exp(-gate)) * up).astype(jnp.bfloat16)
    for copy in copies[4:]:
        copy.wait()


def first_half_kernel(rows_ref, gain_ref, w0, w1, normed_ref, part_ref, weight_ref, act_ref, sems):
    copies = load_weights((w0, w1), weight_ref, sems)
    for x in range(NX):
        parts = [rows_ref[x * NY + y].astype(jnp.float32) for y in range(NY)]
        square = sum(jnp.sum(part * part, axis=-1, keepdims=True) for part in parts)
        scale = lax.rsqrt(square * (1.0 / WIDTH) + 1e-06)
        for y in range(NY):
            columns = slice(y * QUARTER, (y + 1) * QUARTER)
            normed_ref[x * BLOCK : (x + 1) * BLOCK, columns] = (
                parts[y] * scale * gain_ref[:, columns]
            ).astype(jnp.bfloat16)
    activate(normed_ref, weight_ref, act_ref, copies)
    part_ref[...] = jnp.dot(act_ref[...], weight_ref[2], preferred_element_type=jnp.float32)


def second_half_kernel(normed_ref, part_ref, w2, w3, out_ref, weight_ref, act_ref, sems):
    copies = load_weights((w2, w3), weight_ref, sems)
    activate(normed_ref, weight_ref, act_ref, copies)
    for y in range(NY):
        columns = slice(y * QUARTER, (y + 1) * QUARTER)
        part = part_ref[:, columns] + jnp.dot(
            act_ref[...], weight_ref[2, :, columns], preferred_element_type=jnp.float32
        )
        part = part.astype(jnp.bfloat16)
        for x in range(NX):
            out_ref[x * NY + y] = part[x * BLOCK : (x + 1) * BLOCK, :]


def vmem():
    return pl.BlockSpec(memory_space=pltpu.VMEM)


def anywhere():
    return pl.BlockSpec(memory_space=pl.ANY)


def params(mib=16):
    return pltpu.CompilerParams(vmem_limit_bytes=mib * 1024 * 1024)


def shape(*dims, dtype=jnp.bfloat16):
    return jax.ShapeDtypeStruct(dims, dtype)


def attend(lengths, queries, fresh, cache, weight):
    hbm = pl.BlockSpec(memory_space=pltpu.HBM)
    return pl.pallas_call(
        attention_kernel,
        out_shape=shape(NY, REQ, QUARTER),
        in_specs=[pl.BlockSpec(memory_space=pltpu.SMEM), vmem(), vmem(), hbm, hbm],
        out_specs=vmem(),
        scratch_shapes=[
            pltpu.VMEM((REQ, 2, CTX, HD), jnp.bfloat16),
            pltpu.VMEM((HEADS * HD, WIDTH), jnp.bfloat16),
            pltpu.VMEM((REQ, HEADS * HD), jnp.bfloat16),
            pltpu.SemaphoreType.DMA((REQ // CHUNK,)),
            pltpu.SemaphoreType.DMA,
        ],
        compiler_params=params(60),
        name="attend",
    )(lengths, queries, fresh, cache, weight)


def make_plan(ids, gates):
    return pl.pallas_call(
        plan_kernel,
        out_shape=shape(NZ, PLANE, 2 * REQ),
        in_specs=[vmem(), vmem()],
        out_specs=vmem(),
        compiler_params=params(),
        name="plan",
    )(ids, gates)


def pick_weights(first, after, gate_up, down):
    block = shape(3, EHQ, WIDTH)
    return pl.pallas_call(
        pick_kernel,
        out_shape=(block, block),
        in_specs=[pl.BlockSpec(memory_space=pltpu.SMEM), anywhere()]
        + [pl.BlockSpec(memory_space=pltpu.HBM)] * 2,
        out_specs=(anywhere(), anywhere()),
        scratch_shapes=[pltpu.SemaphoreType.DMA((4,))],
        compiler_params=params(60),
        name="pick_weights",
    )(first, after, gate_up, down)


def sum_middle(pieces, hidden, plan):
    return pl.pallas_call(
        middle_kernel,
        out_shape=(shape(NZ, PLANE, WIDTH + 2 * REQ), shape(REQ, QUARTER)),
        in_specs=[vmem()] * 3,
        out_specs=(vmem(), vmem()),
        compiler_params=params(),
        name="sum_middle",
    )(pieces, hidden, plan)


def gather_rows(spread):
    return pl.pallas_call(
        gather_kernel,
        out_shape=(
            shape(PLANE, BLOCK, QUARTER),
            shape(PLANE, TOKENS, dtype=jnp.float32),
            shape(PLANE, TOKENS, dtype=jnp.float32),
        ),
        in_specs=[vmem()],
        out_specs=(vmem(), vmem(), vmem()),
        scratch_shapes=[
            pltpu.VMEM((PLANE * BLOCK, TOKENS), jnp.bfloat16),
            pltpu.VMEM((TOKENS, QUARTER), jnp.bfloat16),
        ],
        compiler_params=params(),
        name="gather_rows",
    )(spread)


def hold(after, block):
    return pl.pallas_call(
        hold_kernel,
        out_shape=shape(*block.shape),
        in_specs=[anywhere()] * 2,
        out_specs=anywhere(),
        input_output_aliases={1: 0},
        compiler_params=params(),
        name="hold",
    )(after, block)


def combine_rows(target, gate, rows):
    return pl.pallas_call(
        combine_kernel,
        out_shape=shape(NZ, REQ, QUARTER),
        in_specs=[vmem(), vmem(), vmem()],
        out_specs=vmem(),
        scratch_shapes=[
            pltpu.VMEM((PLANE * BLOCK, TOKENS), jnp.bfloat16),
            pltpu.VMEM((PLANE * BLOCK, QUARTER), jnp.bfloat16),
        ],
        compiler_params=params(),
        name="combine_rows",
    )(target, gate, rows)


def half_scratch():
    return [
        pltpu.VMEM((3, 2 * EHQ, WIDTH), jnp.bfloat16),
        pltpu.VMEM((NX * BLOCK, 2 * EHQ), jnp.bfloat16),
        pltpu.SemaphoreType.DMA((3, 2)),
    ]


def first_half(rows, gain, blocks):
    return pl.pallas_call(
        first_half_kernel,
        out_shape=(shape(NX * BLOCK, WIDTH), shape(NX * BLOCK, WIDTH, dtype=jnp.float32)),
        in_specs=[vmem(), vmem()] + [anywhere()] * 2,
        out_specs=(vmem(), vmem()),
        scratch_shapes=half_scratch(),
        compiler_params=params(24),
        name="first_half",
    )(rows, gain, *blocks)


def second_half(normed, part, blocks):
    return pl.pallas_call(
        second_half_kernel,
        out_shape=shape(PLANE, BLOCK, QUARTER),
        in_specs=[vmem(), vmem()] + [anywhere()] * 2,
        out_specs=vmem(),
        scratch_shapes=half_scratch(),
        compiler_params=params(24),
        name="second_half",
    )(normed, part, *blocks)


def move_weights(blocks):
    even, odd = [], []
    for c in range(NC):
        for y in range(NY):
            even.append((c * NY + y, (1 - y // 2) * NY + 2 * c + y % 2))
            odd.append((c * NY + y, (y // 2) * NY + 2 * c + 1 - y % 2))
    return [lax.ppermute(block, ("c", "y"), to) for block, to in zip(blocks, (even, odd))]


def talker_plan(owners, section):
    own = lax.dynamic_slice_in_dim(owners, section * REQ, REQ)
    order = jnp.arange(REQ, dtype=jnp.int32)
    same = (own[:, None] == own[None, :]) & (order[:, None] > order[None, :])
    position = jnp.sum(same.astype(jnp.int32), axis=1)
    slot = jnp.where(own >= 0, own * HCAP + position, -1)
    send = (jnp.arange(SECTIONS * HCAP, dtype=jnp.int32)[:, None] == slot[None, :]).astype(
        jnp.bfloat16
    )
    counts = jnp.sum((owners == section).reshape(SECTIONS, REQ).astype(jnp.int32), axis=1)
    place = jnp.arange(SECTIONS, dtype=jnp.int32)
    offsets = jnp.sum(jnp.where(place[None, :] < place[:, None], counts[None, :], 0), axis=1)
    index = jnp.arange(HCAP, dtype=jnp.int32)
    put = jnp.where(index[None, :] < counts[:, None], offsets[:, None] + index[None, :], -1)
    put = put.reshape(SECTIONS * HCAP)
    take = (jnp.arange(SECTIONS * HCAP, dtype=jnp.int32)[:, None] == put[None, :]).astype(
        jnp.bfloat16
    )
    return send, take


def local(
    hidden_in,
    queries,
    new_kv,
    cache,
    lengths,
    out_weight,
    moe_gain,
    expert_ids,
    expert_gates,
    gate_up,
    down,
    owners,
):
    z, x, c, y = (lax.axis_index(name) for name in ("z", "x", "c", "y"))
    section = (z * NX + x) * NC + c
    plan = make_plan(expert_ids.T, expert_gates.T)
    pieces = attend(lengths, queries, new_kv, cache, out_weight)
    first = (y % 2).astype(jnp.int32).reshape(1)
    blocks = pick_weights(first, pieces, gate_up.transpose(0, 1, 3, 2), down)
    pieces = lax.all_to_all(pieces, "y", 0, 0, tiled=True)
    hidden = lax.dynamic_slice_in_dim(hidden_in, y * QUARTER, QUARTER, 1)
    message, middle = sum_middle(pieces, hidden, plan)
    even, odd = move_weights(blocks)
    swap = [(0, 1), (1, 0)]

    spread = lax.all_to_all(message, "z", 0, 0, tiled=True)
    send, target, gate = gather_rows(spread)
    rows = lax.all_to_all(send, ("x", "y"), 0, 0, tiled=True)
    odd = hold(rows, odd)
    even_swapped = lax.ppermute(even, "c", swap)
    odd_swapped = lax.ppermute(odd, "c", swap)
    normed, half = first_half(rows, moe_gain.reshape(1, WIDTH), (even, even_swapped))
    done = second_half(normed, half, (odd, odd_swapped))
    back = lax.all_to_all(done, ("x", "y"), 0, 0, tiled=True)
    part = combine_rows(target, gate, back)
    part = lax.all_to_all(part, "z", 0, 0, tiled=True)
    out = middle.astype(jnp.float32) + jnp.sum(part.astype(jnp.float32), axis=0)
    out = out.astype(jnp.bfloat16)

    send_pick, take_pick = talker_plan(owners, section)
    leaving = jnp.dot(send_pick, out, preferred_element_type=jnp.float32).astype(jnp.bfloat16)
    arrived = lax.all_to_all(
        leaving.reshape(SECTIONS, HCAP, QUARTER), ("z", "x", "c"), 0, 0, tiled=True
    )
    talker = jnp.dot(
        take_pick, arrived.reshape(SECTIONS * HCAP, QUARTER), preferred_element_type=jnp.float32
    ).astype(jnp.bfloat16)
    return (out, talker)


def solution(mesh):
    section = ("z", "x", "c")
    fine = Mesh(mesh.devices.reshape(NZ, NX, NC, NY), ("z", "x", "c", "y"))
    in_specs = (
        P(section, None),
        P(section, "y"),
        P(section, None, "y"),
        P(section, None, None, "y"),
        P(section),
        P("y", None),
        P(),
        P(section, None),
        P(section, None),
        P(section, None, None, "y"),
        P(section, "y", None),
        P(),
    )
    out_specs = (P(section, "y"), P(section, "y"))
    return jax.shard_map(local, mesh=fine, in_specs=in_specs, out_specs=out_specs, check_vma=False)
```

```python
import math

import jax
import jax.numpy as jnp
from jax import lax
from jax.experimental import pallas as pl
from jax.experimental.pallas import tpu as pltpu
from jax.sharding import Mesh
from jax.sharding import PartitionSpec as P

HD = 128
HCAP = 2
CAP = 10
NZ, NX, NC, NY = 8, 4, 2, 4
REQ = 64
SECTIONS = NZ * NX * NC
TOKENS = NZ * REQ
PLANE = NX * NY
BLOCK = NZ * CAP
ROWS = REQ // PLANE
QUARTER = 512
HEADS = 8
CTX = 96
CHUNK = 16
WIDTH = 2048
EHQ = 192


def attention_kernel(lengths_ref, queries_ref, fresh_ref, cache, weight, out_ref, *scratch):
    cache_ref, weight_ref, context_ref, cache_sem, weight_sem = scratch
    loads = []
    for i in range(REQ // CHUNK):
        rows = pl.ds(i * CHUNK, CHUNK)
        loads.append(pltpu.make_async_copy(cache.at[rows], cache_ref.at[rows], cache_sem.at[i]))
    for copy in loads:
        copy.start()
    whole = pltpu.make_async_copy(weight, weight_ref, weight_sem)
    whole.start()
    scale = 1.0 / math.sqrt(HD)
    cell = lax.broadcasted_iota(jnp.int32, (HEADS, CTX), 1)
    for i in range(REQ // CHUNK):
        rows = slice(i * CHUNK, (i + 1) * CHUNK)
        heads = queries_ref[rows, :].astype(jnp.float32).reshape(CHUNK, HEADS, HD)
        fresh = fresh_ref[rows].astype(jnp.float32)
        loads[i].wait()
        keys, values = cache_ref[rows, 0], cache_ref[rows, 1]
        scores = lax.dot_general(
            heads.astype(jnp.bfloat16), keys, (((2,), (2,)), ((0,), (0,))), preferred_element_type=jnp.float32
        )
        scores = scores * scale
        scores = jnp.stack(
            [jnp.where(cell < lengths_ref[i * CHUNK + r], scores[r], -jnp.inf) for r in range(CHUNK)]
        )
        new = jnp.sum(heads * fresh[:, 0:1, :], axis=-1, keepdims=True) * scale
        top = jnp.maximum(jnp.max(scores, axis=-1, keepdims=True), new)
        mass = jnp.exp(scores - top)
        new = jnp.exp(new - top)
        total = jnp.sum(mass, axis=-1, keepdims=True) + new
        mass = (mass / total).astype(jnp.bfloat16)
        new = (new / total).astype(jnp.bfloat16).astype(jnp.float32)
        context = lax.dot_general(
            mass, values, (((2,), (1,)), ((0,), (0,))), preferred_element_type=jnp.float32
        ) + new * fresh[:, 1:2, :]
        context_ref[rows, :] = context.reshape(CHUNK, HEADS * HD).astype(jnp.bfloat16)
    whole.wait()
    for y in range(NY):
        out_ref[y] = jnp.dot(
            context_ref[...], weight_ref[:, y * QUARTER : (y + 1) * QUARTER],
            preferred_element_type=jnp.float32,
        ).astype(jnp.bfloat16)


def plan_kernel(ids_ref, gates_ref, out_ref):
    ids = jnp.concatenate([ids_ref[...], ids_ref[...]], axis=1)
    gates = jnp.concatenate([gates_ref[...], gates_ref[...]], axis=1)
    gates = gates / jnp.sum(gates, axis=0, keepdims=True)
    experts = NZ * PLANE
    expert = lax.broadcasted_iota(jnp.int32, (experts, 2 * REQ), 0)
    chosen = jnp.zeros((experts, 2 * REQ), jnp.float32)
    gate = jnp.zeros((experts, 2 * REQ), jnp.float32)
    for k in range(8):
        hit = ids[k : k + 1, :] == expert
        chosen = jnp.where(hit, 1.0, chosen)
        gate = jnp.where(hit, gates[k : k + 1, :], gate)
    earlier = lax.broadcasted_iota(jnp.int32, (2 * REQ, 2 * REQ), 0)
    token = lax.broadcasted_iota(jnp.int32, (2 * REQ, 2 * REQ), 1)
    token = jnp.where(token >= REQ, token - REQ, token)
    before = jnp.where(earlier < token, 1.0, 0.0).astype(jnp.bfloat16)
    rank = jnp.dot(chosen.astype(jnp.bfloat16), before, preferred_element_type=jnp.float32)
    slot = jnp.where(chosen > 0.0, rank, -1.0)
    first = lax.broadcasted_iota(jnp.int32, (experts, 2 * REQ), 1) < REQ
    both = jnp.where(first, slot, gate).astype(jnp.bfloat16)
    for z in range(NZ):
        out_ref[z] = both[z * PLANE : (z + 1) * PLANE, :]


def pick_kernel(first_ref, after_ref, gate_up, down, even_ref, odd_ref, hold_ref, in_sems, out_sems):
    first = first_ref[0]
    loads, stores = [], []
    for k, out in ((0, even_ref), (1, odd_ref)):
        index = first if k == 0 else 1 - first
        for part in range(3):
            source = gate_up.at[index, part] if part < 2 else down.at[index]
            loads.append(
                pltpu.make_async_copy(source, hold_ref.at[k, part], in_sems.at[k, part])
            )
            stores.append(
                pltpu.make_async_copy(hold_ref.at[k, part], out.at[part], out_sems.at[k, part])
            )
    for copy in loads:
        copy.start()
    for load, store in zip(loads, stores):
        load.wait()
        store.start()
    for copy in stores:
        copy.wait()


def middle_kernel(pieces_ref, hidden_ref, plan_ref, message_ref, middle_ref):
    total = hidden_ref[...].astype(jnp.float32)
    for y in range(NY):
        total = total + pieces_ref[y].astype(jnp.float32)
    middle = total.astype(jnp.bfloat16)
    middle_ref[...] = middle
    for z in range(NZ):
        for k in range(ROWS):
            message_ref[z, :, k * QUARTER : (k + 1) * QUARTER] = middle[k * PLANE : (k + 1) * PLANE, :]
        message_ref[z, :, WIDTH:] = plan_ref[z]


def gather_kernel(spread_ref, out_ref, target_ref, gate_ref, pick_ref, rows_ref):
    low = lax.broadcasted_iota(jnp.int32, (PLANE, 2 * REQ), 1) < REQ
    for pair in range(NZ // 2):
        left = spread_ref[2 * pair, :, WIDTH:].astype(jnp.float32)
        right = spread_ref[2 * pair + 1, :, WIDTH:].astype(jnp.float32)
        both = jnp.concatenate([left[:, :REQ], right[:, :REQ]], axis=1)
        block = jnp.where(low, float(2 * pair * CAP), float((2 * pair + 1) * CAP))
        columns = slice(pair * 2 * REQ, (pair + 1) * 2 * REQ)
        target_ref[:, columns] = jnp.where(both >= 0.0, both + block, -1.0)
        gate_ref[:, columns] = jnp.concatenate([left[:, REQ:], right[:, REQ:]], axis=1)
    for z in range(NZ):
        for k in range(ROWS):
            first = z * REQ + k * PLANE
            rows_ref[first : first + PLANE, :] = spread_ref[z, :, k * QUARTER : (k + 1) * QUARTER]
    slot = lax.broadcasted_iota(jnp.int32, (BLOCK, TOKENS), 0).astype(jnp.float32)
    for e in range(PLANE):
        hit = target_ref[e : e + 1, :] == slot
        pick_ref[e * BLOCK : (e + 1) * BLOCK, :] = jnp.where(hit, 1.0, 0.0).astype(jnp.bfloat16)
    for e in range(0, PLANE, 4):
        rows = jnp.dot(
            pick_ref[e * BLOCK : (e + 4) * BLOCK, :],
            rows_ref[...],
            preferred_element_type=jnp.float32,
        ).astype(jnp.bfloat16)
        for k in range(4):
            out_ref[e + k] = rows[k * BLOCK : (k + 1) * BLOCK, :]


def hold_kernel(*refs):
    del refs


def combine_kernel(target_ref, gate_ref, rows_ref, out_ref, weight_ref, packed_ref):
    slot = lax.broadcasted_iota(jnp.int32, (BLOCK, TOKENS), 0).astype(jnp.float32)
    for e in range(PLANE):
        hit = target_ref[e : e + 1, :] == slot
        weight = jnp.where(hit, gate_ref[e : e + 1, :], 0.0)
        weight_ref[e * BLOCK : (e + 1) * BLOCK, :] = weight.astype(jnp.bfloat16)
        packed_ref[e * BLOCK : (e + 1) * BLOCK, :] = rows_ref[e]
    dims = (((0,), (0,)), ((), ()))
    total = lax.dot_general(
        weight_ref[...], packed_ref[...], dims, preferred_element_type=jnp.float32
    ).astype(jnp.bfloat16)
    for z in range(NZ):
        out_ref[z] = total[z * REQ : (z + 1) * REQ, :]


def load_weights(blocks, weight_ref, sems):
    copies = []
    for part in range(3):
        for q, block in enumerate(blocks):
            copies.append(
                pltpu.make_async_copy(
                    block.at[part], weight_ref.at[part, pl.ds(q * EHQ, EHQ)], sems.at[part, q]
                )
            )
    for copy in copies:
        copy.start()
    return copies


def activate(normed_ref, weight_ref, act_ref, copies):
    dims = (((1,), (1,)), ((), ()))
    for copy in copies[:2]:
        copy.wait()
    gate = lax.dot_general(
        normed_ref[...], weight_ref[0], dims, preferred_element_type=jnp.float32
    )
    for copy in copies[2:4]:
        copy.wait()
    up = lax.dot_general(normed_ref[...], weight_ref[1], dims, preferred_element_type=jnp.float32)
    act_ref[...] = (gate / (1.0 + jnp.exp(-gate)) * up).astype(jnp.bfloat16)
    for copy in copies[4:]:
        copy.wait()


def first_half_kernel(rows_ref, gain_ref, w0, w1, normed_ref, part_ref, weight_ref, act_ref, sems):
    copies = load_weights((w0, w1), weight_ref, sems)
    for x in range(NX):
        parts = [rows_ref[x * NY + y].astype(jnp.float32) for y in range(NY)]
        square = sum(jnp.sum(part * part, axis=-1, keepdims=True) for part in parts)
        scale = lax.rsqrt(square * (1.0 / WIDTH) + 1e-06)
        for y in range(NY):
            columns = slice(y * QUARTER, (y + 1) * QUARTER)
            normed_ref[x * BLOCK : (x + 1) * BLOCK, columns] = (
                parts[y] * scale * gain_ref[:, columns]
            ).astype(jnp.bfloat16)
    activate(normed_ref, weight_ref, act_ref, copies)
    part_ref[...] = jnp.dot(act_ref[...], weight_ref[2], preferred_element_type=jnp.float32)


def second_half_kernel(normed_ref, part_ref, w2, w3, out_ref, weight_ref, act_ref, sems):
    copies = load_weights((w2, w3), weight_ref, sems)
    activate(normed_ref, weight_ref, act_ref, copies)
    for y in range(NY):
        columns = slice(y * QUARTER, (y + 1) * QUARTER)
        part = part_ref[:, columns] + jnp.dot(
            act_ref[...], weight_ref[2, :, columns], preferred_element_type=jnp.float32
        )
        part = part.astype(jnp.bfloat16)
        for x in range(NX):
            out_ref[x * NY + y] = part[x * BLOCK : (x + 1) * BLOCK, :]


def vmem():
    return pl.BlockSpec(memory_space=pltpu.VMEM)


def anywhere():
    return pl.BlockSpec(memory_space=pl.ANY)


def params(mib=16):
    return pltpu.CompilerParams(vmem_limit_bytes=mib * 1024 * 1024)


def shape(*dims, dtype=jnp.bfloat16):
    return jax.ShapeDtypeStruct(dims, dtype)


def attend(lengths, queries, fresh, cache, weight):
    hbm = pl.BlockSpec(memory_space=pltpu.HBM)
    return pl.pallas_call(
        attention_kernel,
        out_shape=shape(NY, REQ, QUARTER),
        in_specs=[pl.BlockSpec(memory_space=pltpu.SMEM), vmem(), vmem(), hbm, hbm],
        out_specs=vmem(),
        scratch_shapes=[
            pltpu.VMEM((REQ, 2, CTX, HD), jnp.bfloat16),
            pltpu.VMEM((HEADS * HD, WIDTH), jnp.bfloat16),
            pltpu.VMEM((REQ, HEADS * HD), jnp.bfloat16),
            pltpu.SemaphoreType.DMA((REQ // CHUNK,)),
            pltpu.SemaphoreType.DMA,
        ],
        compiler_params=params(60),
        name="attend",
    )(lengths, queries, fresh, cache, weight)


def make_plan(ids, gates):
    return pl.pallas_call(
        plan_kernel,
        out_shape=shape(NZ, PLANE, 2 * REQ),
        in_specs=[vmem(), vmem()],
        out_specs=vmem(),
        compiler_params=params(),
        name="plan",
    )(ids, gates)


def pick_weights(first, after, gate_up, down):
    block = shape(3, EHQ, WIDTH)
    return pl.pallas_call(
        pick_kernel,
        out_shape=(block, block),
        in_specs=[pl.BlockSpec(memory_space=pltpu.SMEM), anywhere()]
        + [pl.BlockSpec(memory_space=pltpu.HBM)] * 2,
        out_specs=(anywhere(), anywhere()),
        scratch_shapes=[
            pltpu.VMEM((2, 3, EHQ, WIDTH), jnp.bfloat16),
            pltpu.SemaphoreType.DMA((2, 3)),
            pltpu.SemaphoreType.DMA((2, 3)),
        ],
        compiler_params=params(60),
        name="pick_weights",
    )(first, after, gate_up, down)


def sum_middle(pieces, hidden, plan):
    return pl.pallas_call(
        middle_kernel,
        out_shape=(shape(NZ, PLANE, WIDTH + 2 * REQ), shape(REQ, QUARTER)),
        in_specs=[vmem()] * 3,
        out_specs=(vmem(), vmem()),
        compiler_params=params(),
        name="sum_middle",
    )(pieces, hidden, plan)


def gather_rows(spread):
    return pl.pallas_call(
        gather_kernel,
        out_shape=(
            shape(PLANE, BLOCK, QUARTER),
            shape(PLANE, TOKENS, dtype=jnp.float32),
            shape(PLANE, TOKENS, dtype=jnp.float32),
        ),
        in_specs=[vmem()],
        out_specs=(vmem(), vmem(), vmem()),
        scratch_shapes=[
            pltpu.VMEM((PLANE * BLOCK, TOKENS), jnp.bfloat16),
            pltpu.VMEM((TOKENS, QUARTER), jnp.bfloat16),
        ],
        compiler_params=params(),
        name="gather_rows",
    )(spread)


def hold(after, block):
    return pl.pallas_call(
        hold_kernel,
        out_shape=shape(*block.shape),
        in_specs=[anywhere()] * 2,
        out_specs=anywhere(),
        input_output_aliases={1: 0},
        compiler_params=params(),
        name="hold",
    )(after, block)


def combine_rows(target, gate, rows):
    return pl.pallas_call(
        combine_kernel,
        out_shape=shape(NZ, REQ, QUARTER),
        in_specs=[vmem(), vmem(), vmem()],
        out_specs=vmem(),
        scratch_shapes=[
            pltpu.VMEM((PLANE * BLOCK, TOKENS), jnp.bfloat16),
            pltpu.VMEM((PLANE * BLOCK, QUARTER), jnp.bfloat16),
        ],
        compiler_params=params(),
        name="combine_rows",
    )(target, gate, rows)


def half_scratch():
    return [
        pltpu.VMEM((3, 2 * EHQ, WIDTH), jnp.bfloat16),
        pltpu.VMEM((NX * BLOCK, 2 * EHQ), jnp.bfloat16),
        pltpu.SemaphoreType.DMA((3, 2)),
    ]


def first_half(rows, gain, blocks):
    return pl.pallas_call(
        first_half_kernel,
        out_shape=(shape(NX * BLOCK, WIDTH), shape(NX * BLOCK, WIDTH, dtype=jnp.float32)),
        in_specs=[vmem(), vmem()] + [anywhere()] * 2,
        out_specs=(vmem(), vmem()),
        scratch_shapes=half_scratch(),
        compiler_params=params(24),
        name="first_half",
    )(rows, gain, *blocks)


def second_half(normed, part, blocks):
    return pl.pallas_call(
        second_half_kernel,
        out_shape=shape(PLANE, BLOCK, QUARTER),
        in_specs=[vmem(), vmem()] + [anywhere()] * 2,
        out_specs=vmem(),
        scratch_shapes=half_scratch(),
        compiler_params=params(24),
        name="second_half",
    )(normed, part, *blocks)


def move_weights(blocks):
    even, odd = [], []
    for c in range(NC):
        for y in range(NY):
            even.append((c * NY + y, (1 - y // 2) * NY + 2 * c + y % 2))
            odd.append((c * NY + y, (y // 2) * NY + 2 * c + 1 - y % 2))
    return [lax.ppermute(block, ("c", "y"), to) for block, to in zip(blocks, (even, odd))]


def talker_plan(owners, section):
    own = lax.dynamic_slice_in_dim(owners, section * REQ, REQ)
    order = jnp.arange(REQ, dtype=jnp.int32)
    same = (own[:, None] == own[None, :]) & (order[:, None] > order[None, :])
    position = jnp.sum(same.astype(jnp.int32), axis=1)
    slot = jnp.where(own >= 0, own * HCAP + position, -1)
    send = (jnp.arange(SECTIONS * HCAP, dtype=jnp.int32)[:, None] == slot[None, :]).astype(
        jnp.bfloat16
    )
    counts = jnp.sum((owners == section).reshape(SECTIONS, REQ).astype(jnp.int32), axis=1)
    place = jnp.arange(SECTIONS, dtype=jnp.int32)
    offsets = jnp.sum(jnp.where(place[None, :] < place[:, None], counts[None, :], 0), axis=1)
    index = jnp.arange(HCAP, dtype=jnp.int32)
    put = jnp.where(index[None, :] < counts[:, None], offsets[:, None] + index[None, :], -1)
    put = put.reshape(SECTIONS * HCAP)
    take = (jnp.arange(SECTIONS * HCAP, dtype=jnp.int32)[:, None] == put[None, :]).astype(
        jnp.bfloat16
    )
    return send, take


def local(
    hidden_in,
    queries,
    new_kv,
    cache,
    lengths,
    out_weight,
    moe_gain,
    expert_ids,
    expert_gates,
    gate_up,
    down,
    owners,
):
    z, x, c, y = (lax.axis_index(name) for name in ("z", "x", "c", "y"))
    section = (z * NX + x) * NC + c
    plan = make_plan(expert_ids.T, expert_gates.T)
    pieces = attend(lengths, queries, new_kv, cache, out_weight)
    first = (y % 2).astype(jnp.int32).reshape(1)
    blocks = pick_weights(first, pieces, gate_up.transpose(0, 1, 3, 2), down)
    pieces = lax.all_to_all(pieces, "y", 0, 0, tiled=True)
    hidden = lax.dynamic_slice_in_dim(hidden_in, y * QUARTER, QUARTER, 1)
    message, middle = sum_middle(pieces, hidden, plan)
    even, odd = move_weights(blocks)
    swap = [(0, 1), (1, 0)]

    spread = lax.all_to_all(message, "z", 0, 0, tiled=True)
    send, target, gate = gather_rows(spread)
    rows = lax.all_to_all(send, ("x", "y"), 0, 0, tiled=True)
    odd = hold(rows, odd)
    even_swapped = lax.ppermute(even, "c", swap)
    odd_swapped = lax.ppermute(odd, "c", swap)
    normed, half = first_half(rows, moe_gain.reshape(1, WIDTH), (even, even_swapped))
    done = second_half(normed, half, (odd, odd_swapped))
    back = lax.all_to_all(done, ("x", "y"), 0, 0, tiled=True)
    part = combine_rows(target, gate, back)
    part = lax.all_to_all(part, "z", 0, 0, tiled=True)
    out = middle.astype(jnp.float32) + jnp.sum(part.astype(jnp.float32), axis=0)
    out = out.astype(jnp.bfloat16)

    send_pick, take_pick = talker_plan(owners, section)
    leaving = jnp.dot(send_pick, out, preferred_element_type=jnp.float32).astype(jnp.bfloat16)
    arrived = lax.all_to_all(
        leaving.reshape(SECTIONS, HCAP, QUARTER), ("z", "x", "c"), 0, 0, tiled=True
    )
    talker = jnp.dot(
        take_pick, arrived.reshape(SECTIONS * HCAP, QUARTER), preferred_element_type=jnp.float32
    ).astype(jnp.bfloat16)
    return (out, talker)


def solution(mesh):
    section = ("z", "x", "c")
    fine = Mesh(mesh.devices.reshape(NZ, NX, NC, NY), ("z", "x", "c", "y"))
    in_specs = (
        P(section, None),
        P(section, "y"),
        P(section, None, "y"),
        P(section, None, None, "y"),
        P(section),
        P("y", None),
        P(),
        P(section, None),
        P(section, None),
        P(section, None, None, "y"),
        P(section, "y", None),
        P(),
    )
    out_specs = (P(section, "y"), P(section, "y"))
    return jax.shard_map(local, mesh=fine, in_specs=in_specs, out_specs=out_specs, check_vma=False)
```

```python
import math

import jax
import jax.numpy as jnp
from jax import lax
from jax.experimental import pallas as pl
from jax.experimental.pallas import tpu as pltpu
from jax.sharding import Mesh
from jax.sharding import PartitionSpec as P

HD = 128
HCAP = 2
CAP = 10
NZ, NX, NC, NY = 8, 4, 2, 4
REQ = 64
SECTIONS = NZ * NX * NC
TOKENS = NZ * REQ
PLANE = NX * NY
BLOCK = NZ * CAP
ROWS = REQ // PLANE
QUARTER = 512
HEADS = 8
CTX = 96
CHUNK = 16
WIDTH = 2048
EHQ = 192


def select_blocks(first, gate_up, down, blocks, hold_ref, in_sems, out_sems):
    loads, stores = [], []
    for k, out in enumerate(blocks):
        index = first if k == 0 else 1 - first
        for part in range(3):
            source = gate_up.at[index, part] if part < 2 else down.at[index]
            loads.append(pltpu.make_async_copy(source, hold_ref.at[k, part], in_sems.at[k, part]))
            stores.append(
                pltpu.make_async_copy(hold_ref.at[k, part], out.at[part], out_sems.at[k, part])
            )
    return loads, stores


def attention_kernel(first_ref, lengths_ref, queries_ref, fresh_ref, cache, weight, *refs):
    gate_up, down, out_ref, even_ref, odd_ref, cache_ref, weight_ref, context_ref = refs[:8]
    hold_ref, cache_sem, weight_sem, in_sems, out_sems = refs[8:]
    blocks = (even_ref, odd_ref)
    picks, stores = select_blocks(first_ref[0], gate_up, down, blocks, hold_ref, in_sems, out_sems)
    loads = []
    for i in range(REQ // CHUNK):
        rows = pl.ds(i * CHUNK, CHUNK)
        loads.append(pltpu.make_async_copy(cache.at[rows], cache_ref.at[rows], cache_sem.at[i]))
    for copy in loads:
        copy.start()
    whole = pltpu.make_async_copy(weight, weight_ref, weight_sem)
    whole.start()
    for copy in picks:
        copy.start()
    scale = 1.0 / math.sqrt(HD)
    cell = lax.broadcasted_iota(jnp.int32, (HEADS, CTX), 1)
    for i in range(REQ // CHUNK):
        rows = slice(i * CHUNK, (i + 1) * CHUNK)
        heads = queries_ref[rows, :].astype(jnp.float32).reshape(CHUNK, HEADS, HD)
        fresh = fresh_ref[rows].astype(jnp.float32)
        loads[i].wait()
        keys, values = cache_ref[rows, 0], cache_ref[rows, 1]
        scores = lax.dot_general(
            heads.astype(jnp.bfloat16), keys, (((2,), (2,)), ((0,), (0,))), preferred_element_type=jnp.float32
        )
        scores = scores * scale
        scores = jnp.stack(
            [jnp.where(cell < lengths_ref[i * CHUNK + r], scores[r], -jnp.inf) for r in range(CHUNK)]
        )
        new = jnp.sum(heads * fresh[:, 0:1, :], axis=-1, keepdims=True) * scale
        top = jnp.maximum(jnp.max(scores, axis=-1, keepdims=True), new)
        mass = jnp.exp(scores - top)
        new = jnp.exp(new - top)
        total = jnp.sum(mass, axis=-1, keepdims=True) + new
        mass = (mass / total).astype(jnp.bfloat16)
        new = (new / total).astype(jnp.bfloat16).astype(jnp.float32)
        context = lax.dot_general(
            mass, values, (((2,), (1,)), ((0,), (0,))), preferred_element_type=jnp.float32
        ) + new * fresh[:, 1:2, :]
        context_ref[rows, :] = context.reshape(CHUNK, HEADS * HD).astype(jnp.bfloat16)
    for load, store in zip(picks, stores):
        load.wait()
        store.start()
    whole.wait()
    for y in range(NY):
        out_ref[y] = jnp.dot(
            context_ref[...], weight_ref[:, y * QUARTER : (y + 1) * QUARTER],
            preferred_element_type=jnp.float32,
        ).astype(jnp.bfloat16)
    for copy in stores:
        copy.wait()


def plan_kernel(ids_ref, gates_ref, even, odd, out_ref, *same):
    ids = jnp.concatenate([ids_ref[...], ids_ref[...]], axis=1)
    gates = jnp.concatenate([gates_ref[...], gates_ref[...]], axis=1)
    gates = gates / jnp.sum(gates, axis=0, keepdims=True)
    experts = NZ * PLANE
    expert = lax.broadcasted_iota(jnp.int32, (experts, 2 * REQ), 0)
    chosen = jnp.zeros((experts, 2 * REQ), jnp.float32)
    gate = jnp.zeros((experts, 2 * REQ), jnp.float32)
    for k in range(8):
        hit = ids[k : k + 1, :] == expert
        chosen = jnp.where(hit, 1.0, chosen)
        gate = jnp.where(hit, gates[k : k + 1, :], gate)
    earlier = lax.broadcasted_iota(jnp.int32, (2 * REQ, 2 * REQ), 0)
    token = lax.broadcasted_iota(jnp.int32, (2 * REQ, 2 * REQ), 1)
    token = jnp.where(token >= REQ, token - REQ, token)
    before = jnp.where(earlier < token, 1.0, 0.0).astype(jnp.bfloat16)
    rank = jnp.dot(chosen.astype(jnp.bfloat16), before, preferred_element_type=jnp.float32)
    slot = jnp.where(chosen > 0.0, rank, -1.0)
    first = lax.broadcasted_iota(jnp.int32, (experts, 2 * REQ), 1) < REQ
    both = jnp.where(first, slot, gate).astype(jnp.bfloat16)
    for z in range(NZ):
        out_ref[z] = both[z * PLANE : (z + 1) * PLANE, :]


def middle_kernel(pieces_ref, hidden_ref, plan_ref, message_ref, middle_ref):
    total = hidden_ref[...].astype(jnp.float32)
    for y in range(NY):
        total = total + pieces_ref[y].astype(jnp.float32)
    middle = total.astype(jnp.bfloat16)
    middle_ref[...] = middle
    for z in range(NZ):
        for k in range(ROWS):
            message_ref[z, :, k * QUARTER : (k + 1) * QUARTER] = middle[k * PLANE : (k + 1) * PLANE, :]
        message_ref[z, :, WIDTH:] = plan_ref[z]


def gather_kernel(spread_ref, out_ref, target_ref, gate_ref, pick_ref, rows_ref):
    low = lax.broadcasted_iota(jnp.int32, (PLANE, 2 * REQ), 1) < REQ
    for pair in range(NZ // 2):
        left = spread_ref[2 * pair, :, WIDTH:].astype(jnp.float32)
        right = spread_ref[2 * pair + 1, :, WIDTH:].astype(jnp.float32)
        both = jnp.concatenate([left[:, :REQ], right[:, :REQ]], axis=1)
        block = jnp.where(low, float(2 * pair * CAP), float((2 * pair + 1) * CAP))
        columns = slice(pair * 2 * REQ, (pair + 1) * 2 * REQ)
        target_ref[:, columns] = jnp.where(both >= 0.0, both + block, -1.0)
        gate_ref[:, columns] = jnp.concatenate([left[:, REQ:], right[:, REQ:]], axis=1)
    for z in range(NZ):
        for k in range(ROWS):
            first = z * REQ + k * PLANE
            rows_ref[first : first + PLANE, :] = spread_ref[z, :, k * QUARTER : (k + 1) * QUARTER]
    slot = lax.broadcasted_iota(jnp.int32, (BLOCK, TOKENS), 0).astype(jnp.float32)
    for e in range(PLANE):
        hit = target_ref[e : e + 1, :] == slot
        pick_ref[e * BLOCK : (e + 1) * BLOCK, :] = jnp.where(hit, 1.0, 0.0).astype(jnp.bfloat16)
    for e in range(0, PLANE, 4):
        rows = jnp.dot(
            pick_ref[e * BLOCK : (e + 4) * BLOCK, :],
            rows_ref[...],
            preferred_element_type=jnp.float32,
        ).astype(jnp.bfloat16)
        for k in range(4):
            out_ref[e + k] = rows[k * BLOCK : (k + 1) * BLOCK, :]


def hold_kernel(*refs):
    del refs


def combine_kernel(target_ref, gate_ref, rows_ref, out_ref, weight_ref, packed_ref):
    slot = lax.broadcasted_iota(jnp.int32, (BLOCK, TOKENS), 0).astype(jnp.float32)
    for e in range(PLANE):
        hit = target_ref[e : e + 1, :] == slot
        weight = jnp.where(hit, gate_ref[e : e + 1, :], 0.0)
        weight_ref[e * BLOCK : (e + 1) * BLOCK, :] = weight.astype(jnp.bfloat16)
        packed_ref[e * BLOCK : (e + 1) * BLOCK, :] = rows_ref[e]
    dims = (((0,), (0,)), ((), ()))
    total = lax.dot_general(
        weight_ref[...], packed_ref[...], dims, preferred_element_type=jnp.float32
    ).astype(jnp.bfloat16)
    for z in range(NZ):
        out_ref[z] = total[z * REQ : (z + 1) * REQ, :]


def load_block(block, weight_ref, sems):
    copies = [
        pltpu.make_async_copy(block.at[part], weight_ref.at[part], sems.at[part])
        for part in range(3)
    ]
    for copy in copies:
        copy.start()
    return copies


def activate(normed_ref, block_ref):
    dims = (((1,), (1,)), ((), ()))
    gate, up = (
        lax.dot_general(normed_ref[...], block_ref[k], dims, preferred_element_type=jnp.float32)
        for k in range(2)
    )
    return (gate / (1.0 + jnp.exp(-gate)) * up).astype(jnp.bfloat16)


def first_half_kernel(rows_ref, gain_ref, w0, w1, normed_ref, part_ref, w0_ref, w1_ref, sems):
    copies = load_block(w0, w0_ref, sems.at[0]), load_block(w1, w1_ref, sems.at[1])
    for x in range(NX):
        parts = [rows_ref[x * NY + y].astype(jnp.float32) for y in range(NY)]
        square = sum(jnp.sum(part * part, axis=-1, keepdims=True) for part in parts)
        scale = lax.rsqrt(square * (1.0 / WIDTH) + 1e-06)
        for y in range(NY):
            columns = slice(y * QUARTER, (y + 1) * QUARTER)
            normed_ref[x * BLOCK : (x + 1) * BLOCK, columns] = (
                parts[y] * scale * gain_ref[:, columns]
            ).astype(jnp.bfloat16)
    for copy in copies[0]:
        copy.wait()
    first = activate(normed_ref, w0_ref)
    for copy in copies[1]:
        copy.wait()
    second = activate(normed_ref, w1_ref)
    part_ref[...] = jnp.dot(first, w0_ref[2], preferred_element_type=jnp.float32) + jnp.dot(
        second, w1_ref[2], preferred_element_type=jnp.float32
    )


def second_half_kernel(normed_ref, part_ref, w2, w3_ref, out_ref, w2_ref, sems):
    copies = load_block(w2, w2_ref, sems)
    second = activate(normed_ref, w3_ref)
    for copy in copies:
        copy.wait()
    first = activate(normed_ref, w2_ref)
    for y in range(NY):
        columns = slice(y * QUARTER, (y + 1) * QUARTER)
        part = part_ref[:, columns] + jnp.dot(
            first, w2_ref[2, :, columns], preferred_element_type=jnp.float32
        )
        part = part + jnp.dot(second, w3_ref[2, :, columns], preferred_element_type=jnp.float32)
        part = part.astype(jnp.bfloat16)
        for x in range(NX):
            out_ref[x * NY + y] = part[x * BLOCK : (x + 1) * BLOCK, :]


def vmem():
    return pl.BlockSpec(memory_space=pltpu.VMEM)


def anywhere():
    return pl.BlockSpec(memory_space=pl.ANY)


def params(mib=16):
    return pltpu.CompilerParams(vmem_limit_bytes=mib * 1024 * 1024)


def shape(*dims, dtype=jnp.bfloat16):
    return jax.ShapeDtypeStruct(dims, dtype)


def attend(first, lengths, queries, fresh, cache, weight, gate_up, down):
    hbm = pl.BlockSpec(memory_space=pltpu.HBM)
    smem = pl.BlockSpec(memory_space=pltpu.SMEM)
    block = shape(3, EHQ, WIDTH)
    return pl.pallas_call(
        attention_kernel,
        out_shape=(shape(NY, REQ, QUARTER), block, block),
        in_specs=[smem, smem, vmem(), vmem(), hbm, hbm, hbm, hbm],
        out_specs=(vmem(), hbm, hbm),
        scratch_shapes=[
            pltpu.VMEM((REQ, 2, CTX, HD), jnp.bfloat16),
            pltpu.VMEM((HEADS * HD, WIDTH), jnp.bfloat16),
            pltpu.VMEM((REQ, HEADS * HD), jnp.bfloat16),
            pltpu.VMEM((2, 3, EHQ, WIDTH), jnp.bfloat16),
            pltpu.SemaphoreType.DMA((REQ // CHUNK,)),
            pltpu.SemaphoreType.DMA,
            pltpu.SemaphoreType.DMA((2, 3)),
            pltpu.SemaphoreType.DMA((2, 3)),
        ],
        compiler_params=params(60),
        name="attend",
    )(first, lengths, queries, fresh, cache, weight, gate_up, down)


def make_plan(ids, gates, blocks):
    return pl.pallas_call(
        plan_kernel,
        out_shape=(shape(NZ, PLANE, 2 * REQ), *[shape(*block.shape) for block in blocks]),
        in_specs=[vmem(), vmem()] + [anywhere()] * 2,
        out_specs=(vmem(), anywhere(), anywhere()),
        input_output_aliases={2: 1, 3: 2},
        compiler_params=params(),
        name="plan",
    )(ids, gates, *blocks)


def sum_middle(pieces, hidden, plan):
    return pl.pallas_call(
        middle_kernel,
        out_shape=(shape(NZ, PLANE, WIDTH + 2 * REQ), shape(REQ, QUARTER)),
        in_specs=[vmem()] * 3,
        out_specs=(vmem(), vmem()),
        compiler_params=params(),
        name="sum_middle",
    )(pieces, hidden, plan)


def gather_rows(spread):
    return pl.pallas_call(
        gather_kernel,
        out_shape=(
            shape(PLANE, BLOCK, QUARTER),
            shape(PLANE, TOKENS, dtype=jnp.float32),
            shape(PLANE, TOKENS, dtype=jnp.float32),
        ),
        in_specs=[vmem()],
        out_specs=(vmem(), vmem(), vmem()),
        scratch_shapes=[
            pltpu.VMEM((PLANE * BLOCK, TOKENS), jnp.bfloat16),
            pltpu.VMEM((TOKENS, QUARTER), jnp.bfloat16),
        ],
        compiler_params=params(),
        name="gather_rows",
    )(spread)


def hold(after, block):
    return pl.pallas_call(
        hold_kernel,
        out_shape=shape(*block.shape),
        in_specs=[anywhere()] * 2,
        out_specs=anywhere(),
        input_output_aliases={1: 0},
        compiler_params=params(),
        name="hold",
    )(after, block)


def combine_rows(target, gate, rows):
    return pl.pallas_call(
        combine_kernel,
        out_shape=shape(NZ, REQ, QUARTER),
        in_specs=[vmem(), vmem(), vmem()],
        out_specs=vmem(),
        scratch_shapes=[
            pltpu.VMEM((PLANE * BLOCK, TOKENS), jnp.bfloat16),
            pltpu.VMEM((PLANE * BLOCK, QUARTER), jnp.bfloat16),
        ],
        compiler_params=params(),
        name="combine_rows",
    )(target, gate, rows)


def first_half(rows, gain, blocks):
    return pl.pallas_call(
        first_half_kernel,
        out_shape=(shape(NX * BLOCK, WIDTH), shape(NX * BLOCK, WIDTH, dtype=jnp.float32)),
        in_specs=[vmem(), vmem(), anywhere(), anywhere()],
        out_specs=(vmem(), vmem()),
        scratch_shapes=[
            pltpu.VMEM((3, EHQ, WIDTH), jnp.bfloat16),
            pltpu.VMEM((3, EHQ, WIDTH), jnp.bfloat16),
            pltpu.SemaphoreType.DMA((2, 3)),
        ],
        compiler_params=params(24),
        name="first_half",
    )(rows, gain, *blocks)


def second_half(normed, part, blocks):
    return pl.pallas_call(
        second_half_kernel,
        out_shape=shape(PLANE, BLOCK, QUARTER),
        in_specs=[vmem(), vmem(), anywhere(), vmem()],
        out_specs=vmem(),
        scratch_shapes=[
            pltpu.VMEM((3, EHQ, WIDTH), jnp.bfloat16),
            pltpu.SemaphoreType.DMA((3,)),
        ],
        compiler_params=params(24),
        name="second_half",
    )(normed, part, *blocks)


def move_weights(blocks):
    even, odd = [], []
    for c in range(NC):
        for y in range(NY):
            even.append((c * NY + y, (1 - y // 2) * NY + 2 * c + y % 2))
            odd.append((c * NY + y, (y // 2) * NY + 2 * c + 1 - y % 2))
    return [lax.ppermute(block, ("c", "y"), to) for block, to in zip(blocks, (even, odd))]


def talker_plan(owners, section):
    own = lax.dynamic_slice_in_dim(owners, section * REQ, REQ)
    order = jnp.arange(REQ, dtype=jnp.int32)
    same = (own[:, None] == own[None, :]) & (order[:, None] > order[None, :])
    position = jnp.sum(same.astype(jnp.int32), axis=1)
    slot = jnp.where(own >= 0, own * HCAP + position, -1)
    send = (jnp.arange(SECTIONS * HCAP, dtype=jnp.int32)[:, None] == slot[None, :]).astype(
        jnp.bfloat16
    )
    counts = jnp.sum((owners == section).reshape(SECTIONS, REQ).astype(jnp.int32), axis=1)
    place = jnp.arange(SECTIONS, dtype=jnp.int32)
    offsets = jnp.sum(jnp.where(place[None, :] < place[:, None], counts[None, :], 0), axis=1)
    index = jnp.arange(HCAP, dtype=jnp.int32)
    put = jnp.where(index[None, :] < counts[:, None], offsets[:, None] + index[None, :], -1)
    put = put.reshape(SECTIONS * HCAP)
    take = (jnp.arange(SECTIONS * HCAP, dtype=jnp.int32)[:, None] == put[None, :]).astype(
        jnp.bfloat16
    )
    return send, take


def local(
    hidden_in,
    queries,
    new_kv,
    cache,
    lengths,
    out_weight,
    moe_gain,
    expert_ids,
    expert_gates,
    gate_up,
    down,
    owners,
):
    z, x, c, y = (lax.axis_index(name) for name in ("z", "x", "c", "y"))
    section = (z * NX + x) * NC + c
    first = (y % 2).astype(jnp.int32).reshape(1)
    pieces, *blocks = attend(
        first,
        lengths,
        queries,
        new_kv,
        cache,
        out_weight,
        gate_up.transpose(0, 1, 3, 2),
        down,
    )
    plan, *blocks = make_plan(expert_ids.T, expert_gates.T, blocks)
    pieces = lax.all_to_all(pieces, "y", 0, 0, tiled=True)
    hidden = lax.dynamic_slice_in_dim(hidden_in, y * QUARTER, QUARTER, 1)
    message, middle = sum_middle(pieces, hidden, plan)
    even, odd = move_weights(blocks)
    swap = [(0, 1), (1, 0)]

    spread = lax.all_to_all(message, "z", 0, 0, tiled=True)
    send, target, gate = gather_rows(spread)
    rows = lax.all_to_all(send, ("x", "y"), 0, 0, tiled=True)
    odd = hold(rows, odd)
    even_swapped = lax.ppermute(even, "c", swap)
    odd_swapped = lax.ppermute(odd, "c", swap)
    normed, half = first_half(rows, moe_gain.reshape(1, WIDTH), (even, even_swapped))
    done = second_half(normed, half, (odd, odd_swapped))
    back = lax.all_to_all(done, ("x", "y"), 0, 0, tiled=True)
    part = combine_rows(target, gate, back)
    part = lax.all_to_all(part, "z", 0, 0, tiled=True)
    out = middle.astype(jnp.float32) + jnp.sum(part.astype(jnp.float32), axis=0)
    out = out.astype(jnp.bfloat16)

    send_pick, take_pick = talker_plan(owners, section)
    leaving = jnp.dot(send_pick, out, preferred_element_type=jnp.float32).astype(jnp.bfloat16)
    arrived = lax.all_to_all(
        leaving.reshape(SECTIONS, HCAP, QUARTER), ("z", "x", "c"), 0, 0, tiled=True
    )
    talker = jnp.dot(
        take_pick, arrived.reshape(SECTIONS * HCAP, QUARTER), preferred_element_type=jnp.float32
    ).astype(jnp.bfloat16)
    return (out, talker)


def solution(mesh):
    section = ("z", "x", "c")
    fine = Mesh(mesh.devices.reshape(NZ, NX, NC, NY), ("z", "x", "c", "y"))
    in_specs = (
        P(section, None),
        P(section, "y"),
        P(section, None, "y"),
        P(section, None, None, "y"),
        P(section),
        P("y", None),
        P(),
        P(section, None),
        P(section, None),
        P(section, None, None, "y"),
        P(section, "y", None),
        P(),
    )
    out_specs = (P(section, "y"), P(section, "y"))
    return jax.shard_map(local, mesh=fine, in_specs=in_specs, out_specs=out_specs, check_vma=False)
```

```python
import math

import jax
import jax.numpy as jnp
from jax import lax
from jax.experimental import pallas as pl
from jax.experimental.pallas import tpu as pltpu
from jax.sharding import Mesh
from jax.sharding import PartitionSpec as P

HD = 128
HCAP = 2
CAP = 10
NZ, NX, NC, NY = 8, 4, 2, 4
REQ = 64
SECTIONS = NZ * NX * NC
TOKENS = NZ * REQ
PLANE = NX * NY
BLOCK = NZ * CAP
ROWS = REQ // PLANE
QUARTER = 512
HEADS = 8
CTX = 96
CHUNK = 16
WIDTH = 2048
EHQ = 192


def select_blocks(first, gate_up, down, blocks, hold_ref, in_sems, out_sems):
    loads, stores = [], []
    for k, out in enumerate(blocks):
        index = first if k == 0 else 1 - first
        for part in range(3):
            source = gate_up.at[index, part] if part < 2 else down.at[index]
            loads.append(pltpu.make_async_copy(source, hold_ref.at[k, part], in_sems.at[k, part]))
            stores.append(
                pltpu.make_async_copy(hold_ref.at[k, part], out.at[part], out_sems.at[k, part])
            )
    return loads, stores


def attention_kernel(first_ref, lengths_ref, queries_ref, fresh_ref, cache, weight, *refs):
    gate_up, down, out_ref, even_ref, odd_ref, cache_ref, weight_ref, context_ref = refs[:8]
    hold_ref, cache_sem, weight_sem, in_sems, out_sems = refs[8:]
    blocks = (even_ref, odd_ref)
    picks, stores = select_blocks(first_ref[0], gate_up, down, blocks, hold_ref, in_sems, out_sems)
    loads = []
    for i in range(REQ // CHUNK):
        rows = pl.ds(i * CHUNK, CHUNK)
        loads.append(pltpu.make_async_copy(cache.at[rows], cache_ref.at[rows], cache_sem.at[i]))
    for copy in loads:
        copy.start()
    whole = pltpu.make_async_copy(weight, weight_ref, weight_sem)
    whole.start()
    for copy in picks:
        copy.start()
    scale = 1.0 / math.sqrt(HD)
    cell = lax.broadcasted_iota(jnp.int32, (HEADS, CTX), 1)
    for i in range(REQ // CHUNK):
        rows = slice(i * CHUNK, (i + 1) * CHUNK)
        heads = queries_ref[rows, :].astype(jnp.float32).reshape(CHUNK, HEADS, HD)
        fresh = fresh_ref[rows].astype(jnp.float32)
        loads[i].wait()
        keys, values = cache_ref[rows, 0], cache_ref[rows, 1]
        scores = lax.dot_general(
            heads.astype(jnp.bfloat16), keys, (((2,), (2,)), ((0,), (0,))), preferred_element_type=jnp.float32
        )
        scores = scores * scale
        scores = jnp.stack(
            [jnp.where(cell < lengths_ref[i * CHUNK + r], scores[r], -jnp.inf) for r in range(CHUNK)]
        )
        new = jnp.sum(heads * fresh[:, 0:1, :], axis=-1, keepdims=True) * scale
        top = jnp.maximum(jnp.max(scores, axis=-1, keepdims=True), new)
        mass = jnp.exp(scores - top)
        new = jnp.exp(new - top)
        total = jnp.sum(mass, axis=-1, keepdims=True) + new
        mass = (mass / total).astype(jnp.bfloat16)
        new = (new / total).astype(jnp.bfloat16).astype(jnp.float32)
        context = lax.dot_general(
            mass, values, (((2,), (1,)), ((0,), (0,))), preferred_element_type=jnp.float32
        ) + new * fresh[:, 1:2, :]
        context_ref[rows, :] = context.reshape(CHUNK, HEADS * HD).astype(jnp.bfloat16)
        if i > 0:
            for k in (2 * i - 2, 2 * i - 1):
                picks[k].wait()
                stores[k].start()
    whole.wait()
    for y in range(NY):
        out_ref[y] = jnp.dot(
            context_ref[...], weight_ref[:, y * QUARTER : (y + 1) * QUARTER],
            preferred_element_type=jnp.float32,
        ).astype(jnp.bfloat16)
    for copy in stores:
        copy.wait()


def plan_kernel(ids_ref, gates_ref, even, odd, out_ref, *same):
    ids = jnp.concatenate([ids_ref[...], ids_ref[...]], axis=1)
    gates = jnp.concatenate([gates_ref[...], gates_ref[...]], axis=1)
    gates = gates / jnp.sum(gates, axis=0, keepdims=True)
    experts = NZ * PLANE
    expert = lax.broadcasted_iota(jnp.int32, (experts, 2 * REQ), 0)
    chosen = jnp.zeros((experts, 2 * REQ), jnp.float32)
    gate = jnp.zeros((experts, 2 * REQ), jnp.float32)
    for k in range(8):
        hit = ids[k : k + 1, :] == expert
        chosen = jnp.where(hit, 1.0, chosen)
        gate = jnp.where(hit, gates[k : k + 1, :], gate)
    earlier = lax.broadcasted_iota(jnp.int32, (2 * REQ, 2 * REQ), 0)
    token = lax.broadcasted_iota(jnp.int32, (2 * REQ, 2 * REQ), 1)
    token = jnp.where(token >= REQ, token - REQ, token)
    before = jnp.where(earlier < token, 1.0, 0.0).astype(jnp.bfloat16)
    rank = jnp.dot(chosen.astype(jnp.bfloat16), before, preferred_element_type=jnp.float32)
    slot = jnp.where(chosen > 0.0, rank, -1.0)
    first = lax.broadcasted_iota(jnp.int32, (experts, 2 * REQ), 1) < REQ
    both = jnp.where(first, slot, gate).astype(jnp.bfloat16)
    for z in range(NZ):
        out_ref[z] = both[z * PLANE : (z + 1) * PLANE, :]


def middle_kernel(pieces_ref, hidden_ref, plan_ref, message_ref, middle_ref):
    total = hidden_ref[...].astype(jnp.float32)
    for y in range(NY):
        total = total + pieces_ref[y].astype(jnp.float32)
    middle = total.astype(jnp.bfloat16)
    middle_ref[...] = middle
    for z in range(NZ):
        for k in range(ROWS):
            message_ref[z, :, k * QUARTER : (k + 1) * QUARTER] = middle[k * PLANE : (k + 1) * PLANE, :]
        message_ref[z, :, WIDTH:] = plan_ref[z]


def gather_kernel(spread_ref, out_ref, target_ref, gate_ref, pick_ref, rows_ref):
    low = lax.broadcasted_iota(jnp.int32, (PLANE, 2 * REQ), 1) < REQ
    for pair in range(NZ // 2):
        left = spread_ref[2 * pair, :, WIDTH:].astype(jnp.float32)
        right = spread_ref[2 * pair + 1, :, WIDTH:].astype(jnp.float32)
        both = jnp.concatenate([left[:, :REQ], right[:, :REQ]], axis=1)
        block = jnp.where(low, float(2 * pair * CAP), float((2 * pair + 1) * CAP))
        columns = slice(pair * 2 * REQ, (pair + 1) * 2 * REQ)
        target_ref[:, columns] = jnp.where(both >= 0.0, both + block, -1.0)
        gate_ref[:, columns] = jnp.concatenate([left[:, REQ:], right[:, REQ:]], axis=1)
    for z in range(NZ):
        for k in range(ROWS):
            first = z * REQ + k * PLANE
            rows_ref[first : first + PLANE, :] = spread_ref[z, :, k * QUARTER : (k + 1) * QUARTER]
    slot = lax.broadcasted_iota(jnp.int32, (BLOCK, TOKENS), 0).astype(jnp.float32)
    for e in range(PLANE):
        hit = target_ref[e : e + 1, :] == slot
        pick_ref[e * BLOCK : (e + 1) * BLOCK, :] = jnp.where(hit, 1.0, 0.0).astype(jnp.bfloat16)
    for e in range(0, PLANE, 4):
        rows = jnp.dot(
            pick_ref[e * BLOCK : (e + 4) * BLOCK, :],
            rows_ref[...],
            preferred_element_type=jnp.float32,
        ).astype(jnp.bfloat16)
        for k in range(4):
            out_ref[e + k] = rows[k * BLOCK : (k + 1) * BLOCK, :]


def hold_kernel(*refs):
    del refs


def combine_kernel(target_ref, gate_ref, rows_ref, out_ref, weight_ref, packed_ref):
    slot = lax.broadcasted_iota(jnp.int32, (BLOCK, TOKENS), 0).astype(jnp.float32)
    for e in range(PLANE):
        hit = target_ref[e : e + 1, :] == slot
        weight = jnp.where(hit, gate_ref[e : e + 1, :], 0.0)
        weight_ref[e * BLOCK : (e + 1) * BLOCK, :] = weight.astype(jnp.bfloat16)
        packed_ref[e * BLOCK : (e + 1) * BLOCK, :] = rows_ref[e]
    dims = (((0,), (0,)), ((), ()))
    total = lax.dot_general(
        weight_ref[...], packed_ref[...], dims, preferred_element_type=jnp.float32
    ).astype(jnp.bfloat16)
    for z in range(NZ):
        out_ref[z] = total[z * REQ : (z + 1) * REQ, :]


def load_block(block, weight_ref, sems):
    copies = [
        pltpu.make_async_copy(block.at[part], weight_ref.at[part], sems.at[part])
        for part in range(3)
    ]
    for copy in copies:
        copy.start()
    return copies


def activate(normed_ref, block_ref):
    dims = (((1,), (1,)), ((), ()))
    gate, up = (
        lax.dot_general(normed_ref[...], block_ref[k], dims, preferred_element_type=jnp.float32)
        for k in range(2)
    )
    return (gate / (1.0 + jnp.exp(-gate)) * up).astype(jnp.bfloat16)


def first_half_kernel(rows_ref, gain_ref, w0, w1, normed_ref, part_ref, w0_ref, w1_ref, sems):
    copies = load_block(w0, w0_ref, sems.at[0]), load_block(w1, w1_ref, sems.at[1])
    for x in range(NX):
        parts = [rows_ref[x * NY + y].astype(jnp.float32) for y in range(NY)]
        square = sum(jnp.sum(part * part, axis=-1, keepdims=True) for part in parts)
        scale = lax.rsqrt(square * (1.0 / WIDTH) + 1e-06)
        for y in range(NY):
            columns = slice(y * QUARTER, (y + 1) * QUARTER)
            normed_ref[x * BLOCK : (x + 1) * BLOCK, columns] = (
                parts[y] * scale * gain_ref[:, columns]
            ).astype(jnp.bfloat16)
    for copy in copies[0]:
        copy.wait()
    first = activate(normed_ref, w0_ref)
    for copy in copies[1]:
        copy.wait()
    second = activate(normed_ref, w1_ref)
    part_ref[...] = jnp.dot(first, w0_ref[2], preferred_element_type=jnp.float32) + jnp.dot(
        second, w1_ref[2], preferred_element_type=jnp.float32
    )


def second_half_kernel(normed_ref, part_ref, w2, w3_ref, out_ref, w2_ref, sems):
    copies = load_block(w2, w2_ref, sems)
    second = activate(normed_ref, w3_ref)
    for copy in copies:
        copy.wait()
    first = activate(normed_ref, w2_ref)
    for y in range(NY):
        columns = slice(y * QUARTER, (y + 1) * QUARTER)
        part = part_ref[:, columns] + jnp.dot(
            first, w2_ref[2, :, columns], preferred_element_type=jnp.float32
        )
        part = part + jnp.dot(second, w3_ref[2, :, columns], preferred_element_type=jnp.float32)
        part = part.astype(jnp.bfloat16)
        for x in range(NX):
            out_ref[x * NY + y] = part[x * BLOCK : (x + 1) * BLOCK, :]


def vmem():
    return pl.BlockSpec(memory_space=pltpu.VMEM)


def anywhere():
    return pl.BlockSpec(memory_space=pl.ANY)


def params(mib=16):
    return pltpu.CompilerParams(vmem_limit_bytes=mib * 1024 * 1024)


def shape(*dims, dtype=jnp.bfloat16):
    return jax.ShapeDtypeStruct(dims, dtype)


def attend(first, lengths, queries, fresh, cache, weight, gate_up, down):
    hbm = pl.BlockSpec(memory_space=pltpu.HBM)
    smem = pl.BlockSpec(memory_space=pltpu.SMEM)
    block = shape(3, EHQ, WIDTH)
    return pl.pallas_call(
        attention_kernel,
        out_shape=(shape(NY, REQ, QUARTER), block, block),
        in_specs=[smem, smem, vmem(), vmem(), hbm, hbm, hbm, hbm],
        out_specs=(vmem(), hbm, hbm),
        scratch_shapes=[
            pltpu.VMEM((REQ, 2, CTX, HD), jnp.bfloat16),
            pltpu.VMEM((HEADS * HD, WIDTH), jnp.bfloat16),
            pltpu.VMEM((REQ, HEADS * HD), jnp.bfloat16),
            pltpu.VMEM((2, 3, EHQ, WIDTH), jnp.bfloat16),
            pltpu.SemaphoreType.DMA((REQ // CHUNK,)),
            pltpu.SemaphoreType.DMA,
            pltpu.SemaphoreType.DMA((2, 3)),
            pltpu.SemaphoreType.DMA((2, 3)),
        ],
        compiler_params=params(60),
        name="attend",
    )(first, lengths, queries, fresh, cache, weight, gate_up, down)


def make_plan(ids, gates, blocks):
    return pl.pallas_call(
        plan_kernel,
        out_shape=(shape(NZ, PLANE, 2 * REQ), *[shape(*block.shape) for block in blocks]),
        in_specs=[vmem(), vmem()] + [anywhere()] * 2,
        out_specs=(vmem(), anywhere(), anywhere()),
        input_output_aliases={2: 1, 3: 2},
        compiler_params=params(),
        name="plan",
    )(ids, gates, *blocks)


def sum_middle(pieces, hidden, plan):
    return pl.pallas_call(
        middle_kernel,
        out_shape=(shape(NZ, PLANE, WIDTH + 2 * REQ), shape(REQ, QUARTER)),
        in_specs=[vmem()] * 3,
        out_specs=(vmem(), vmem()),
        compiler_params=params(),
        name="sum_middle",
    )(pieces, hidden, plan)


def gather_rows(spread):
    return pl.pallas_call(
        gather_kernel,
        out_shape=(
            shape(PLANE, BLOCK, QUARTER),
            shape(PLANE, TOKENS, dtype=jnp.float32),
            shape(PLANE, TOKENS, dtype=jnp.float32),
        ),
        in_specs=[vmem()],
        out_specs=(vmem(), vmem(), vmem()),
        scratch_shapes=[
            pltpu.VMEM((PLANE * BLOCK, TOKENS), jnp.bfloat16),
            pltpu.VMEM((TOKENS, QUARTER), jnp.bfloat16),
        ],
        compiler_params=params(),
        name="gather_rows",
    )(spread)


def hold(after, block):
    return pl.pallas_call(
        hold_kernel,
        out_shape=shape(*block.shape),
        in_specs=[anywhere()] * 2,
        out_specs=anywhere(),
        input_output_aliases={1: 0},
        compiler_params=params(),
        name="hold",
    )(after, block)


def combine_rows(target, gate, rows):
    return pl.pallas_call(
        combine_kernel,
        out_shape=shape(NZ, REQ, QUARTER),
        in_specs=[vmem(), vmem(), vmem()],
        out_specs=vmem(),
        scratch_shapes=[
            pltpu.VMEM((PLANE * BLOCK, TOKENS), jnp.bfloat16),
            pltpu.VMEM((PLANE * BLOCK, QUARTER), jnp.bfloat16),
        ],
        compiler_params=params(),
        name="combine_rows",
    )(target, gate, rows)


def first_half(rows, gain, blocks):
    return pl.pallas_call(
        first_half_kernel,
        out_shape=(shape(NX * BLOCK, WIDTH), shape(NX * BLOCK, WIDTH, dtype=jnp.float32)),
        in_specs=[vmem(), vmem(), anywhere(), anywhere()],
        out_specs=(vmem(), vmem()),
        scratch_shapes=[
            pltpu.VMEM((3, EHQ, WIDTH), jnp.bfloat16),
            pltpu.VMEM((3, EHQ, WIDTH), jnp.bfloat16),
            pltpu.SemaphoreType.DMA((2, 3)),
        ],
        compiler_params=params(24),
        name="first_half",
    )(rows, gain, *blocks)


def second_half(normed, part, blocks):
    return pl.pallas_call(
        second_half_kernel,
        out_shape=shape(PLANE, BLOCK, QUARTER),
        in_specs=[vmem(), vmem(), anywhere(), vmem()],
        out_specs=vmem(),
        scratch_shapes=[
            pltpu.VMEM((3, EHQ, WIDTH), jnp.bfloat16),
            pltpu.SemaphoreType.DMA((3,)),
        ],
        compiler_params=params(24),
        name="second_half",
    )(normed, part, *blocks)


def move_weights(blocks):
    even, odd = [], []
    for c in range(NC):
        for y in range(NY):
            even.append((c * NY + y, (1 - y // 2) * NY + 2 * c + y % 2))
            odd.append((c * NY + y, (y // 2) * NY + 2 * c + 1 - y % 2))
    return [lax.ppermute(block, ("c", "y"), to) for block, to in zip(blocks, (even, odd))]


def talker_plan(owners, section):
    own = lax.dynamic_slice_in_dim(owners, section * REQ, REQ)
    order = jnp.arange(REQ, dtype=jnp.int32)
    same = (own[:, None] == own[None, :]) & (order[:, None] > order[None, :])
    position = jnp.sum(same.astype(jnp.int32), axis=1)
    slot = jnp.where(own >= 0, own * HCAP + position, -1)
    send = (jnp.arange(SECTIONS * HCAP, dtype=jnp.int32)[:, None] == slot[None, :]).astype(
        jnp.bfloat16
    )
    counts = jnp.sum((owners == section).reshape(SECTIONS, REQ).astype(jnp.int32), axis=1)
    place = jnp.arange(SECTIONS, dtype=jnp.int32)
    offsets = jnp.sum(jnp.where(place[None, :] < place[:, None], counts[None, :], 0), axis=1)
    index = jnp.arange(HCAP, dtype=jnp.int32)
    put = jnp.where(index[None, :] < counts[:, None], offsets[:, None] + index[None, :], -1)
    put = put.reshape(SECTIONS * HCAP)
    take = (jnp.arange(SECTIONS * HCAP, dtype=jnp.int32)[:, None] == put[None, :]).astype(
        jnp.bfloat16
    )
    return send, take


def local(
    hidden_in,
    queries,
    new_kv,
    cache,
    lengths,
    out_weight,
    moe_gain,
    expert_ids,
    expert_gates,
    gate_up,
    down,
    owners,
):
    z, x, c, y = (lax.axis_index(name) for name in ("z", "x", "c", "y"))
    section = (z * NX + x) * NC + c
    first = (y % 2).astype(jnp.int32).reshape(1)
    pieces, *blocks = attend(
        first,
        lengths,
        queries,
        new_kv,
        cache,
        out_weight,
        gate_up.transpose(0, 1, 3, 2),
        down,
    )
    plan, *blocks = make_plan(expert_ids.T, expert_gates.T, blocks)
    pieces = lax.all_to_all(pieces, "y", 0, 0, tiled=True)
    hidden = lax.dynamic_slice_in_dim(hidden_in, y * QUARTER, QUARTER, 1)
    message, middle = sum_middle(pieces, hidden, plan)
    even, odd = move_weights(blocks)
    swap = [(0, 1), (1, 0)]

    spread = lax.all_to_all(message, "z", 0, 0, tiled=True)
    send, target, gate = gather_rows(spread)
    rows = lax.all_to_all(send, ("x", "y"), 0, 0, tiled=True)
    odd = hold(rows, odd)
    even_swapped = lax.ppermute(even, "c", swap)
    odd_swapped = lax.ppermute(odd, "c", swap)
    normed, half = first_half(rows, moe_gain.reshape(1, WIDTH), (even, odd))
    done = second_half(normed, half, (odd_swapped, even_swapped))
    back = lax.all_to_all(done, ("x", "y"), 0, 0, tiled=True)
    part = combine_rows(target, gate, back)
    part = lax.all_to_all(part, "z", 0, 0, tiled=True)
    out = middle.astype(jnp.float32) + jnp.sum(part.astype(jnp.float32), axis=0)
    out = out.astype(jnp.bfloat16)

    send_pick, take_pick = talker_plan(owners, section)
    leaving = jnp.dot(send_pick, out, preferred_element_type=jnp.float32).astype(jnp.bfloat16)
    arrived = lax.all_to_all(
        leaving.reshape(SECTIONS, HCAP, QUARTER), ("z", "x", "c"), 0, 0, tiled=True
    )
    talker = jnp.dot(
        take_pick, arrived.reshape(SECTIONS * HCAP, QUARTER), preferred_element_type=jnp.float32
    ).astype(jnp.bfloat16)
    return (out, talker)


def solution(mesh):
    section = ("z", "x", "c")
    fine = Mesh(mesh.devices.reshape(NZ, NX, NC, NY), ("z", "x", "c", "y"))
    in_specs = (
        P(section, None),
        P(section, "y"),
        P(section, None, "y"),
        P(section, None, None, "y"),
        P(section),
        P("y", None),
        P(),
        P(section, None),
        P(section, None),
        P(section, None, None, "y"),
        P(section, "y", None),
        P(),
    )
    out_specs = (P(section, "y"), P(section, "y"))
    return jax.shard_map(local, mesh=fine, in_specs=in_specs, out_specs=out_specs, check_vma=False)
```

```python
import math

import jax
import jax.numpy as jnp
from jax import lax
from jax.experimental import pallas as pl
from jax.experimental.pallas import tpu as pltpu
from jax.sharding import Mesh
from jax.sharding import PartitionSpec as P

HD = 128
HCAP = 2
CAP = 10
NZ, NX, NC, NY = 8, 4, 2, 4
REQ = 64
SECTIONS = NZ * NX * NC
TOKENS = NZ * REQ
PLANE = NX * NY
BLOCK = NZ * CAP
ROWS = REQ // PLANE
QUARTER = 512
HEADS = 8
CTX = 96
CHUNK = 16
WIDTH = 2048
EHQ = 192


def select_blocks(first, gate_up, down, blocks, hold_ref, in_sems, out_sems):
    loads, stores = [], []
    for k, out in enumerate(blocks):
        index = first if k == 0 else 1 - first
        for part in range(3):
            source = gate_up.at[index, part] if part < 2 else down.at[index]
            loads.append(pltpu.make_async_copy(source, hold_ref.at[k, part], in_sems.at[k, part]))
            stores.append(
                pltpu.make_async_copy(hold_ref.at[k, part], out.at[part], out_sems.at[k, part])
            )
    return loads, stores


def attention_kernel(first_ref, lengths_ref, queries_ref, fresh_ref, cache, weight, *refs):
    gate_up, down, out_ref, even_ref, odd_ref, cache_ref, weight_ref, context_ref = refs[:8]
    hold_ref, cache_sem, weight_sem, in_sems, out_sems = refs[8:]
    blocks = (even_ref, odd_ref)
    picks, stores = select_blocks(first_ref[0], gate_up, down, blocks, hold_ref, in_sems, out_sems)
    loads = []
    for i in range(REQ // CHUNK):
        rows = pl.ds(i * CHUNK, CHUNK)
        loads.append(pltpu.make_async_copy(cache.at[rows], cache_ref.at[rows], cache_sem.at[i]))
    for copy in loads:
        copy.start()
    whole = pltpu.make_async_copy(weight, weight_ref, weight_sem)
    for copy in picks:
        copy.start()
    whole.start()
    scale = 1.0 / math.sqrt(HD)
    cell = lax.broadcasted_iota(jnp.int32, (HEADS, CTX), 1)
    for i in range(REQ // CHUNK):
        rows = slice(i * CHUNK, (i + 1) * CHUNK)
        heads = queries_ref[rows, :].astype(jnp.float32).reshape(CHUNK, HEADS, HD)
        fresh = fresh_ref[rows].astype(jnp.float32)
        loads[i].wait()
        keys, values = cache_ref[rows, 0], cache_ref[rows, 1]
        scores = lax.dot_general(
            heads.astype(jnp.bfloat16), keys, (((2,), (2,)), ((0,), (0,))), preferred_element_type=jnp.float32
        )
        scores = scores * scale
        scores = jnp.stack(
            [jnp.where(cell < lengths_ref[i * CHUNK + r], scores[r], -jnp.inf) for r in range(CHUNK)]
        )
        new = jnp.sum(heads * fresh[:, 0:1, :], axis=-1, keepdims=True) * scale
        top = jnp.maximum(jnp.max(scores, axis=-1, keepdims=True), new)
        mass = jnp.exp(scores - top)
        new = jnp.exp(new - top)
        total = jnp.sum(mass, axis=-1, keepdims=True) + new
        mass = (mass / total).astype(jnp.bfloat16)
        new = (new / total).astype(jnp.bfloat16).astype(jnp.float32)
        context = lax.dot_general(
            mass, values, (((2,), (1,)), ((0,), (0,))), preferred_element_type=jnp.float32
        ) + new * fresh[:, 1:2, :]
        context_ref[rows, :] = context.reshape(CHUNK, HEADS * HD).astype(jnp.bfloat16)
        if i == 2:
            for load, store in zip(picks, stores):
                load.wait()
                store.start()
    whole.wait()
    for y in range(NY):
        out_ref[y] = jnp.dot(
            context_ref[...], weight_ref[:, y * QUARTER : (y + 1) * QUARTER],
            preferred_element_type=jnp.float32,
        ).astype(jnp.bfloat16)
    for copy in stores:
        copy.wait()


def plan_kernel(ids_ref, gates_ref, even, odd, out_ref, *same):
    ids = jnp.concatenate([ids_ref[...], ids_ref[...]], axis=1)
    gates = jnp.concatenate([gates_ref[...], gates_ref[...]], axis=1)
    gates = gates / jnp.sum(gates, axis=0, keepdims=True)
    experts = NZ * PLANE
    expert = lax.broadcasted_iota(jnp.int32, (experts, 2 * REQ), 0)
    chosen = jnp.zeros((experts, 2 * REQ), jnp.float32)
    gate = jnp.zeros((experts, 2 * REQ), jnp.float32)
    for k in range(8):
        hit = ids[k : k + 1, :] == expert
        chosen = jnp.where(hit, 1.0, chosen)
        gate = jnp.where(hit, gates[k : k + 1, :], gate)
    earlier = lax.broadcasted_iota(jnp.int32, (2 * REQ, 2 * REQ), 0)
    token = lax.broadcasted_iota(jnp.int32, (2 * REQ, 2 * REQ), 1)
    token = jnp.where(token >= REQ, token - REQ, token)
    before = jnp.where(earlier < token, 1.0, 0.0).astype(jnp.bfloat16)
    rank = jnp.dot(chosen.astype(jnp.bfloat16), before, preferred_element_type=jnp.float32)
    slot = jnp.where(chosen > 0.0, rank, -1.0)
    first = lax.broadcasted_iota(jnp.int32, (experts, 2 * REQ), 1) < REQ
    both = jnp.where(first, slot, gate).astype(jnp.bfloat16)
    for z in range(NZ):
        out_ref[z] = both[z * PLANE : (z + 1) * PLANE, :]


def middle_kernel(pieces_ref, hidden_ref, plan_ref, message_ref, middle_ref):
    total = hidden_ref[...].astype(jnp.float32)
    for y in range(NY):
        total = total + pieces_ref[y].astype(jnp.float32)
    middle = total.astype(jnp.bfloat16)
    middle_ref[...] = middle
    for z in range(NZ):
        for k in range(ROWS):
            message_ref[z, :, k * QUARTER : (k + 1) * QUARTER] = middle[k * PLANE : (k + 1) * PLANE, :]
        message_ref[z, :, WIDTH:] = plan_ref[z]


def gather_kernel(spread_ref, out_ref, target_ref, gate_ref, pick_ref, rows_ref):
    low = lax.broadcasted_iota(jnp.int32, (PLANE, 2 * REQ), 1) < REQ
    for pair in range(NZ // 2):
        left = spread_ref[2 * pair, :, WIDTH:].astype(jnp.float32)
        right = spread_ref[2 * pair + 1, :, WIDTH:].astype(jnp.float32)
        both = jnp.concatenate([left[:, :REQ], right[:, :REQ]], axis=1)
        block = jnp.where(low, float(2 * pair * CAP), float((2 * pair + 1) * CAP))
        columns = slice(pair * 2 * REQ, (pair + 1) * 2 * REQ)
        target_ref[:, columns] = jnp.where(both >= 0.0, both + block, -1.0)
        gate_ref[:, columns] = jnp.concatenate([left[:, REQ:], right[:, REQ:]], axis=1)
    for z in range(NZ):
        for k in range(ROWS):
            first = z * REQ + k * PLANE
            rows_ref[first : first + PLANE, :] = spread_ref[z, :, k * QUARTER : (k + 1) * QUARTER]
    slot = lax.broadcasted_iota(jnp.int32, (BLOCK, TOKENS), 0).astype(jnp.float32)
    for e in range(PLANE):
        hit = target_ref[e : e + 1, :] == slot
        pick_ref[e * BLOCK : (e + 1) * BLOCK, :] = jnp.where(hit, 1.0, 0.0).astype(jnp.bfloat16)
    for e in range(0, PLANE, 4):
        rows = jnp.dot(
            pick_ref[e * BLOCK : (e + 4) * BLOCK, :],
            rows_ref[...],
            preferred_element_type=jnp.float32,
        ).astype(jnp.bfloat16)
        for k in range(4):
            out_ref[e + k] = rows[k * BLOCK : (k + 1) * BLOCK, :]


def hold_kernel(*refs):
    del refs


def combine_kernel(target_ref, gate_ref, rows_ref, out_ref, weight_ref, packed_ref):
    slot = lax.broadcasted_iota(jnp.int32, (BLOCK, TOKENS), 0).astype(jnp.float32)
    for e in range(PLANE):
        hit = target_ref[e : e + 1, :] == slot
        weight = jnp.where(hit, gate_ref[e : e + 1, :], 0.0)
        weight_ref[e * BLOCK : (e + 1) * BLOCK, :] = weight.astype(jnp.bfloat16)
        packed_ref[e * BLOCK : (e + 1) * BLOCK, :] = rows_ref[e]
    dims = (((0,), (0,)), ((), ()))
    total = lax.dot_general(
        weight_ref[...], packed_ref[...], dims, preferred_element_type=jnp.float32
    ).astype(jnp.bfloat16)
    for z in range(NZ):
        out_ref[z] = total[z * REQ : (z + 1) * REQ, :]


def load_block(block, weight_ref, sems):
    copies = [
        pltpu.make_async_copy(block.at[part], weight_ref.at[part], sems.at[part])
        for part in range(3)
    ]
    for copy in copies:
        copy.start()
    return copies


def activate(normed_ref, block_ref):
    dims = (((1,), (1,)), ((), ()))
    gate, up = (
        lax.dot_general(normed_ref[...], block_ref[k], dims, preferred_element_type=jnp.float32)
        for k in range(2)
    )
    return (gate / (1.0 + jnp.exp(-gate)) * up).astype(jnp.bfloat16)


def first_half_kernel(rows_ref, gain_ref, w0, w1, normed_ref, part_ref, w0_ref, w1_ref, sems):
    copies = load_block(w0, w0_ref, sems.at[0]), load_block(w1, w1_ref, sems.at[1])
    for x in range(NX):
        parts = [rows_ref[x * NY + y].astype(jnp.float32) for y in range(NY)]
        square = sum(jnp.sum(part * part, axis=-1, keepdims=True) for part in parts)
        scale = lax.rsqrt(square * (1.0 / WIDTH) + 1e-06)
        for y in range(NY):
            columns = slice(y * QUARTER, (y + 1) * QUARTER)
            normed_ref[x * BLOCK : (x + 1) * BLOCK, columns] = (
                parts[y] * scale * gain_ref[:, columns]
            ).astype(jnp.bfloat16)
    for copy in copies[0]:
        copy.wait()
    first = activate(normed_ref, w0_ref)
    for copy in copies[1]:
        copy.wait()
    second = activate(normed_ref, w1_ref)
    part_ref[...] = jnp.dot(first, w0_ref[2], preferred_element_type=jnp.float32) + jnp.dot(
        second, w1_ref[2], preferred_element_type=jnp.float32
    )


def second_half_kernel(normed_ref, part_ref, w2, w3_ref, out_ref, w2_ref, sems):
    copies = load_block(w2, w2_ref, sems)
    second = activate(normed_ref, w3_ref)
    for copy in copies:
        copy.wait()
    first = activate(normed_ref, w2_ref)
    for y in range(NY):
        columns = slice(y * QUARTER, (y + 1) * QUARTER)
        part = part_ref[:, columns] + jnp.dot(
            first, w2_ref[2, :, columns], preferred_element_type=jnp.float32
        )
        part = part + jnp.dot(second, w3_ref[2, :, columns], preferred_element_type=jnp.float32)
        part = part.astype(jnp.bfloat16)
        for x in range(NX):
            out_ref[x * NY + y] = part[x * BLOCK : (x + 1) * BLOCK, :]


def vmem():
    return pl.BlockSpec(memory_space=pltpu.VMEM)


def anywhere():
    return pl.BlockSpec(memory_space=pl.ANY)


def params(mib=16):
    return pltpu.CompilerParams(vmem_limit_bytes=mib * 1024 * 1024)


def shape(*dims, dtype=jnp.bfloat16):
    return jax.ShapeDtypeStruct(dims, dtype)


def attend(first, lengths, queries, fresh, cache, weight, gate_up, down):
    hbm = pl.BlockSpec(memory_space=pltpu.HBM)
    smem = pl.BlockSpec(memory_space=pltpu.SMEM)
    block = shape(3, EHQ, WIDTH)
    return pl.pallas_call(
        attention_kernel,
        out_shape=(shape(NY, REQ, QUARTER), block, block),
        in_specs=[smem, smem, vmem(), vmem(), hbm, hbm, hbm, hbm],
        out_specs=(vmem(), hbm, hbm),
        scratch_shapes=[
            pltpu.VMEM((REQ, 2, CTX, HD), jnp.bfloat16),
            pltpu.VMEM((HEADS * HD, WIDTH), jnp.bfloat16),
            pltpu.VMEM((REQ, HEADS * HD), jnp.bfloat16),
            pltpu.VMEM((2, 3, EHQ, WIDTH), jnp.bfloat16),
            pltpu.SemaphoreType.DMA((REQ // CHUNK,)),
            pltpu.SemaphoreType.DMA,
            pltpu.SemaphoreType.DMA((2, 3)),
            pltpu.SemaphoreType.DMA((2, 3)),
        ],
        compiler_params=params(60),
        name="attend",
    )(first, lengths, queries, fresh, cache, weight, gate_up, down)


def make_plan(ids, gates, blocks):
    return pl.pallas_call(
        plan_kernel,
        out_shape=(shape(NZ, PLANE, 2 * REQ), *[shape(*block.shape) for block in blocks]),
        in_specs=[vmem(), vmem()] + [anywhere()] * 2,
        out_specs=(vmem(), anywhere(), anywhere()),
        input_output_aliases={2: 1, 3: 2},
        compiler_params=params(),
        name="plan",
    )(ids, gates, *blocks)


def sum_middle(pieces, hidden, plan):
    return pl.pallas_call(
        middle_kernel,
        out_shape=(shape(NZ, PLANE, WIDTH + 2 * REQ), shape(REQ, QUARTER)),
        in_specs=[vmem()] * 3,
        out_specs=(vmem(), vmem()),
        compiler_params=params(),
        name="sum_middle",
    )(pieces, hidden, plan)


def gather_rows(spread):
    return pl.pallas_call(
        gather_kernel,
        out_shape=(
            shape(PLANE, BLOCK, QUARTER),
            shape(PLANE, TOKENS, dtype=jnp.float32),
            shape(PLANE, TOKENS, dtype=jnp.float32),
        ),
        in_specs=[vmem()],
        out_specs=(vmem(), vmem(), vmem()),
        scratch_shapes=[
            pltpu.VMEM((PLANE * BLOCK, TOKENS), jnp.bfloat16),
            pltpu.VMEM((TOKENS, QUARTER), jnp.bfloat16),
        ],
        compiler_params=params(),
        name="gather_rows",
    )(spread)


def hold(after, block):
    return pl.pallas_call(
        hold_kernel,
        out_shape=shape(*block.shape),
        in_specs=[anywhere()] * 2,
        out_specs=anywhere(),
        input_output_aliases={1: 0},
        compiler_params=params(),
        name="hold",
    )(after, block)


def combine_rows(target, gate, rows):
    return pl.pallas_call(
        combine_kernel,
        out_shape=shape(NZ, REQ, QUARTER),
        in_specs=[vmem(), vmem(), vmem()],
        out_specs=vmem(),
        scratch_shapes=[
            pltpu.VMEM((PLANE * BLOCK, TOKENS), jnp.bfloat16),
            pltpu.VMEM((PLANE * BLOCK, QUARTER), jnp.bfloat16),
        ],
        compiler_params=params(),
        name="combine_rows",
    )(target, gate, rows)


def first_half(rows, gain, blocks):
    return pl.pallas_call(
        first_half_kernel,
        out_shape=(shape(NX * BLOCK, WIDTH), shape(NX * BLOCK, WIDTH, dtype=jnp.float32)),
        in_specs=[vmem(), vmem(), anywhere(), anywhere()],
        out_specs=(vmem(), vmem()),
        scratch_shapes=[
            pltpu.VMEM((3, EHQ, WIDTH), jnp.bfloat16),
            pltpu.VMEM((3, EHQ, WIDTH), jnp.bfloat16),
            pltpu.SemaphoreType.DMA((2, 3)),
        ],
        compiler_params=params(24),
        name="first_half",
    )(rows, gain, *blocks)


def second_half(normed, part, blocks):
    return pl.pallas_call(
        second_half_kernel,
        out_shape=shape(PLANE, BLOCK, QUARTER),
        in_specs=[vmem(), vmem(), anywhere(), vmem()],
        out_specs=vmem(),
        scratch_shapes=[
            pltpu.VMEM((3, EHQ, WIDTH), jnp.bfloat16),
            pltpu.SemaphoreType.DMA((3,)),
        ],
        compiler_params=params(24),
        name="second_half",
    )(normed, part, *blocks)


def move_weights(blocks):
    even, odd = [], []
    for c in range(NC):
        for y in range(NY):
            even.append((c * NY + y, (1 - y // 2) * NY + 2 * c + y % 2))
            odd.append((c * NY + y, (y // 2) * NY + 2 * c + 1 - y % 2))
    return [lax.ppermute(block, ("c", "y"), to) for block, to in zip(blocks, (even, odd))]


def talker_plan(owners, section):
    own = lax.dynamic_slice_in_dim(owners, section * REQ, REQ)
    order = jnp.arange(REQ, dtype=jnp.int32)
    same = (own[:, None] == own[None, :]) & (order[:, None] > order[None, :])
    position = jnp.sum(same.astype(jnp.int32), axis=1)
    slot = jnp.where(own >= 0, own * HCAP + position, -1)
    send = (jnp.arange(SECTIONS * HCAP, dtype=jnp.int32)[:, None] == slot[None, :]).astype(
        jnp.bfloat16
    )
    counts = jnp.sum((owners == section).reshape(SECTIONS, REQ).astype(jnp.int32), axis=1)
    place = jnp.arange(SECTIONS, dtype=jnp.int32)
    offsets = jnp.sum(jnp.where(place[None, :] < place[:, None], counts[None, :], 0), axis=1)
    index = jnp.arange(HCAP, dtype=jnp.int32)
    put = jnp.where(index[None, :] < counts[:, None], offsets[:, None] + index[None, :], -1)
    put = put.reshape(SECTIONS * HCAP)
    take = (jnp.arange(SECTIONS * HCAP, dtype=jnp.int32)[:, None] == put[None, :]).astype(
        jnp.bfloat16
    )
    return send, take


def local(
    hidden_in,
    queries,
    new_kv,
    cache,
    lengths,
    out_weight,
    moe_gain,
    expert_ids,
    expert_gates,
    gate_up,
    down,
    owners,
):
    z, x, c, y = (lax.axis_index(name) for name in ("z", "x", "c", "y"))
    section = (z * NX + x) * NC + c
    first = (y % 2).astype(jnp.int32).reshape(1)
    pieces, *blocks = attend(
        first,
        lengths,
        queries,
        new_kv,
        cache,
        out_weight,
        gate_up.transpose(0, 1, 3, 2),
        down,
    )
    plan, *blocks = make_plan(expert_ids.T, expert_gates.T, blocks)
    pieces = lax.all_to_all(pieces, "y", 0, 0, tiled=True)
    hidden = lax.dynamic_slice_in_dim(hidden_in, y * QUARTER, QUARTER, 1)
    message, middle = sum_middle(pieces, hidden, plan)
    even, odd = move_weights(blocks)
    swap = [(0, 1), (1, 0)]

    spread = lax.all_to_all(message, "z", 0, 0, tiled=True)
    send, target, gate = gather_rows(spread)
    rows = lax.all_to_all(send, ("x", "y"), 0, 0, tiled=True)
    odd = hold(rows, odd)
    even_swapped = lax.ppermute(even, "c", swap)
    odd_swapped = lax.ppermute(odd, "c", swap)
    normed, half = first_half(rows, moe_gain.reshape(1, WIDTH), (even, even_swapped))
    done = second_half(normed, half, (odd, odd_swapped))
    back = lax.all_to_all(done, ("x", "y"), 0, 0, tiled=True)
    part = combine_rows(target, gate, back)
    part = lax.all_to_all(part, "z", 0, 0, tiled=True)
    out = middle.astype(jnp.float32) + jnp.sum(part.astype(jnp.float32), axis=0)
    out = out.astype(jnp.bfloat16)

    send_pick, take_pick = talker_plan(owners, section)
    leaving = jnp.dot(send_pick, out, preferred_element_type=jnp.float32).astype(jnp.bfloat16)
    arrived = lax.all_to_all(
        leaving.reshape(SECTIONS, HCAP, QUARTER), ("z", "x", "c"), 0, 0, tiled=True
    )
    talker = jnp.dot(
        take_pick, arrived.reshape(SECTIONS * HCAP, QUARTER), preferred_element_type=jnp.float32
    ).astype(jnp.bfloat16)
    return (out, talker)


def solution(mesh):
    section = ("z", "x", "c")
    fine = Mesh(mesh.devices.reshape(NZ, NX, NC, NY), ("z", "x", "c", "y"))
    in_specs = (
        P(section, None),
        P(section, "y"),
        P(section, None, "y"),
        P(section, None, None, "y"),
        P(section),
        P("y", None),
        P(),
        P(section, None),
        P(section, None),
        P(section, None, None, "y"),
        P(section, "y", None),
        P(),
    )
    out_specs = (P(section, "y"), P(section, "y"))
    return jax.shard_map(local, mesh=fine, in_specs=in_specs, out_specs=out_specs, check_vma=False)
```

```python
import math

import jax
import jax.numpy as jnp
from jax import lax
from jax.experimental import pallas as pl
from jax.experimental.pallas import tpu as pltpu
from jax.sharding import Mesh
from jax.sharding import PartitionSpec as P

HD = 128
HCAP = 2
CAP = 10
NZ, NX, NC, NY = 8, 4, 2, 4
REQ = 64
SECTIONS = NZ * NX * NC
TOKENS = NZ * REQ
PLANE = NX * NY
BLOCK = NZ * CAP
ROWS = REQ // PLANE
QUARTER = 512
HEADS = 8
CTX = 96
CHUNK = 16
WIDTH = 2048
EHQ = 192


def select_blocks(first, gate_up, down, blocks, hold_ref, in_sems, out_sems):
    loads, stores = [], []
    for k, out in enumerate(blocks):
        index = first if k == 0 else 1 - first
        for part in range(3):
            source = gate_up.at[index, part] if part < 2 else down.at[index]
            loads.append(pltpu.make_async_copy(source, hold_ref.at[k, part], in_sems.at[k, part]))
            stores.append(
                pltpu.make_async_copy(hold_ref.at[k, part], out.at[part], out_sems.at[k, part])
            )
    return loads, stores


def attention_kernel(first_ref, lengths_ref, queries_ref, fresh_ref, cache, weight, *refs):
    gate_up, down, out_ref, even_ref, odd_ref, cache_ref, weight_ref, context_ref = refs[:8]
    hold_ref, cache_sem, weight_sem, in_sems, out_sems = refs[8:]
    blocks = (even_ref, odd_ref)
    picks, stores = select_blocks(first_ref[0], gate_up, down, blocks, hold_ref, in_sems, out_sems)
    loads = []
    for i in range(REQ // CHUNK):
        rows = pl.ds(i * CHUNK, CHUNK)
        loads.append(pltpu.make_async_copy(cache.at[rows], cache_ref.at[rows], cache_sem.at[i]))
    for copy in loads:
        copy.start()
    whole = pltpu.make_async_copy(weight, weight_ref, weight_sem)
    for copy in picks:
        copy.start()
    whole.start()
    scale = 1.0 / math.sqrt(HD)
    cell = lax.broadcasted_iota(jnp.int32, (HEADS, CTX), 1)
    for i in range(REQ // CHUNK):
        rows = slice(i * CHUNK, (i + 1) * CHUNK)
        heads = queries_ref[rows, :].astype(jnp.float32).reshape(CHUNK, HEADS, HD)
        fresh = fresh_ref[rows].astype(jnp.float32)
        loads[i].wait()
        keys, values = cache_ref[rows, 0], cache_ref[rows, 1]
        scores = lax.dot_general(
            heads.astype(jnp.bfloat16), keys, (((2,), (2,)), ((0,), (0,))), preferred_element_type=jnp.float32
        )
        scores = scores * scale
        scores = jnp.stack(
            [jnp.where(cell < lengths_ref[i * CHUNK + r], scores[r], -jnp.inf) for r in range(CHUNK)]
        )
        new = jnp.sum(heads * fresh[:, 0:1, :], axis=-1, keepdims=True) * scale
        top = jnp.maximum(jnp.max(scores, axis=-1, keepdims=True), new)
        mass = jnp.exp(scores - top)
        new = jnp.exp(new - top)
        total = jnp.sum(mass, axis=-1, keepdims=True) + new
        mass = (mass / total).astype(jnp.bfloat16)
        new = (new / total).astype(jnp.bfloat16).astype(jnp.float32)
        context = lax.dot_general(
            mass, values, (((2,), (1,)), ((0,), (0,))), preferred_element_type=jnp.float32
        ) + new * fresh[:, 1:2, :]
        context_ref[rows, :] = context.reshape(CHUNK, HEADS * HD).astype(jnp.bfloat16)
        if i == 2:
            for load, store in zip(picks, stores):
                load.wait()
                store.start()
    whole.wait()
    for y in range(NY):
        out_ref[y] = jnp.dot(
            context_ref[...], weight_ref[:, y * QUARTER : (y + 1) * QUARTER],
            preferred_element_type=jnp.float32,
        ).astype(jnp.bfloat16)
    for copy in stores:
        copy.wait()


def plan_kernel(ids_ref, gates_ref, even, odd, out_ref, *same):
    ids = jnp.concatenate([ids_ref[...], ids_ref[...]], axis=1)
    gates = jnp.concatenate([gates_ref[...], gates_ref[...]], axis=1)
    gates = gates / jnp.sum(gates, axis=0, keepdims=True)
    experts = NZ * PLANE
    expert = lax.broadcasted_iota(jnp.int32, (experts, 2 * REQ), 0)
    chosen = jnp.zeros((experts, 2 * REQ), jnp.float32)
    gate = jnp.zeros((experts, 2 * REQ), jnp.float32)
    for k in range(8):
        hit = ids[k : k + 1, :] == expert
        chosen = jnp.where(hit, 1.0, chosen)
        gate = jnp.where(hit, gates[k : k + 1, :], gate)
    earlier = lax.broadcasted_iota(jnp.int32, (2 * REQ, 2 * REQ), 0)
    token = lax.broadcasted_iota(jnp.int32, (2 * REQ, 2 * REQ), 1)
    token = jnp.where(token >= REQ, token - REQ, token)
    before = jnp.where(earlier < token, 1.0, 0.0).astype(jnp.bfloat16)
    rank = jnp.dot(chosen.astype(jnp.bfloat16), before, preferred_element_type=jnp.float32)
    slot = jnp.where(chosen > 0.0, rank, -1.0)
    first = lax.broadcasted_iota(jnp.int32, (experts, 2 * REQ), 1) < REQ
    both = jnp.where(first, slot, gate).astype(jnp.bfloat16)
    for z in range(NZ):
        out_ref[z] = both[z * PLANE : (z + 1) * PLANE, :]


def middle_kernel(pieces_ref, hidden_ref, plan_ref, message_ref, middle_ref):
    total = hidden_ref[...].astype(jnp.float32)
    for y in range(NY):
        total = total + pieces_ref[y].astype(jnp.float32)
    middle = total.astype(jnp.bfloat16)
    middle_ref[...] = middle
    for z in range(NZ):
        for k in range(ROWS):
            message_ref[z, :, k * QUARTER : (k + 1) * QUARTER] = middle[k * PLANE : (k + 1) * PLANE, :]
        message_ref[z, :, WIDTH:] = plan_ref[z]


def gather_kernel(spread_ref, out_ref, weight_ref, target_ref, gate_ref, pick_ref, rows_ref):
    low = lax.broadcasted_iota(jnp.int32, (PLANE, 2 * REQ), 1) < REQ
    for pair in range(NZ // 2):
        left = spread_ref[2 * pair, :, WIDTH:].astype(jnp.float32)
        right = spread_ref[2 * pair + 1, :, WIDTH:].astype(jnp.float32)
        both = jnp.concatenate([left[:, :REQ], right[:, :REQ]], axis=1)
        block = jnp.where(low, float(2 * pair * CAP), float((2 * pair + 1) * CAP))
        columns = slice(pair * 2 * REQ, (pair + 1) * 2 * REQ)
        target_ref[:, columns] = jnp.where(both >= 0.0, both + block, -1.0)
        gate_ref[:, columns] = jnp.concatenate([left[:, REQ:], right[:, REQ:]], axis=1)
    for z in range(NZ):
        for k in range(ROWS):
            first = z * REQ + k * PLANE
            rows_ref[first : first + PLANE, :] = spread_ref[z, :, k * QUARTER : (k + 1) * QUARTER]
    slot = lax.broadcasted_iota(jnp.int32, (BLOCK, TOKENS), 0).astype(jnp.float32)
    for e in range(PLANE):
        hit = target_ref[e : e + 1, :] == slot
        pick_ref[e * BLOCK : (e + 1) * BLOCK, :] = jnp.where(hit, 1.0, 0.0).astype(jnp.bfloat16)
        weight = jnp.where(hit, gate_ref[e : e + 1, :], 0.0)
        weight_ref[e * BLOCK : (e + 1) * BLOCK, :] = weight.astype(jnp.bfloat16)
    for e in range(0, PLANE, 4):
        rows = jnp.dot(
            pick_ref[e * BLOCK : (e + 4) * BLOCK, :],
            rows_ref[...],
            preferred_element_type=jnp.float32,
        ).astype(jnp.bfloat16)
        for k in range(4):
            out_ref[e + k] = rows[k * BLOCK : (k + 1) * BLOCK, :]


def hold_kernel(*refs):
    del refs


def combine_kernel(weight_ref, rows_ref, out_ref):
    rows = rows_ref[...].reshape(PLANE * BLOCK, QUARTER)
    dims = (((0,), (0,)), ((), ()))
    total = lax.dot_general(weight_ref[...], rows, dims, preferred_element_type=jnp.float32)
    total = total.astype(jnp.bfloat16)
    for z in range(NZ):
        out_ref[z] = total[z * REQ : (z + 1) * REQ, :]


def load_block(block, weight_ref, sems):
    copies = [
        pltpu.make_async_copy(block.at[part], weight_ref.at[part], sems.at[part])
        for part in range(3)
    ]
    for copy in copies:
        copy.start()
    return copies


def activate(normed_ref, block_ref):
    dims = (((1,), (1,)), ((), ()))
    gate, up = (
        lax.dot_general(normed_ref[...], block_ref[k], dims, preferred_element_type=jnp.float32)
        for k in range(2)
    )
    return (gate / (1.0 + jnp.exp(-gate)) * up).astype(jnp.bfloat16)


def first_half_kernel(rows_ref, gain_ref, w0, w1, normed_ref, part_ref, w0_ref, w1_ref, sems):
    copies = load_block(w0, w0_ref, sems.at[0]), load_block(w1, w1_ref, sems.at[1])
    for x in range(NX):
        parts = [rows_ref[x * NY + y].astype(jnp.float32) for y in range(NY)]
        square = sum(jnp.sum(part * part, axis=-1, keepdims=True) for part in parts)
        scale = lax.rsqrt(square * (1.0 / WIDTH) + 1e-06)
        for y in range(NY):
            columns = slice(y * QUARTER, (y + 1) * QUARTER)
            normed_ref[x * BLOCK : (x + 1) * BLOCK, columns] = (
                parts[y] * scale * gain_ref[:, columns]
            ).astype(jnp.bfloat16)
    for copy in copies[0]:
        copy.wait()
    first = activate(normed_ref, w0_ref)
    for copy in copies[1]:
        copy.wait()
    second = activate(normed_ref, w1_ref)
    part_ref[...] = jnp.dot(first, w0_ref[2], preferred_element_type=jnp.float32) + jnp.dot(
        second, w1_ref[2], preferred_element_type=jnp.float32
    )


def second_half_kernel(normed_ref, part_ref, w2, w3_ref, out_ref, w2_ref, sems):
    copies = load_block(w2, w2_ref, sems)
    second = activate(normed_ref, w3_ref)
    for copy in copies:
        copy.wait()
    first = activate(normed_ref, w2_ref)
    for y in range(NY):
        columns = slice(y * QUARTER, (y + 1) * QUARTER)
        part = part_ref[:, columns] + jnp.dot(
            first, w2_ref[2, :, columns], preferred_element_type=jnp.float32
        )
        part = part + jnp.dot(second, w3_ref[2, :, columns], preferred_element_type=jnp.float32)
        part = part.astype(jnp.bfloat16)
        for x in range(NX):
            out_ref[x * NY + y] = part[x * BLOCK : (x + 1) * BLOCK, :]


def vmem():
    return pl.BlockSpec(memory_space=pltpu.VMEM)


def anywhere():
    return pl.BlockSpec(memory_space=pl.ANY)


def params(mib=16):
    return pltpu.CompilerParams(vmem_limit_bytes=mib * 1024 * 1024)


def shape(*dims, dtype=jnp.bfloat16):
    return jax.ShapeDtypeStruct(dims, dtype)


def attend(first, lengths, queries, fresh, cache, weight, gate_up, down):
    hbm = pl.BlockSpec(memory_space=pltpu.HBM)
    smem = pl.BlockSpec(memory_space=pltpu.SMEM)
    block = shape(3, EHQ, WIDTH)
    return pl.pallas_call(
        attention_kernel,
        out_shape=(shape(NY, REQ, QUARTER), block, block),
        in_specs=[smem, smem, vmem(), vmem(), hbm, hbm, hbm, hbm],
        out_specs=(vmem(), hbm, hbm),
        scratch_shapes=[
            pltpu.VMEM((REQ, 2, CTX, HD), jnp.bfloat16),
            pltpu.VMEM((HEADS * HD, WIDTH), jnp.bfloat16),
            pltpu.VMEM((REQ, HEADS * HD), jnp.bfloat16),
            pltpu.VMEM((2, 3, EHQ, WIDTH), jnp.bfloat16),
            pltpu.SemaphoreType.DMA((REQ // CHUNK,)),
            pltpu.SemaphoreType.DMA,
            pltpu.SemaphoreType.DMA((2, 3)),
            pltpu.SemaphoreType.DMA((2, 3)),
        ],
        compiler_params=params(60),
        name="attend",
    )(first, lengths, queries, fresh, cache, weight, gate_up, down)


def make_plan(ids, gates, blocks):
    return pl.pallas_call(
        plan_kernel,
        out_shape=(shape(NZ, PLANE, 2 * REQ), *[shape(*block.shape) for block in blocks]),
        in_specs=[vmem(), vmem()] + [anywhere()] * 2,
        out_specs=(vmem(), anywhere(), anywhere()),
        input_output_aliases={2: 1, 3: 2},
        compiler_params=params(),
        name="plan",
    )(ids, gates, *blocks)


def sum_middle(pieces, hidden, plan):
    return pl.pallas_call(
        middle_kernel,
        out_shape=(shape(NZ, PLANE, WIDTH + 2 * REQ), shape(REQ, QUARTER)),
        in_specs=[vmem()] * 3,
        out_specs=(vmem(), vmem()),
        compiler_params=params(),
        name="sum_middle",
    )(pieces, hidden, plan)


def gather_rows(spread):
    return pl.pallas_call(
        gather_kernel,
        out_shape=(
            shape(PLANE, BLOCK, QUARTER),
            shape(PLANE * BLOCK, TOKENS),
        ),
        in_specs=[vmem()],
        out_specs=(vmem(), vmem()),
        scratch_shapes=[
            pltpu.VMEM((PLANE, TOKENS), jnp.float32),
            pltpu.VMEM((PLANE, TOKENS), jnp.float32),
            pltpu.VMEM((PLANE * BLOCK, TOKENS), jnp.bfloat16),
            pltpu.VMEM((TOKENS, QUARTER), jnp.bfloat16),
        ],
        compiler_params=params(),
        name="gather_rows",
    )(spread)


def hold(after, block):
    return pl.pallas_call(
        hold_kernel,
        out_shape=shape(*block.shape),
        in_specs=[anywhere()] * 2,
        out_specs=anywhere(),
        input_output_aliases={1: 0},
        compiler_params=params(),
        name="hold",
    )(after, block)


def combine_rows(weight, rows):
    return pl.pallas_call(
        combine_kernel,
        out_shape=shape(NZ, REQ, QUARTER),
        in_specs=[vmem(), vmem()],
        out_specs=vmem(),
        compiler_params=params(),
        name="combine_rows",
    )(weight, rows)


def first_half(rows, gain, blocks):
    return pl.pallas_call(
        first_half_kernel,
        out_shape=(shape(NX * BLOCK, WIDTH), shape(NX * BLOCK, WIDTH, dtype=jnp.float32)),
        in_specs=[vmem(), vmem(), anywhere(), anywhere()],
        out_specs=(vmem(), vmem()),
        scratch_shapes=[
            pltpu.VMEM((3, EHQ, WIDTH), jnp.bfloat16),
            pltpu.VMEM((3, EHQ, WIDTH), jnp.bfloat16),
            pltpu.SemaphoreType.DMA((2, 3)),
        ],
        compiler_params=params(24),
        name="first_half",
    )(rows, gain, *blocks)


def second_half(normed, part, blocks):
    return pl.pallas_call(
        second_half_kernel,
        out_shape=shape(PLANE, BLOCK, QUARTER),
        in_specs=[vmem(), vmem(), anywhere(), vmem()],
        out_specs=vmem(),
        scratch_shapes=[
            pltpu.VMEM((3, EHQ, WIDTH), jnp.bfloat16),
            pltpu.SemaphoreType.DMA((3,)),
        ],
        compiler_params=params(24),
        name="second_half",
    )(normed, part, *blocks)


def move_weights(blocks):
    even, odd = [], []
    for c in range(NC):
        for y in range(NY):
            even.append((c * NY + y, (1 - y // 2) * NY + 2 * c + y % 2))
            odd.append((c * NY + y, (y // 2) * NY + 2 * c + 1 - y % 2))
    return [lax.ppermute(block, ("c", "y"), to) for block, to in zip(blocks, (even, odd))]


def talker_plan(owners, section):
    own = lax.dynamic_slice_in_dim(owners, section * REQ, REQ)
    order = jnp.arange(REQ, dtype=jnp.int32)
    same = (own[:, None] == own[None, :]) & (order[:, None] > order[None, :])
    position = jnp.sum(same.astype(jnp.int32), axis=1)
    slot = jnp.where(own >= 0, own * HCAP + position, -1)
    send = (jnp.arange(SECTIONS * HCAP, dtype=jnp.int32)[:, None] == slot[None, :]).astype(
        jnp.bfloat16
    )
    counts = jnp.sum((owners == section).reshape(SECTIONS, REQ).astype(jnp.int32), axis=1)
    place = jnp.arange(SECTIONS, dtype=jnp.int32)
    offsets = jnp.sum(jnp.where(place[None, :] < place[:, None], counts[None, :], 0), axis=1)
    index = jnp.arange(HCAP, dtype=jnp.int32)
    put = jnp.where(index[None, :] < counts[:, None], offsets[:, None] + index[None, :], -1)
    put = put.reshape(SECTIONS * HCAP)
    take = (jnp.arange(SECTIONS * HCAP, dtype=jnp.int32)[:, None] == put[None, :]).astype(
        jnp.bfloat16
    )
    return send, take


def local(
    hidden_in,
    queries,
    new_kv,
    cache,
    lengths,
    out_weight,
    moe_gain,
    expert_ids,
    expert_gates,
    gate_up,
    down,
    owners,
):
    z, x, c, y = (lax.axis_index(name) for name in ("z", "x", "c", "y"))
    section = (z * NX + x) * NC + c
    first = (y % 2).astype(jnp.int32).reshape(1)
    pieces, *blocks = attend(
        first,
        lengths,
        queries,
        new_kv,
        cache,
        out_weight,
        gate_up.transpose(0, 1, 3, 2),
        down,
    )
    plan, *blocks = make_plan(expert_ids.T, expert_gates.T, blocks)
    pieces = lax.all_to_all(pieces, "y", 0, 0, tiled=True)
    hidden = lax.dynamic_slice_in_dim(hidden_in, y * QUARTER, QUARTER, 1)
    message, middle = sum_middle(pieces, hidden, plan)
    even, odd = move_weights(blocks)
    swap = [(0, 1), (1, 0)]

    spread = lax.all_to_all(message, "z", 0, 0, tiled=True)
    send, weight = gather_rows(spread)
    rows = lax.all_to_all(send, ("x", "y"), 0, 0, tiled=True)
    odd = hold(rows, odd)
    even_swapped = lax.ppermute(even, "c", swap)
    odd_swapped = lax.ppermute(odd, "c", swap)
    normed, half = first_half(rows, moe_gain.reshape(1, WIDTH), (even, even_swapped))
    done = second_half(normed, half, (odd, odd_swapped))
    back = lax.all_to_all(done, ("x", "y"), 0, 0, tiled=True)
    part = combine_rows(weight, back)
    part = lax.all_to_all(part, "z", 0, 0, tiled=True)
    out = middle.astype(jnp.float32) + jnp.sum(part.astype(jnp.float32), axis=0)
    out = out.astype(jnp.bfloat16)

    send_pick, take_pick = talker_plan(owners, section)
    leaving = jnp.dot(send_pick, out, preferred_element_type=jnp.float32).astype(jnp.bfloat16)
    arrived = lax.all_to_all(
        leaving.reshape(SECTIONS, HCAP, QUARTER), ("z", "x", "c"), 0, 0, tiled=True
    )
    talker = jnp.dot(
        take_pick, arrived.reshape(SECTIONS * HCAP, QUARTER), preferred_element_type=jnp.float32
    ).astype(jnp.bfloat16)
    return (out, talker)


def solution(mesh):
    section = ("z", "x", "c")
    fine = Mesh(mesh.devices.reshape(NZ, NX, NC, NY), ("z", "x", "c", "y"))
    in_specs = (
        P(section, None),
        P(section, "y"),
        P(section, None, "y"),
        P(section, None, None, "y"),
        P(section),
        P("y", None),
        P(),
        P(section, None),
        P(section, None),
        P(section, None, None, "y"),
        P(section, "y", None),
        P(),
    )
    out_specs = (P(section, "y"), P(section, "y"))
    return jax.shard_map(local, mesh=fine, in_specs=in_specs, out_specs=out_specs, check_vma=False)
```
